32 devices in a mesh: parts: 2 (over y), dp: 4 (over z), tensor: 2 (over x), sub: 2 (over core).
Axes of the slice: x: 2, y: 2, z: 4, core: 2. Of those that a mesh axis runs over, the one named last changes fastest.
Arguments:
- tokens: bfloat16 [6144, 8192], P(('parts', 'dp'), ('tensor', 'sub')), parts along dimension 0, may hold values from -6 to 6
- key_value_weight: bfloat16 [8192, 1024], P(('tensor', 'sub')), may hold values from -0.09375 to 0.09375
- adapter_down_weight: bfloat16 [96, 128, 8192], P('dp', None, ('tensor', 'sub')), may hold values from -0.0625 to 0.0625
- adapter_up_weight: bfloat16 [96, 64, 1024], P('dp', None, ('tensor', 'sub')), may hold values from -0.75 to 0.75
- adapter_scale: float32 [96], P('dp'), may hold values from 0.5 to 2
- token_adapter_index: int32 [6144, 1], P(('parts', 'dp')), parts along dimension 0, may hold values from 0 to 95; in each aligned block of 768 rows (0 to 767, 768 to 1535, ...) at most 12 rows name the same one
Outputs:
- kv_out: bfloat16 [6144, 1024], P(('parts', 'dp'), ('tensor', 'sub')), parts along dimension 0
The draws below stay inside these ranges and needn't reach their ends.
There are 2 independent parts, one for each index of `parts`. The reference program is written for one: setup_inputs(seed, part) draws one part's arguments, and reference() takes and returns one part's arrays. A program takes and returns all parts, laid end to end along the dimension named above; an argument that names none is the same for every part. Nothing has to cross between parts.
Inputs may be any that keep to these rules, and one draw needn't show every extreme that they name: `token_adapter_index`: within the 768 rows of one index of dp no adapter is named by more than 12 rows, and one adapter is named by exactly 12 rows of some index; every adapter is named by some row.
All inputs are finite; a program needn't handle non-finite values.
Results may differ from the reference program's by a relative error of at most 0.001.
Values may be sent and summed in bfloat16 or wider, within the bound.
No kernel may reach another device: no remote copies, remote signals or barrier semaphores. Data moves between devices by JAX's collectives and lax.ppermute only.
A program may use at most 128 MiB of HBM per device.

```python
import math
import jax
import jax.numpy as jnp
import numpy as np
from jax import lax

MODEL_WIDTH = 8192
ADAPTER_RANK = 64
ADAPTER_COUNT = 96
TOK_DEV = 768
KEY_VALUE_WIDTH = 512
TOKENS = 3072
TOKEN_LIMIT = 12
N_DP = 4


def strengthened(drawn, stream_key, source, target, parts, factor):
    owner, partner = [(jnp.arange(drawn.shape[dim]) // (drawn.shape[dim] // parts)).reshape([-1 if axis == dim else 1 for axis in range(drawn.ndim)]) for dim in (source, target)]
    chosen = jax.random.permutation(stream_key, parts)[partner]
    strong = (owner == chosen) | (owner == (partner + parts // 2) % parts)
    return jnp.where(strong, factor * drawn, drawn)


def block_levels(key, shape, cuts, low, high):
    def one(axis_at, shards_of):
        steps = jax.random.uniform(jax.random.fold_in(jax.random.fold_in(key, 6), axis_at), (shards_of,), jnp.float32, low / len(cuts), high / len(cuts))
        return jnp.repeat(jnp.exp(steps), shape[axis_at] // shards_of).reshape((-1,) + (1,) * (len(shape) - axis_at - 1))

    gain = one(*cuts[0])
    for cut in cuts[1:]:
        gain = gain * one(*cut)
    return gain


def shared_out(own_key, own, number, rows, number_of, top, limit, slope):
    ranking = jax.random.permutation(own_key, number_of)
    crowded, common = load_shares(number_of, rows * top, limit, slope, True), load_shares(number_of, rows * top, limit, slope, False)
    places = jnp.arange(number_of)

    def named(sizes, rotation):
        used = int((sizes > 0).sum())
        fixed = max(1, used // 4)
        passed = fixed + (places - fixed + rotation * (used - fixed)) % max(1, number_of - fixed)
        return jnp.zeros((number_of,), jnp.int32).at[ranking[jnp.where(places < fixed, places, passed)]].set(jnp.asarray(sizes, jnp.int32))

    sizes = jnp.where(number % 4 == 0, named(crowded, number // 4), named(common, number - number // 4 - 1))
    mixed = jax.random.permutation(jax.random.fold_in(own, 3), number_of)
    source_of, sink = mixed[0:number_of // 2 * 2:2], mixed[1:number_of // 2 * 2:2]
    margin = jnp.minimum(sizes[source_of] - 1, limit - sizes[sink]) // 2
    margin = jnp.where((source_of == ranking[0]) | (sink == ranking[0]) | (sizes[sink] == 0), 0, jnp.maximum(margin, 0))
    passed = jax.random.randint(jax.random.fold_in(own, 4), (number_of // 2,), 0, 1 << 20) % (margin + 1)
    sizes = sizes.at[source_of].add(-passed).at[sink].add(passed)
    labels = jnp.searchsorted(jnp.cumsum(sizes), jnp.arange(rows * top), side="right").astype(jnp.int32)
    listing = labels.reshape(top, rows).T
    listing = listing[jax.random.permutation(jax.random.fold_in(own, 1), rows)]
    rotation = jax.random.randint(jax.random.fold_in(own, 2), (rows, 1), 0, top)
    return jnp.take_along_axis(listing, (jnp.arange(top)[None, :] + rotation) % top, axis=1)


def load_shares(amount, total, reach, lean, full):
    portions = [(1 << 20) // math.isqrt(grade ** lean) + 1 for grade in range(1, amount + 1)]
    largest = reach if full else min(reach, max(-(-total // amount), total * portions[0] // sum(portions)))
    least = 1 if total - largest >= amount - 1 else 0
    given, rest = [largest] + [least] * (amount - 1), total - largest - least * (amount - 1)
    while rest > 0:
        movable = [i for i in range(1, amount) if given[i] < largest] or [i for i in range(1, amount) if given[i] < reach]
        whole, budget = sum([portions[i] for i in movable]), rest
        for i in movable:
            extra = min(reach - given[i], max(1, budget * portions[i] // whole), rest)
            given[i] = given[i] + extra
            rest = rest - extra
    return np.array(given)


def normal_values(rng, dims, width, reach, shards=(), kind=jnp.bfloat16):
    level = block_levels(rng, dims, shards, -0.22, 0.18) if shards else 1.0
    entries = jax.random.normal(rng, dims, jnp.float32) * width * level
    return jnp.minimum(jnp.maximum(entries, -reach), reach).astype(kind)


def heavy_noise(key, extent, scale, most, cuts, heavy, held_as=jnp.bfloat16):
    drawn = scale * jax.random.normal(key, extent, jnp.float32)
    if cuts:
        drawn = drawn * block_levels(key, extent, cuts, -0.22, 0.18)
    return jnp.clip(strengthened(drawn, jax.random.fold_in(key, 3), *heavy), -most, most).astype(held_as)


def setup_inputs(seed: int = 0, part: int = 0) -> dict:
    streams_of = jax.random.split(jax.random.key(seed), 7)
    own_keys = jax.random.split(jax.random.fold_in(streams_of[6], part), 7)
    tokens = normal_values(own_keys[0], (TOKENS, MODEL_WIDTH), 1.0, 6.0, ((0, 4), (1, 4)))
    key_value_weight = heavy_noise(streams_of[1], (MODEL_WIDTH, 2 * KEY_VALUE_WIDTH), MODEL_WIDTH ** -0.5, 0.09375, ((0, 4),), (0, 1, 4, 2.0))
    adapter_down_weight = normal_values(streams_of[2], (ADAPTER_COUNT, 2 * ADAPTER_RANK, MODEL_WIDTH), MODEL_WIDTH ** -0.5, 0.0625, ((0, 4), (2, 4)))
    adapter_up_weight = normal_values(streams_of[3], (ADAPTER_COUNT, ADAPTER_RANK, 2 * KEY_VALUE_WIDTH), ADAPTER_RANK ** -0.5, 0.75, ((0, 4), (2, 4)))
    adapter_scale = jnp.clip(jnp.exp(math.log(2.0) - 1.3862944 * jax.random.uniform(streams_of[4], (ADAPTER_COUNT,), jnp.float32) ** block_levels(streams_of[4], (ADAPTER_COUNT,), ((0, 4),), -0.2, 0.2)), 0.5, 2.0)
    token_adapter_index_keys = jax.random.split(jax.random.fold_in(own_keys[5], 1), TOKENS // TOK_DEV)
    token_adapter_index_turns = jax.random.permutation(jax.random.fold_in(own_keys[5], 3), TOKENS // TOK_DEV)
    token_adapter_index = jax.vmap(lambda own, number: shared_out(jax.random.fold_in(own_keys[5], 2), own, number, TOK_DEV, ADAPTER_COUNT, 1, TOKEN_LIMIT, 2))(token_adapter_index_keys, token_adapter_index_turns).reshape((TOKENS, 1))
    return dict(tokens=tokens, key_value_weight=key_value_weight, adapter_down_weight=adapter_down_weight, adapter_up_weight=adapter_up_weight, adapter_scale=adapter_scale, token_adapter_index=token_adapter_index)


def reference(tokens, key_value_weight, adapter_down_weight, adapter_up_weight, adapter_scale, token_adapter_index):
    width_halved = key_value_weight.shape[1] // 2
    base_out = jnp.dot(tokens, key_value_weight, preferred_element_type=jnp.float32)
    adapter_ids = token_adapter_index[:, 0]
    capacity = N_DP * TOKEN_LIMIT

    def one_adapter(adapter_index):
        chosen = adapter_ids == adapter_index
        slot_positions = jnp.nonzero(chosen, size=capacity, fill_value=0)[0].astype(jnp.int32)
        active_mask = jnp.arange(capacity, dtype=jnp.int32) < jnp.sum(chosen.astype(jnp.int32))
        picked = tokens[slot_positions]
        down_matrix = adapter_down_weight[adapter_index]
        shrink = lax.dot_general(picked, down_matrix, (((1,), (1,)), ((), ())), preferred_element_type=jnp.float32)
        up_matrix = adapter_up_weight[adapter_index].astype(jnp.float32)
        key_update = jnp.dot(shrink[:, :ADAPTER_RANK], up_matrix[:, :width_halved], precision=lax.Precision.HIGHEST)
        value_update = jnp.dot(shrink[:, ADAPTER_RANK:], up_matrix[:, width_halved:], precision=lax.Precision.HIGHEST)
        adapter_update = jnp.concatenate([key_update, value_update], axis=1) * adapter_scale[adapter_index]
        adapter_update = jnp.where(active_mask[:, None], adapter_update, jnp.zeros_like(adapter_update))
        return slot_positions, adapter_update

    slot_positions, deltas = lax.map(one_adapter, jnp.arange(ADAPTER_COUNT, dtype=jnp.int32))
    combined = base_out.at[slot_positions.reshape(-1)].add(deltas.reshape(-1, 2 * width_halved))
    return combined.astype(jnp.bfloat16)
```

```python
import functools

import jax
import jax.numpy as jnp
from jax import lax
from jax.experimental import pallas as pl
from jax.experimental.pallas import tpu as pltpu
from jax.sharding import PartitionSpec as P

ADAPTER_RANK = 64
TOKEN_LIMIT = 12
VMEM_LIMIT = 60 * 1024 * 1024
F32 = jnp.float32
BF16 = jnp.bfloat16
I32 = jnp.int32


def owner_of(ids, owners, owned):
    total = jnp.zeros_like(ids)
    for o in range(1, owners):
        total = total + jnp.where(ids >= o * owned, 1, 0)
    return total


def pack_kernel(owners, owned, cap, pieces, me_ref, row_ref, col_ref, tok_ref, *refs):
    outs, target_ref, place = refs[: len(pieces)], refs[-2], refs[-1]
    rows = col_ref.shape[0]

    @pl.when(pl.program_id(0) == 0)
    def _():
        me = me_ref[0]
        id_row, id_col = row_ref[...], col_ref[...]
        key_row = id_row * rows + lax.broadcasted_iota(I32, (1, rows), 1)
        key_col = id_col * rows + lax.broadcasted_iota(I32, (rows, 1), 0)
        own_row, own_col = owner_of(id_row, owners, owned), owner_of(id_col, owners, owned)
        low_row, low_col = own_row * owned * rows, own_col * owned * rows
        before = (key_col < key_row) & (key_col >= low_row)
        rank_row = jnp.sum(jnp.where(before, 1, 0), axis=0, keepdims=True)
        before = (key_row < key_col) & (key_row >= low_col)
        rank_col = jnp.sum(jnp.where(before, 1, 0), axis=1, keepdims=True)
        target_ref[...] = (own_col ^ me) * cap + rank_col
        slot = (own_row ^ me) * cap + rank_row
        at = lax.broadcasted_iota(I32, (owners * cap, rows), 0)
        place[...] = jnp.where(at == slot, 1.0, 0.0).astype(BF16)

    for (block, first, count), out in zip(pieces, outs):
        begin = block * cap + first
        out[...] = jnp.dot(
            place[begin : begin + count, :], tok_ref[...], preferred_element_type=F32
        ).astype(BF16)


def pack(tokens, ids_row, ids_col, me, owners, owned, cap, pieces):
    rows, width = tokens.shape
    step = min(512, width)
    res = pl.pallas_call(
        functools.partial(pack_kernel, owners, owned, cap, pieces),
        grid=(width // step,),
        in_specs=[
            pl.BlockSpec(memory_space=pltpu.SMEM),
            pl.BlockSpec((1, rows), lambda i: (0, 0)),
            pl.BlockSpec((rows, 1), lambda i: (0, 0)),
            pl.BlockSpec((rows, step), lambda i: (0, i)),
        ],
        out_specs=[pl.BlockSpec((count, step), lambda i: (0, i)) for _, _, count in pieces]
        + [pl.BlockSpec((rows, 1), lambda i: (0, 0))],
        out_shape=[jax.ShapeDtypeStruct((count, width), BF16) for _, _, count in pieces]
        + [jax.ShapeDtypeStruct((rows, 1), I32)],
        scratch_shapes=[pltpu.VMEM((owners * cap, rows), BF16)],
        compiler_params=pltpu.CompilerParams(vmem_limit_bytes=VMEM_LIMIT),
        name="pack",
    )(me, ids_row, ids_col, tokens)
    return res[:-1], res[-1]


def shrink_kernel(sizes, group, half_ref, which_ref, down_ref, *refs):
    blocks, (mine_ref, other_ref, acc) = refs[: len(sizes)], refs[len(sizes) :]
    step = pl.program_id(0)
    factors = down_ref[...].reshape(group * 2 * ADAPTER_RANK, down_ref.shape[2])
    begin = 0
    for size, block in zip(sizes, blocks):
        product = lax.dot_general(
            block[...], factors, (((1,), (1,)), ((), ())), preferred_element_type=F32
        )
        which = which_ref[begin : begin + size, :]
        found = jnp.zeros((size, 2 * ADAPTER_RANK), F32)
        for q in range(group):
            part = product[:, q * 2 * ADAPTER_RANK : (q + 1) * 2 * ADAPTER_RANK]
            found = found + jnp.where(which == step * group + q, part, 0.0)
        here = slice(begin, begin + size)
        acc[here, :] = jnp.where(step == 0, found, acc[here, :] + found)
        begin += size

    @pl.when(step == pl.num_programs(0) - 1)
    def _():
        total = sum(sizes)
        upper, lower = acc[: total // 2, :], acc[total // 2 :, :]
        keys = jnp.concatenate([upper[:, :ADAPTER_RANK], lower[:, :ADAPTER_RANK]], axis=1)
        values = jnp.concatenate([upper[:, ADAPTER_RANK:], lower[:, ADAPTER_RANK:]], axis=1)
        second = half_ref[0] == 1
        mine_ref[...] = jnp.where(second, values, keys)
        other_ref[...] = jnp.where(second, keys, values)


def shrink(blocks, which, down, half):
    sizes = tuple(b.shape[0] for b in blocks)
    total = sum(sizes)
    owned, rank2, width = down.shape
    group = next(g for g in (4, 3, 2, 1) if owned % g == 0)
    line = jax.ShapeDtypeStruct((total // 2, 2 * ADAPTER_RANK), F32)
    return pl.pallas_call(
        functools.partial(shrink_kernel, sizes, group),
        grid=(owned // group,),
        in_specs=[
            pl.BlockSpec(memory_space=pltpu.SMEM),
            pl.BlockSpec((total, 1), lambda i: (0, 0)),
            pl.BlockSpec((group, rank2, width), lambda i: (i, 0, 0)),
        ]
        + [pl.BlockSpec((s, width), lambda i: (0, 0)) for s in sizes],
        out_specs=[pl.BlockSpec((total // 2, rank2), lambda i: (0, 0))] * 2,
        out_shape=[line, line],
        scratch_shapes=[pltpu.VMEM((total, rank2), F32)],
        compiler_params=pltpu.CompilerParams(vmem_limit_bytes=VMEM_LIMIT),
        name="shrink",
    )(half, which, down, *blocks)


def three_way(x):
    high = x.astype(BF16).astype(F32)
    middle = (x - high).astype(BF16).astype(F32)
    return high, middle, x - high - middle


def expand_kernel(sizes, heard, which_ref, scale_ref, up_ref, *refs):
    lines, outs = refs[:heard], refs[heard:]
    total = lines[0][...]
    for line in lines[1:]:
        total = total + line[...]
    upper, lower = total[:, :ADAPTER_RANK], total[:, ADAPTER_RANK:]
    twice = jnp.concatenate(
        [jnp.concatenate([upper, upper], axis=1), jnp.concatenate([lower, lower], axis=1)], axis=0
    )
    which = which_ref[...]
    parity = jnp.where(lax.broadcasted_iota(I32, (1, 2 * ADAPTER_RANK), 1) >= ADAPTER_RANK, 1, 0)
    pairs = up_ref.shape[0] // (2 * ADAPTER_RANK)
    wanted = [which == 2 * p + parity for p in range(pairs)]
    delta = None
    for term in three_way(twice):
        spread = jnp.concatenate(
            [jnp.where(w, term, 0.0).astype(BF16) for w in wanted], axis=1
        )
        product = jnp.dot(spread, up_ref[...], preferred_element_type=F32)
        delta = product if delta is None else delta + product
    adapters = lax.broadcasted_iota(I32, scale_ref.shape, 1)
    gain = jnp.sum(jnp.where(which == adapters, scale_ref[...], 0.0), axis=1, keepdims=True)
    delta = delta * gain
    begin = 0
    for size, out in zip(sizes, outs):
        out[...] = delta[begin : begin + size, :]
        begin += size


def expand(lines, which, scale, up, sizes):
    columns = up.shape[1]
    return pl.pallas_call(
        functools.partial(expand_kernel, sizes, len(lines)),
        out_shape=[jax.ShapeDtypeStruct((s, columns), F32) for s in sizes],
        compiler_params=pltpu.CompilerParams(vmem_limit_bytes=VMEM_LIMIT),
        name="expand",
    )(which, scale, up, *lines)


def merge_kernel(begins, base_ref, target_ref, *refs):
    blocks, out_ref = refs[:-1], refs[-1]
    returned = jnp.concatenate([b[...] for b in blocks], axis=0)
    target = target_ref[...]
    place = jnp.concatenate(
        [
            jnp.where(
                target == begin + lax.broadcasted_iota(I32, (1, block.shape[0]), 1), 1.0, 0.0
            ).astype(BF16)
            for begin, block in zip(begins, blocks)
        ],
        axis=1,
    )
    total = None
    for term in three_way(returned):
        moved = jnp.dot(place, term.astype(BF16), preferred_element_type=F32)
        total = moved if total is None else total + moved
    out_ref[...] = (base_ref[...] + total).astype(BF16)


def merge(base, target, begins, blocks):
    return pl.pallas_call(
        functools.partial(merge_kernel, begins),
        out_shape=jax.ShapeDtypeStruct(base.shape, BF16),
        compiler_params=pltpu.CompilerParams(vmem_limit_bytes=VMEM_LIMIT),
        name="merge",
    )(base, target, *blocks)


def swap(x, axes, size, distance):
    return lax.ppermute(x, axes, [(i, i ^ distance) for i in range(size)])


def local(
    tokens,
    key_value_weight,
    adapter_down_weight,
    adapter_up_weight,
    adapter_scale,
    token_adapter_index,
):
    feature_axes = ("tensor", "sub")
    rows = tokens.shape[0]
    owned, _, width = adapter_down_weight.shape
    owners = lax.axis_size("dp")
    sharers = lax.axis_size(feature_axes)
    me = lax.axis_index("dp")
    half = (lax.axis_index(feature_axes) >= sharers // 2).astype(I32).reshape(1)
    cap = -(-owned * TOKEN_LIMIT // 16) * 16

    first = cap if owners > 4 else 144
    parts = [(0, first)] + ([(first, cap - first)] if first < cap else [])
    pieces = [(0, 0, cap)] + [(j, f, c) for f, c in parts for j in range(1, owners)]

    ids_row = token_adapter_index.reshape(1, rows)
    ids_heard = [ids_row] + [swap(ids_row, "dp", owners, j) for j in range(1, owners)]
    packed, target = pack(
        tokens, ids_row, token_adapter_index, me.reshape(1), owners, owned, cap, pieces
    )
    received = [packed[0]] + [
        swap(rows_out, "dp", owners, j) for (j, _, _), rows_out in zip(pieces[1:], packed[1:])
    ]

    base_part = jnp.dot(tokens, key_value_weight, preferred_element_type=F32)
    base = lax.psum_scatter(base_part, feature_axes, scatter_dimension=1, tiled=True)

    heard = jnp.concatenate(ids_heard, axis=0) - me * owned
    adapters = jnp.arange(owned, dtype=I32)
    upto = jnp.sum(
        (heard[:, None, :] >= 0) & (heard[:, None, :] <= adapters[None, :, None]), axis=2, dtype=I32
    )
    at = jnp.arange(cap, dtype=I32)
    which = jnp.sum(upto[:, None, :] <= at[None, :, None], axis=2, dtype=I32)

    if owned % 2:
        adapter_up_weight = jnp.pad(adapter_up_weight, ((0, 1), (0, 0), (0, 0)))
    up = adapter_up_weight.reshape(-1, adapter_up_weight.shape[2])
    scale = adapter_scale.reshape(1, owned)

    sets = [[0]]
    for p in range(len(parts)):
        sets.append([1 + p * (owners - 1) + j for j in range(owners - 1)])
    returned = [None] * len(pieces)
    for members in sets:
        blocks = [received[m] for m in members]
        sizes = tuple(pieces[m][2] for m in members)
        names = jnp.concatenate(
            [which[b, f : f + c] for b, f, c in (pieces[m] for m in members)]
        ).reshape(-1, 1)
        mine, other = shrink(blocks, names, adapter_down_weight, half)
        lines = [mine] + [
            swap(mine if d < sharers // 2 else other, feature_axes, sharers, d)
            for d in range(1, sharers)
        ]
        deltas = expand(lines, names, scale, up, sizes)
        for m, delta in zip(members, deltas):
            block = pieces[m][0]
            returned[m] = swap(delta, "dp", owners, block) if block else delta
    begins = tuple(b * cap + f for b, f, _ in pieces)
    return merge(base, target, begins, returned)


def solution(mesh):
    return jax.shard_map(
        local,
        mesh=mesh,
        in_specs=(
            P(("parts", "dp"), ("tensor", "sub")),
            P(("tensor", "sub"), None),
            P("dp", None, ("tensor", "sub")),
            P("dp", None, ("tensor", "sub")),
            P("dp"),
            P(("parts", "dp"), None),
        ),
        out_specs=P(("parts", "dp"), ("tensor", "sub")),
        check_vma=False,
    )
```

```python
import functools

import jax
import jax.numpy as jnp
from jax import lax
from jax.experimental import pallas as pl
from jax.experimental.pallas import tpu as pltpu
from jax.sharding import PartitionSpec as P

ADAPTER_RANK = 64
TOKEN_LIMIT = 12
VMEM_LIMIT = 48 * 1024 * 1024
F32 = jnp.float32
BF16 = jnp.bfloat16
I32 = jnp.int32
ANYWHERE = pl.BlockSpec(memory_space=pl.ANY)
PARAMS = pltpu.CompilerParams(vmem_limit_bytes=VMEM_LIMIT)


def cost(rows, depth, columns, terms=1):
    return pl.CostEstimate(
        flops=2 * rows * depth * columns * terms,
        transcendentals=0,
        bytes_accessed=2 * terms * (rows + columns) * depth + 4 * rows * columns,
    )


def owner_of(ids, owners, owned):
    total = jnp.zeros_like(ids)
    for o in range(1, owners):
        total = total + jnp.where(ids >= o * owned, 1, 0)
    return total


def move_rows(pieces, cap, slot, tok_ref, outs):
    for (block, first, count), out in zip(pieces, outs):
        at = block * cap + first + lax.broadcasted_iota(I32, (count, slot.shape[1]), 0)
        place = jnp.where(at == slot, 1.0, 0.0).astype(BF16)
        out[...] = jnp.dot(place, tok_ref[...], preferred_element_type=F32).astype(BF16)


def head_kernel(owners, owned, cap, pieces, me_ref, row_ref, tok_ref, *refs):
    outs, slot_ref, slot = refs[: len(pieces)], refs[-2], refs[-1]
    rows = row_ref.shape[1]

    @pl.when(pl.program_id(0) == 0)
    def _():
        id_row = row_ref[...]
        key_row = id_row * rows + lax.broadcasted_iota(I32, (1, rows), 1)
        down = lax.broadcasted_iota(I32, (rows, rows), 0)
        across = lax.broadcasted_iota(I32, (rows, rows), 1)
        key_col = jnp.sum(jnp.where(down == across, key_row, 0), axis=1, keepdims=True)
        own_row = owner_of(id_row, owners, owned)
        before = (key_col < key_row) & (key_col >= own_row * (owned * rows))
        rank = jnp.sum(jnp.where(before, 1, 0), axis=0, keepdims=True)
        found = (own_row ^ me_ref[0]) * cap + rank
        slot[...] = found
        slot_ref[...] = found

    move_rows(pieces, cap, slot[...], tok_ref, outs)


def rest_kernel(cap, pieces, slot_ref, tok_ref, *refs):
    outs, target_ref = refs[: len(pieces)], refs[-1]
    rows = slot_ref.shape[1]

    @pl.when(pl.program_id(0) == 0)
    def _():
        down = lax.broadcasted_iota(I32, (rows, rows), 0)
        across = lax.broadcasted_iota(I32, (rows, rows), 1)
        target_ref[...] = jnp.sum(
            jnp.where(down == across, slot_ref[...], 0), axis=1, keepdims=True
        )

    move_rows(pieces, cap, slot_ref[...], tok_ref, outs)


def sort_rows(tokens, ids_row, me, owners, owned, cap, first, rest):
    rows, width = tokens.shape
    step = min(512, width)
    line = pl.BlockSpec((1, rows), lambda i: (0, 0))
    strip = pl.BlockSpec((rows, step), lambda i: (0, i))

    def outs(pieces):
        specs = [pl.BlockSpec((count, step), lambda i: (0, i)) for _, _, count in pieces]
        return specs, [jax.ShapeDtypeStruct((count, width), BF16) for _, _, count in pieces]

    specs, shapes = outs(first)
    *sent, slot = pl.pallas_call(
        functools.partial(head_kernel, owners, owned, cap, first),
        grid=(width // step,),
        in_specs=[pl.BlockSpec(memory_space=pltpu.SMEM), line, strip],
        out_specs=specs + [line],
        out_shape=shapes + [jax.ShapeDtypeStruct((1, rows), I32)],
        scratch_shapes=[pltpu.VMEM((1, rows), I32)],
        compiler_params=PARAMS,
        cost_estimate=cost(sum(c for _, _, c in first), rows, width),
        name="sort_first",
    )(me, ids_row, tokens)
    specs, shapes = outs(rest)
    *others, target = pl.pallas_call(
        functools.partial(rest_kernel, cap, rest),
        grid=(width // step,),
        in_specs=[line, strip],
        out_specs=specs + [pl.BlockSpec((rows, 1), lambda i: (0, 0))],
        out_shape=shapes + [jax.ShapeDtypeStruct((rows, 1), I32)],
        compiler_params=PARAMS,
        cost_estimate=cost(sum(c for _, _, c in rest), rows, width),
        name="sort_rest",
    )(slot, tokens)
    return sent, others, target


def base_kernel(tok_ref, weight_ref, _, out_ref):
    out_ref[...] = jnp.dot(tok_ref[...], weight_ref[...], preferred_element_type=F32)


def base_product(tokens, weight, later_than):
    (rows, width), columns = tokens.shape, weight.shape[1]
    step = min(256, columns)
    return pl.pallas_call(
        base_kernel,
        grid=(columns // step,),
        in_specs=[
            pl.BlockSpec((rows, width), lambda i: (0, 0)),
            pl.BlockSpec((width, step), lambda i: (0, i)),
            ANYWHERE,
        ],
        out_specs=pl.BlockSpec((rows, step), lambda i: (0, i)),
        out_shape=jax.ShapeDtypeStruct((rows, columns), F32),
        compiler_params=PARAMS,
        cost_estimate=cost(rows, width, columns),
        name="base",
    )(tokens, weight, later_than)


def shrink_kernel(sizes, group, fine, waits, plan_ref, which_ref, down_ref, *refs):
    blocks, (mine_ref, other_ref, rows, acc) = refs[: len(sizes)], refs[len(sizes) + waits :]
    step, rank2 = pl.program_id(0), 2 * ADAPTER_RANK
    low, high, second = plan_ref[0], plan_ref[1], plan_ref[2] == 1
    begin = (low // group + step) * group

    @pl.when(step == 0)
    def _():
        at = 0
        for size, block in zip(sizes, blocks):
            rows[at : at + size, :] = block[...]
            at += size
        acc[...] = jnp.zeros_like(acc)

    for f in range(0, group, fine):

        @pl.when((begin + f <= high) & (begin + f + fine > low))
        def _(f=f):
            factors = down_ref[f : f + fine].reshape(fine * rank2, down_ref.shape[2])
            product = lax.dot_general(
                rows[...], factors, (((1,), (1,)), ((), ())), preferred_element_type=F32
            )
            which = which_ref[...] - (begin + f)
            found = acc[...]
            for q in range(fine):
                part = product[:, q * rank2 : (q + 1) * rank2]
                found = found + jnp.where(which == q, part, 0.0)
            acc[...] = found

    @pl.when(step == pl.num_programs(0) - 1)
    def _():
        total = sum(sizes)
        upper, lower = acc[: total // 2, :], acc[total // 2 :, :]
        keys = jnp.concatenate([upper[:, :ADAPTER_RANK], lower[:, :ADAPTER_RANK]], axis=1)
        values = jnp.concatenate([upper[:, ADAPTER_RANK:], lower[:, ADAPTER_RANK:]], axis=1)
        mine_ref[...] = jnp.where(second, values, keys)
        other_ref[...] = jnp.where(second, keys, values)


def shrink(blocks, names, down, half, later_than=()):
    sizes = tuple(b.shape[0] for b in blocks)
    total = sum(sizes)
    owned, rank2, width = down.shape
    group = next(g for g in (4, 3, 2, 1) if owned % g == 0)
    fine = next(g for g in (2, 3, 1) if group % g == 0)
    low = jnp.minimum(jnp.min(names), owned - 1)
    high = jnp.maximum(jnp.max(jnp.where(names < owned, names, 0)), low)
    line = jax.ShapeDtypeStruct((total // 2, 2 * ADAPTER_RANK), F32)
    return pl.pallas_call(
        functools.partial(shrink_kernel, sizes, group, fine, len(later_than)),
        grid_spec=pltpu.PrefetchScalarGridSpec(
            num_scalar_prefetch=1,
            grid=(owned // group,),
            in_specs=[
                pl.BlockSpec((total, 1), lambda i, p: (0, 0)),
                pl.BlockSpec(
                    (group, rank2, width),
                    lambda i, p: (jnp.minimum(p[0] // group + i, p[1] // group), 0, 0),
                ),
            ]
            + [pl.BlockSpec((s, width), lambda i, p: (0, 0)) for s in sizes]
            + [ANYWHERE] * len(later_than),
            out_specs=[pl.BlockSpec((total // 2, rank2), lambda i, p: (0, 0))] * 2,
            scratch_shapes=[pltpu.VMEM((total, width), BF16), pltpu.VMEM((total, rank2), F32)],
        ),
        out_shape=[line, line],
        compiler_params=PARAMS,
        cost_estimate=cost(total, width, owned * rank2),
        name="shrink",
    )(jnp.stack([low, high, half]).astype(I32), names.reshape(-1, 1), down, *blocks, *later_than)


def split(x, terms):
    parts = []
    for _ in range(terms - 1):
        parts.append(x.astype(BF16).astype(F32))
        x = x - parts[-1]
    return parts + [x]


def expand_kernel(sizes, heard, which_ref, scale_ref, up_ref, *refs):
    lines, outs = refs[:heard], refs[heard:]
    total = lines[0][...]
    for line in lines[1:]:
        total = total + line[...]
    upper, lower = total[:, :ADAPTER_RANK], total[:, ADAPTER_RANK:]
    twice = jnp.concatenate(
        [jnp.concatenate([upper, upper], axis=1), jnp.concatenate([lower, lower], axis=1)], axis=0
    )
    which = which_ref[...]
    parity = jnp.where(lax.broadcasted_iota(I32, (1, 2 * ADAPTER_RANK), 1) >= ADAPTER_RANK, 1, 0)
    pairs = up_ref.shape[0] // (2 * ADAPTER_RANK)
    wanted = [which == 2 * p + parity for p in range(pairs)]
    delta = None
    for term in split(twice, 3):
        spread = jnp.concatenate([jnp.where(w, term, 0.0).astype(BF16) for w in wanted], axis=1)
        product = jnp.dot(spread, up_ref[...], preferred_element_type=F32)
        delta = product if delta is None else delta + product
    adapters = lax.broadcasted_iota(I32, scale_ref.shape, 1)
    gain = jnp.sum(jnp.where(which == adapters, scale_ref[...], 0.0), axis=1, keepdims=True)
    delta = delta * gain
    begin = 0
    for size, out in zip(sizes, outs):
        out[...] = delta[begin : begin + size, :]
        begin += size


def expand(lines, names, scale, up, sizes):
    columns = up.shape[1]
    return pl.pallas_call(
        functools.partial(expand_kernel, sizes, len(lines)),
        out_shape=[jax.ShapeDtypeStruct((s, columns), F32) for s in sizes],
        compiler_params=PARAMS,
        cost_estimate=cost(sum(sizes), up.shape[0], columns, 3),
        name="expand",
    )(names.reshape(-1, 1), scale, up, *lines)


def merge_kernel(begins, parts, target_ref, *refs):
    blocks, out_ref = refs[parts:-1], refs[-1]
    returned = jnp.concatenate([b[...] for b in blocks], axis=0)
    target = target_ref[...]
    place = jnp.concatenate(
        [
            jnp.where(
                target == begin + lax.broadcasted_iota(I32, (1, block.shape[0]), 1), 1.0, 0.0
            ).astype(BF16)
            for begin, block in zip(begins, blocks)
        ],
        axis=1,
    )
    total = refs[0][...]
    for part in refs[1:parts]:
        total = total + part[...]
    for term in split(returned, 3):
        total = total + jnp.dot(place, term.astype(BF16), preferred_element_type=F32)
    out_ref[...] = total.astype(out_ref.dtype)


def merge(parts, target, begins, blocks, kind):
    return pl.pallas_call(
        functools.partial(merge_kernel, tuple(begins), len(parts)),
        out_shape=jax.ShapeDtypeStruct(parts[0].shape, kind),
        compiler_params=PARAMS,
        cost_estimate=cost(parts[0].shape[0], sum(b.shape[0] for b in blocks), parts[0].shape[1], 3),
        name="merge",
    )(target, *parts, *blocks)


def swap(x, axes, size, distance):
    return lax.ppermute(x, axes, [(i, i ^ distance) for i in range(size)])


def up_to_16(count):
    return -(-count // 16) * 16


def local(
    tokens,
    key_value_weight,
    adapter_down_weight,
    adapter_up_weight,
    adapter_scale,
    token_adapter_index,
):
    feature_axes = ("tensor", "sub")
    rows = tokens.shape[0]
    owned = adapter_down_weight.shape[0]
    owners = lax.axis_size("dp")
    sharers = lax.axis_size(feature_axes)
    me = lax.axis_index("dp")
    half = (lax.axis_index(feature_axes) >= sharers // 2).astype(I32)
    cap = up_to_16(owned * TOKEN_LIMIT)

    if owners == 4:
        usual = up_to_16(cap * 5 // 6)
        most = up_to_16(usual * 4 // 5)
        near = [(1, 0, cap)]
        far = [[(3, 0, most), (2, 0, most)], [(3, most, usual - most), (2, most, usual - most)]]
        extra = [(3, usual, cap - usual), (2, usual, cap - usual)]
    else:
        usual, near, extra = cap, [(1, 0, cap)], []
        far = [[(j, 0, cap) for j in range(2, owners)]]
    head = far[0]
    own = (0, 0, cap)

    ids_row = token_adapter_index.reshape(1, rows)
    ids_all = lax.all_gather(ids_row, ("parts", "dp"), axis=0, tiled=True)
    rest = near + [p for s in far[1:] for p in s] + extra + [own]
    sent_first, sent_rest, target = sort_rows(
        tokens, ids_row, me.reshape(1), owners, owned, cap, head, rest
    )
    packed = dict(zip(head + rest, sent_first + sent_rest))
    received = {p: swap(packed[p], "dp", owners, p[0]) for s in [near, *far] for p in s}

    group_of = lax.axis_index("parts") * owners
    sources = group_of + (me ^ jnp.arange(owners, dtype=I32))
    everyone = jnp.arange(ids_all.shape[0], dtype=I32)
    chosen = sources[:, None, None] == everyone[None, :, None]
    heard = jnp.sum(jnp.where(chosen, ids_all[None], 0), axis=1, dtype=I32) - me * owned
    adapters = jnp.arange(owned, dtype=I32)
    upto = jnp.sum(
        (heard[:, None, :] >= 0) & (heard[:, None, :] <= adapters[None, :, None]), axis=2, dtype=I32
    )
    at = jnp.arange(cap, dtype=I32)
    which = jnp.sum(upto[:, None, :] <= at[None, :, None], axis=2, dtype=I32)

    if owned % 2:
        adapter_up_weight = jnp.pad(adapter_up_weight, ((0, 1), (0, 0), (0, 0)))
    up = adapter_up_weight.reshape(-1, adapter_up_weight.shape[2])
    scale = adapter_scale.reshape(1, owned)

    def shares(pieces, blocks, later_than):
        names = jnp.concatenate([which[b, f : f + c] for b, f, c in pieces])
        mine, other = shrink(blocks, names, adapter_down_weight, half, later_than)
        lines = [mine] + [
            swap(mine if d < sharers // 2 else other, feature_axes, sharers, d)
            for d in range(1, sharers)
        ]
        return expand(lines, names, scale, up, tuple(c for _, _, c in pieces))

    def begins(pieces):
        return [b * cap + f for b, f, _ in pieces]

    arrived = received[near[0]]
    base_part = base_product(tokens, key_value_weight, arrived)
    base = lax.psum_scatter(base_part, feature_axes, scatter_dimension=1, tiled=True)
    at_hand = [own] + near
    deltas = shares(at_hand, [packed[own]] + [received[p] for p in near], (base_part,))
    total = jnp.zeros((rows, up.shape[1]), F32)
    total = merge([total], target, begins([own]), deltas[:1], F32)

    if extra:
        counts = jnp.sum(
            (ids_all[:, None, :] >= owned * jnp.arange(owners, dtype=I32)[None, :, None])
            & (ids_all[:, None, :] < owned * (1 + jnp.arange(owners, dtype=I32))[None, :, None]),
            axis=2,
            dtype=I32,
        )
        away = (everyone[:, None] % owners) ^ jnp.arange(owners, dtype=I32)[None, :]
        more = jnp.max(jnp.where(away >= 2, counts, 0)) > usual

        def with_extra(so_far):
            blocks = [swap(packed[p], "dp", owners, p[0]) for p in extra]
            found = shares(extra, blocks, ())
            back = [swap(d, "dp", owners, p[0]) for p, d in zip(extra, found)]
            return merge([so_far], target, begins(extra), back, F32)

        total = lax.cond(more, with_extra, lambda so_far: so_far, total)

    last = total
    returned = [swap(d, "dp", owners, p[0]) for p, d in zip(near, deltas[1:])]
    for pieces in far:
        deltas = shares(pieces, [received[p] for p in pieces], (last,))
        returned += [swap(d, "dp", owners, p[0]) for p, d in zip(pieces, deltas)]
        last = deltas[0]
    pieces = near + [p for s in far for p in s]
    return merge([base, total], target, begins(pieces), returned, BF16)


def solution(mesh):
    return jax.shard_map(
        local,
        mesh=mesh,
        in_specs=(
            P(("parts", "dp"), ("tensor", "sub")),
            P(("tensor", "sub"), None),
            P("dp", None, ("tensor", "sub")),
            P("dp", None, ("tensor", "sub")),
            P("dp"),
            P(("parts", "dp"), None),
        ),
        out_specs=P(("parts", "dp"), ("tensor", "sub")),
        check_vma=False,
    )
```

```python
import functools

import jax
import jax.numpy as jnp
from jax import lax
from jax.experimental import pallas as pl
from jax.experimental.pallas import tpu as pltpu
from jax.sharding import PartitionSpec as P

ADAPTER_RANK = 64
TOKEN_LIMIT = 12
VMEM_LIMIT = 48 * 1024 * 1024
F32 = jnp.float32
BF16 = jnp.bfloat16
I32 = jnp.int32
ANYWHERE = pl.BlockSpec(memory_space=pl.ANY)
PARAMS = pltpu.CompilerParams(vmem_limit_bytes=VMEM_LIMIT)


def cost(rows, depth, columns, terms=1):
    return pl.CostEstimate(
        flops=2 * rows * depth * columns * terms,
        transcendentals=0,
        bytes_accessed=2 * terms * (rows + columns) * depth + 4 * rows * columns,
    )


def owner_of(ids, owners, owned):
    total = jnp.zeros_like(ids)
    for o in range(1, owners):
        total = total + jnp.where(ids >= o * owned, 1, 0)
    return total


def as_column(line):
    size = line.shape[1]
    here = lax.broadcasted_iota(I32, (size, size), 0) == lax.broadcasted_iota(I32, (size, size), 1)
    return jnp.sum(jnp.where(here, line, 0), axis=1, keepdims=True)


def route_kernel(owners, owned, cap, me_ref, row_ref, slot_ref, target_ref):
    rows = row_ref.shape[1]
    id_row = row_ref[...]
    key_row = id_row * rows + lax.broadcasted_iota(I32, (1, rows), 1)
    key_col = as_column(key_row)
    own_row = owner_of(id_row, owners, owned)
    before = (key_col < key_row) & (key_col >= own_row * (owned * rows))
    rank = jnp.sum(jnp.where(before, 1, 0), axis=0, keepdims=True)
    found = (own_row ^ me_ref[0]) * cap + rank
    slot_ref[...] = found
    target_ref[...] = as_column(found)


def route(ids_row, me, owners, owned, cap):
    rows = ids_row.shape[1]
    return pl.pallas_call(
        functools.partial(route_kernel, owners, owned, cap),
        in_specs=[
            pl.BlockSpec(memory_space=pltpu.SMEM),
            pl.BlockSpec(memory_space=pltpu.VMEM),
        ],
        out_shape=[jax.ShapeDtypeStruct((1, rows), I32), jax.ShapeDtypeStruct((rows, 1), I32)],
        compiler_params=PARAMS,
        cost_estimate=cost(rows, rows, 8),
        name="route",
    )(me, ids_row)


def sort_kernel(cap, pieces, waits, slot_ref, tok_ref, *refs):
    for (block, first, count), out in zip(pieces, refs[waits:]):
        at = block * cap + first + lax.broadcasted_iota(I32, (count, slot_ref.shape[1]), 0)
        place = jnp.where(at == slot_ref[...], 1.0, 0.0).astype(BF16)
        out[...] = jnp.dot(place, tok_ref[...], preferred_element_type=F32).astype(BF16)


def sort_rows(tokens, slot, cap, pieces, later_than=()):
    rows, width = tokens.shape
    step = min(512, width)
    return pl.pallas_call(
        functools.partial(sort_kernel, cap, pieces, len(later_than)),
        grid=(width // step,),
        in_specs=[
            pl.BlockSpec((1, rows), lambda i: (0, 0)),
            pl.BlockSpec((rows, step), lambda i: (0, i)),
        ]
        + [ANYWHERE] * len(later_than),
        out_specs=[pl.BlockSpec((count, step), lambda i: (0, i)) for _, _, count in pieces],
        out_shape=[jax.ShapeDtypeStruct((count, width), BF16) for _, _, count in pieces],
        compiler_params=PARAMS,
        cost_estimate=cost(sum(c for _, _, c in pieces), rows, width),
        name="sort",
    )(slot, tokens, *later_than)


def name_kernel(owners, owned, sets, here_ref, *refs):
    lines, outs, plan_ref, most_ref = refs[:owners], refs[owners:-2], refs[-2], refs[-1]
    me, half = here_ref[0], here_ref[1]
    held = -(-owned // 8) * 8
    owner = lax.broadcasted_iota(I32, (-(-owners // 8) * 8, 1), 0)
    adapter = lax.broadcasted_iota(I32, (held, 1), 0)
    diagonal = adapter == lax.broadcasted_iota(I32, (held, 128), 1)
    used = lax.broadcasted_iota(I32, (1, 128), 1) < owned
    most = jnp.zeros(owner.shape, I32)
    ends = []
    for j, line in enumerate(lines):
        ids = line[...]
        chosen = jnp.where(owner_of(ids, owners, owned) == owner, 1, 0)
        count = jnp.sum(chosen, axis=1, keepdims=True)
        far = (me ^ j ^ owner >= 2) & (owner < owners)
        most = jnp.maximum(most, jnp.where(far, count, 0))
        mine = ids - me * owned
        upto = jnp.sum(jnp.where((mine >= 0) & (mine <= adapter), 1, 0), axis=1, keepdims=True)
        across = jnp.sum(jnp.where(diagonal, upto, 0), axis=0, keepdims=True)
        ends.append(jnp.where(used, across, 1 << 20))
    most_ref[...] = jnp.broadcast_to(jnp.max(most, axis=0, keepdims=True), most_ref.shape)
    for k, (pieces, out) in enumerate(zip(sets, outs)):
        begin, low, high = 0, owned - 1, 0
        for block, first, count in pieces:
            at = first + lax.broadcasted_iota(I32, (count, 1), 0)
            names = jnp.sum(jnp.where(ends[block] <= at, 1, 0), axis=1, keepdims=True)
            out[begin : begin + count, :] = names
            low = jnp.minimum(low, jnp.min(names))
            high = jnp.maximum(high, jnp.max(jnp.where(names < owned, names, 0)))
            begin += count
        plan_ref[3 * k] = low
        plan_ref[3 * k + 1] = jnp.maximum(low, high)
        plan_ref[3 * k + 2] = half


def name_rows(lines, here, owned, sets):
    totals = [sum(c for _, _, c in pieces) for pieces in sets]
    on_chip, scalars = (pl.BlockSpec(memory_space=m) for m in (pltpu.VMEM, pltpu.SMEM))
    *names, plan, most = pl.pallas_call(
        functools.partial(name_kernel, len(lines), owned, sets),
        in_specs=[scalars] + [on_chip] * len(lines),
        out_specs=[on_chip] * len(sets) + [scalars, on_chip],
        out_shape=[jax.ShapeDtypeStruct((t, 1), I32) for t in totals]
        + [jax.ShapeDtypeStruct((3 * len(sets),), I32), jax.ShapeDtypeStruct((1, 128), I32)],
        compiler_params=PARAMS,
        cost_estimate=cost(sum(totals), owned, 8),
        name="name_rows",
    )(here, *lines)
    plans = [plan[3 * k : 3 * k + 3] for k in range(len(sets))]
    return names, plans, most


def base_kernel(tok_ref, weight_ref, _, out_ref):
    out_ref[...] = jnp.dot(tok_ref[...], weight_ref[...], preferred_element_type=F32)


def base_product(tokens, weight, later_than):
    (rows, width), columns = tokens.shape, weight.shape[1]
    step = min(256, columns)
    return pl.pallas_call(
        base_kernel,
        grid=(columns // step,),
        in_specs=[
            pl.BlockSpec((rows, width), lambda i: (0, 0)),
            pl.BlockSpec((width, step), lambda i: (0, i)),
            ANYWHERE,
        ],
        out_specs=pl.BlockSpec((rows, step), lambda i: (0, i)),
        out_shape=jax.ShapeDtypeStruct((rows, columns), F32),
        compiler_params=PARAMS,
        cost_estimate=cost(rows, width, columns),
        name="base",
    )(tokens, weight, later_than)


def shrink_kernel(sizes, group, fine, waits, plan_ref, which_ref, down_ref, *refs):
    blocks, (mine_ref, other_ref, rows, acc) = refs[: len(sizes)], refs[len(sizes) + waits :]
    step, rank2 = pl.program_id(0), 2 * ADAPTER_RANK
    low, high, second = plan_ref[0], plan_ref[1], plan_ref[2] == 1
    begin = (low // group + step) * group

    @pl.when(step == 0)
    def _():
        at = 0
        for size, block in zip(sizes, blocks):
            rows[at : at + size, :] = block[...]
            at += size
        acc[...] = jnp.zeros_like(acc)

    for f in range(0, group, fine):

        @pl.when((begin + f <= high) & (begin + f + fine > low))
        def _(f=f):
            factors = down_ref[f : f + fine].reshape(fine * rank2, down_ref.shape[2])
            product = lax.dot_general(
                rows[...], factors, (((1,), (1,)), ((), ())), preferred_element_type=F32
            )
            which = which_ref[...] - (begin + f)
            found = acc[...]
            for q in range(fine):
                part = product[:, q * rank2 : (q + 1) * rank2]
                found = found + jnp.where(which == q, part, 0.0)
            acc[...] = found

    @pl.when(step == pl.num_programs(0) - 1)
    def _():
        total = sum(sizes)
        upper, lower = acc[: total // 2, :], acc[total // 2 :, :]
        keys = jnp.concatenate([upper[:, :ADAPTER_RANK], lower[:, :ADAPTER_RANK]], axis=1)
        values = jnp.concatenate([upper[:, ADAPTER_RANK:], lower[:, ADAPTER_RANK:]], axis=1)
        mine_ref[...] = jnp.where(second, values, keys)
        other_ref[...] = jnp.where(second, keys, values)


def shrink(blocks, names, plan, down, later_than=()):
    sizes = tuple(b.shape[0] for b in blocks)
    total = sum(sizes)
    owned, rank2, width = down.shape
    group = next(g for g in (4, 3, 2, 1) if owned % g == 0)
    fine = next(g for g in (2, 3, 1) if group % g == 0)
    line = jax.ShapeDtypeStruct((total // 2, 2 * ADAPTER_RANK), F32)
    return pl.pallas_call(
        functools.partial(shrink_kernel, sizes, group, fine, len(later_than)),
        grid_spec=pltpu.PrefetchScalarGridSpec(
            num_scalar_prefetch=1,
            grid=(owned // group,),
            in_specs=[
                pl.BlockSpec((total, 1), lambda i, p: (0, 0)),
                pl.BlockSpec(
                    (group, rank2, width),
                    lambda i, p: (jnp.minimum(p[0] // group + i, p[1] // group), 0, 0),
                ),
            ]
            + [pl.BlockSpec((s, width), lambda i, p: (0, 0)) for s in sizes]
            + [ANYWHERE] * len(later_than),
            out_specs=[pl.BlockSpec((total // 2, rank2), lambda i, p: (0, 0))] * 2,
            scratch_shapes=[pltpu.VMEM((total, width), BF16), pltpu.VMEM((total, rank2), F32)],
        ),
        out_shape=[line, line],
        compiler_params=PARAMS,
        cost_estimate=cost(total, width, owned * rank2),
        name="shrink",
    )(plan, names, down, *blocks, *later_than)


def split(x, terms):
    parts = []
    for _ in range(terms - 1):
        parts.append(x.astype(BF16).astype(F32))
        x = x - parts[-1]
    return parts + [x]


def expand_kernel(sizes, heard, which_ref, scale_ref, up_ref, *refs):
    lines, outs = refs[:heard], refs[heard:]
    total = lines[0][...]
    for line in lines[1:]:
        total = total + line[...]
    upper, lower = total[:, :ADAPTER_RANK], total[:, ADAPTER_RANK:]
    twice = jnp.concatenate(
        [jnp.concatenate([upper, upper], axis=1), jnp.concatenate([lower, lower], axis=1)], axis=0
    )
    which = which_ref[...]
    parity = jnp.where(lax.broadcasted_iota(I32, (1, 2 * ADAPTER_RANK), 1) >= ADAPTER_RANK, 1, 0)
    pairs = up_ref.shape[0] // (2 * ADAPTER_RANK)
    wanted = [which == 2 * p + parity for p in range(pairs)]
    delta = None
    for term in split(twice, 3):
        spread = jnp.concatenate([jnp.where(w, term, 0.0).astype(BF16) for w in wanted], axis=1)
        product = jnp.dot(spread, up_ref[...], preferred_element_type=F32)
        delta = product if delta is None else delta + product
    adapters = lax.broadcasted_iota(I32, scale_ref.shape, 1)
    gain = jnp.sum(jnp.where(which == adapters, scale_ref[...], 0.0), axis=1, keepdims=True)
    delta = delta * gain
    begin = 0
    for size, out in zip(sizes, outs):
        out[...] = delta[begin : begin + size, :]
        begin += size


def expand(lines, names, scale, up, sizes):
    columns = up.shape[1]
    return pl.pallas_call(
        functools.partial(expand_kernel, sizes, len(lines)),
        out_shape=[jax.ShapeDtypeStruct((s, columns), F32) for s in sizes],
        compiler_params=PARAMS,
        cost_estimate=cost(sum(sizes), up.shape[0], columns, 3),
        name="expand",
    )(names, scale, up, *lines)


def merge_kernel(begins, parts, target_ref, *refs):
    blocks, out_ref = refs[parts:-1], refs[-1]
    returned = jnp.concatenate([b[...] for b in blocks], axis=0)
    target = target_ref[...]
    place = jnp.concatenate(
        [
            jnp.where(
                target == begin + lax.broadcasted_iota(I32, (1, block.shape[0]), 1), 1.0, 0.0
            ).astype(BF16)
            for begin, block in zip(begins, blocks)
        ],
        axis=1,
    )
    total = refs[0][...]
    for part in refs[1:parts]:
        total = total + part[...]
    for term in split(returned, 3):
        total = total + jnp.dot(place, term.astype(BF16), preferred_element_type=F32)
    out_ref[...] = total.astype(out_ref.dtype)


def merge(parts, target, begins, blocks, kind):
    return pl.pallas_call(
        functools.partial(merge_kernel, tuple(begins), len(parts)),
        out_shape=jax.ShapeDtypeStruct(parts[0].shape, kind),
        compiler_params=PARAMS,
        cost_estimate=cost(parts[0].shape[0], sum(b.shape[0] for b in blocks), parts[0].shape[1], 3),
        name="merge",
    )(target, *parts, *blocks)


def swap(x, axes, size, distance):
    return lax.ppermute(x, axes, [(i, i ^ distance) for i in range(size)])


def up_to_16(count):
    return -(-count // 16) * 16


def local(
    tokens,
    key_value_weight,
    adapter_down_weight,
    adapter_up_weight,
    adapter_scale,
    token_adapter_index,
):
    feature_axes = ("tensor", "sub")
    rows = tokens.shape[0]
    owned = adapter_down_weight.shape[0]
    owners = lax.axis_size("dp")
    sharers = lax.axis_size(feature_axes)
    me = lax.axis_index("dp")
    half = (lax.axis_index(feature_axes) >= sharers // 2).astype(I32)
    cap = up_to_16(owned * TOKEN_LIMIT)

    own, near = (0, 0, cap), (1, 0, cap)
    if owners == 4:
        usual = up_to_16(cap * 5 // 6)
        most = up_to_16(usual * 4 // 5)
        far = [[(3, 0, most), (2, 0, most)], [(3, most, usual - most), (2, most, usual - most)]]
        extra = [(3, usual, cap - usual), (2, usual, cap - usual)]
    else:
        usual, far, extra = cap, [[(j, 0, cap) for j in range(2, owners)]], []

    ids_row = token_adapter_index.reshape(1, rows)
    ids_heard = [ids_row] + [swap(ids_row, "dp", owners, j) for j in range(1, owners)]
    slot, target = route(ids_row, me.reshape(1), owners, owned, cap)
    early = sort_rows(tokens, slot, cap, far[0], tuple(ids_heard[1:]))
    later = [near] + [p for s in far[1:] for p in s] + [own] + extra
    packed = dict(zip(far[0] + later, early + sort_rows(tokens, slot, cap, later, early[:1])))
    sent = [p for s in far for p in s] + [near]
    received = {p: swap(packed[p], "dp", owners, p[0]) for p in sent}

    sets = [[own, near]] + far + ([extra] if extra else [])
    here = jnp.stack([me.astype(I32), half])
    names, plans, largest = name_rows(ids_heard, here, owned, sets)

    if owned % 2:
        adapter_up_weight = jnp.pad(adapter_up_weight, ((0, 1), (0, 0), (0, 0)))
    up = adapter_up_weight.reshape(-1, adapter_up_weight.shape[2])
    scale = adapter_scale.reshape(1, owned)

    def deltas_of(blocks, names, plan, down, up, scale, later_than):
        mine, other = shrink(blocks, names, plan, down, later_than)
        lines = [mine] + [
            swap(mine if d < sharers // 2 else other, feature_axes, sharers, d)
            for d in range(1, sharers)
        ]
        return expand(lines, names, scale, up, tuple(b.shape[0] for b in blocks))

    def send_back(pieces, deltas):
        return [swap(d, "dp", owners, p[0]) for p, d in zip(pieces, deltas)]

    def begins(pieces):
        return [b * cap + f for b, f, _ in pieces]

    weights = (adapter_down_weight, up, scale)
    base_part = base_product(tokens, key_value_weight, packed[own])
    base = lax.psum_scatter(base_part, feature_axes, scatter_dimension=1, tiled=True)
    blocks = [packed[own], received[near]]
    deltas = deltas_of(blocks, names[0], plans[0], *weights, (base_part,))
    returned = [deltas[0]] + send_back([near], deltas[1:])
    done = [own, near]
    for k, pieces in enumerate(far):
        blocks = [received[p] for p in pieces]
        deltas = deltas_of(blocks, names[1 + k], plans[1 + k], *weights, (deltas[0],))
        returned += send_back(pieces, deltas)
        done += pieces

    def finish(base, target, returned, *_):
        return merge([base], target, begins(done), returned, BF16)

    if not extra:
        return finish(base, target, returned)

    def finish_with_extra(base, target, returned, blocks, names, plan, weights):
        blocks = send_back(extra, blocks)
        deltas = send_back(extra, deltas_of(blocks, names, plan, *weights, ()))
        return merge([base], target, begins(done + extra), returned + deltas, BF16)

    for d in range(1, lax.axis_size("parts")):
        largest = jnp.maximum(largest, swap(largest, "parts", lax.axis_size("parts"), d))
    return lax.cond(
        largest[0, 0] > usual,
        finish_with_extra,
        finish,
        base,
        target,
        returned,
        [packed[p] for p in extra],
        names[-1],
        plans[-1],
        weights,
    )


def solution(mesh):
    return jax.shard_map(
        local,
        mesh=mesh,
        in_specs=(
            P(("parts", "dp"), ("tensor", "sub")),
            P(("tensor", "sub"), None),
            P("dp", None, ("tensor", "sub")),
            P("dp", None, ("tensor", "sub")),
            P("dp"),
            P(("parts", "dp"), None),
        ),
        out_specs=P(("parts", "dp"), ("tensor", "sub")),
        check_vma=False,
    )
```

```python
import functools

import jax
import jax.numpy as jnp
from jax import lax
from jax.experimental import pallas as pl
from jax.experimental.pallas import tpu as pltpu
from jax.sharding import PartitionSpec as P

ADAPTER_RANK = 64
TOKEN_LIMIT = 12
VMEM_LIMIT = 48 * 1024 * 1024
F32 = jnp.float32
BF16 = jnp.bfloat16
I32 = jnp.int32
ANYWHERE = pl.BlockSpec(memory_space=pl.ANY)
LIGHT = pl.CostEstimate(flops=1, transcendentals=0, bytes_accessed=1)
HEAVY = pl.CostEstimate(flops=26 * 10**9, transcendentals=0, bytes_accessed=1)
PARAMS = pltpu.CompilerParams(vmem_limit_bytes=VMEM_LIMIT)


def owner_of(ids, owners, owned):
    total = jnp.zeros_like(ids)
    for o in range(1, owners):
        total = total + jnp.where(ids >= o * owned, 1, 0)
    return total


def as_column(line):
    size = line.shape[1]
    here = lax.broadcasted_iota(I32, (size, size), 0) == lax.broadcasted_iota(I32, (size, size), 1)
    return jnp.sum(jnp.where(here, line, 0), axis=1, keepdims=True)


def route_kernel(owners, owned, cap, me_ref, row_ref, slot_ref, target_ref):
    rows = row_ref.shape[1]
    id_row = row_ref[...]
    key_row = id_row * rows + lax.broadcasted_iota(I32, (1, rows), 1)
    key_col = as_column(key_row)
    own_row = owner_of(id_row, owners, owned)
    before = (key_col < key_row) & (key_col >= own_row * (owned * rows))
    rank = jnp.sum(jnp.where(before, 1, 0), axis=0, keepdims=True)
    found = (own_row ^ me_ref[0]) * cap + rank
    slot_ref[...] = found
    target_ref[...] = as_column(found)


def route(ids_row, me, owners, owned, cap):
    rows = ids_row.shape[1]
    return pl.pallas_call(
        functools.partial(route_kernel, owners, owned, cap),
        in_specs=[
            pl.BlockSpec(memory_space=pltpu.SMEM),
            pl.BlockSpec(memory_space=pltpu.VMEM),
        ],
        out_shape=[jax.ShapeDtypeStruct((1, rows), I32), jax.ShapeDtypeStruct((rows, 1), I32)],
        compiler_params=PARAMS,
        cost_estimate=LIGHT,
        name="route",
    )(me, ids_row)


def sort_kernel(cap, pieces, waits, slot_ref, tok_ref, *refs):
    outs, place = refs[waits:-1], refs[-1]

    @pl.when(pl.program_id(0) == 0)
    def _():
        begin = 0
        for block, first, count in pieces:
            at = block * cap + first + lax.broadcasted_iota(I32, (count, slot_ref.shape[1]), 0)
            found = jnp.where(at == slot_ref[...], 1.0, 0.0).astype(BF16)
            place[begin : begin + count, :] = found
            begin += count

    moved = jnp.dot(place[...], tok_ref[...], preferred_element_type=F32).astype(BF16)
    begin = 0
    for (_, _, count), out in zip(pieces, outs):
        out[...] = moved[begin : begin + count, :]
        begin += count


def sort_rows(tokens, slot, cap, pieces, later_than=()):
    rows, width = tokens.shape
    step = min(512, width)
    return pl.pallas_call(
        functools.partial(sort_kernel, cap, pieces, len(later_than)),
        grid=(width // step,),
        in_specs=[
            pl.BlockSpec((1, rows), lambda i: (0, 0)),
            pl.BlockSpec((rows, step), lambda i: (0, i)),
        ]
        + [ANYWHERE] * len(later_than),
        out_specs=[pl.BlockSpec((count, step), lambda i: (0, i)) for _, _, count in pieces],
        out_shape=[jax.ShapeDtypeStruct((count, width), BF16) for _, _, count in pieces],
        scratch_shapes=[pltpu.VMEM((sum(c for _, _, c in pieces), rows), BF16)],
        compiler_params=PARAMS,
        cost_estimate=LIGHT,
        name="sort",
    )(slot, tokens, *later_than)


def name_kernel(owners, owned, sets, here_ref, *refs):
    lines, outs, plan_ref, most_ref = refs[:owners], refs[owners:-2], refs[-2], refs[-1]
    me, half = here_ref[0], here_ref[1]
    held = -(-owned // 8) * 8
    owner = lax.broadcasted_iota(I32, (-(-owners // 8) * 8, 1), 0)
    adapter = lax.broadcasted_iota(I32, (held, 1), 0)
    diagonal = adapter == lax.broadcasted_iota(I32, (held, 128), 1)
    used = lax.broadcasted_iota(I32, (1, 128), 1) < owned
    most = jnp.zeros(owner.shape, I32)
    ends = []
    for j, line in enumerate(lines):
        ids = line[...]
        chosen = jnp.where(owner_of(ids, owners, owned) == owner, 1, 0)
        count = jnp.sum(chosen, axis=1, keepdims=True)
        far = (me ^ j ^ owner >= 2) & (owner < owners)
        most = jnp.maximum(most, jnp.where(far, count, 0))
        mine = ids - me * owned
        upto = jnp.sum(jnp.where((mine >= 0) & (mine <= adapter), 1, 0), axis=1, keepdims=True)
        across = jnp.sum(jnp.where(diagonal, upto, 0), axis=0, keepdims=True)
        ends.append(jnp.where(used, across, 1 << 20))
    most_ref[...] = jnp.broadcast_to(jnp.max(most, axis=0, keepdims=True), most_ref.shape)
    for k, (pieces, out) in enumerate(zip(sets, outs)):
        begin, low, high = 0, owned - 1, 0
        for block, first, count in pieces:
            at = first + lax.broadcasted_iota(I32, (count, 1), 0)
            names = jnp.sum(jnp.where(ends[block] <= at, 1, 0), axis=1, keepdims=True)
            out[begin : begin + count, :] = names
            low = jnp.minimum(low, jnp.min(names))
            high = jnp.maximum(high, jnp.max(jnp.where(names < owned, names, 0)))
            begin += count
        plan_ref[3 * k] = low
        plan_ref[3 * k + 1] = jnp.maximum(low, high)
        plan_ref[3 * k + 2] = half


def name_rows(lines, here, owned, sets):
    totals = [sum(c for _, _, c in pieces) for pieces in sets]
    on_chip, scalars = (pl.BlockSpec(memory_space=m) for m in (pltpu.VMEM, pltpu.SMEM))
    *names, plan, most = pl.pallas_call(
        functools.partial(name_kernel, len(lines), owned, sets),
        in_specs=[scalars] + [on_chip] * len(lines),
        out_specs=[on_chip] * len(sets) + [scalars, on_chip],
        out_shape=[jax.ShapeDtypeStruct((t, 1), I32) for t in totals]
        + [jax.ShapeDtypeStruct((3 * len(sets),), I32), jax.ShapeDtypeStruct((1, 128), I32)],
        compiler_params=PARAMS,
        cost_estimate=LIGHT,
        name="name_rows",
    )(here, *lines)
    plans = [plan[3 * k : 3 * k + 3] for k in range(len(sets))]
    return names, plans, most


def base_kernel(tok_ref, weight_ref, _, out_ref):
    out_ref[...] = jnp.dot(tok_ref[...], weight_ref[...], preferred_element_type=F32)


def base_product(tokens, weight, later_than):
    (rows, width), columns = tokens.shape, weight.shape[1]
    step = min(256, columns)
    return pl.pallas_call(
        base_kernel,
        grid=(columns // step,),
        in_specs=[
            pl.BlockSpec((rows, width), lambda i: (0, 0)),
            pl.BlockSpec((width, step), lambda i: (0, i)),
            ANYWHERE,
        ],
        out_specs=pl.BlockSpec((rows, step), lambda i: (0, i)),
        out_shape=jax.ShapeDtypeStruct((rows, columns), F32),
        compiler_params=PARAMS,
        cost_estimate=LIGHT,
        name="base",
    )(tokens, weight, later_than)


def shrink_kernel(sizes, group, fine, waits, plan_ref, which_ref, down_ref, *refs):
    blocks, (mine_ref, other_ref, rows, acc) = refs[: len(sizes)], refs[len(sizes) + waits :]
    step, rank2 = pl.program_id(0), 2 * ADAPTER_RANK
    low, high, second = plan_ref[0], plan_ref[1], plan_ref[2] == 1
    begin = (low // group + step) * group

    @pl.when(step == 0)
    def _():
        at = 0
        for size, block in zip(sizes, blocks):
            rows[at : at + size, :] = block[...]
            at += size
        acc[...] = jnp.zeros_like(acc)

    for f in range(0, group, fine):

        @pl.when((begin + f <= high) & (begin + f + fine > low))
        def _(f=f):
            factors = down_ref[f : f + fine].reshape(fine * rank2, down_ref.shape[2])
            product = lax.dot_general(
                rows[...], factors, (((1,), (1,)), ((), ())), preferred_element_type=F32
            )
            which = which_ref[...] - (begin + f)
            found = acc[...]
            for q in range(fine):
                part = product[:, q * rank2 : (q + 1) * rank2]
                found = found + jnp.where(which == q, part, 0.0)
            acc[...] = found

    @pl.when(step == pl.num_programs(0) - 1)
    def _():
        total = sum(sizes)
        upper, lower = acc[: total // 2, :], acc[total // 2 :, :]
        keys = jnp.concatenate([upper[:, :ADAPTER_RANK], lower[:, :ADAPTER_RANK]], axis=1)
        values = jnp.concatenate([upper[:, ADAPTER_RANK:], lower[:, ADAPTER_RANK:]], axis=1)
        mine_ref[...] = jnp.where(second, values, keys)
        other_ref[...] = jnp.where(second, keys, values)


def shrink(blocks, names, plan, down, later_than=(), cost=LIGHT):
    sizes = tuple(b.shape[0] for b in blocks)
    total = sum(sizes)
    owned, rank2, width = down.shape
    group = next(g for g in (4, 3, 2, 1) if owned % g == 0)
    fine = next(g for g in (2, 3, 1) if group % g == 0)
    line = jax.ShapeDtypeStruct((total // 2, 2 * ADAPTER_RANK), F32)
    return pl.pallas_call(
        functools.partial(shrink_kernel, sizes, group, fine, len(later_than)),
        grid_spec=pltpu.PrefetchScalarGridSpec(
            num_scalar_prefetch=1,
            grid=(owned // group,),
            in_specs=[
                pl.BlockSpec((total, 1), lambda i, p: (0, 0)),
                pl.BlockSpec(
                    (group, rank2, width),
                    lambda i, p: (jnp.minimum(p[0] // group + i, p[1] // group), 0, 0),
                ),
            ]
            + [pl.BlockSpec((s, width), lambda i, p: (0, 0)) for s in sizes]
            + [ANYWHERE] * len(later_than),
            out_specs=[pl.BlockSpec((total // 2, rank2), lambda i, p: (0, 0))] * 2,
            scratch_shapes=[pltpu.VMEM((total, width), BF16), pltpu.VMEM((total, rank2), F32)],
        ),
        out_shape=[line, line],
        compiler_params=PARAMS,
        cost_estimate=cost,
        name="shrink",
    )(plan, names, down, *blocks, *later_than)


def split(x, terms):
    parts = []
    for _ in range(terms - 1):
        parts.append(x.astype(BF16).astype(F32))
        x = x - parts[-1]
    return parts + [x]


def expand_kernel(groups, sizes, heard, which_ref, scale_ref, up_ref, *refs):
    lines, outs = refs[:heard], refs[heard:]
    total = lines[0][...]
    for line in lines[1:]:
        total = total + line[...]
    twice, begin = [], 0
    for count in groups:
        lines = total[begin : begin + count, :]
        for side in (lines[:, :ADAPTER_RANK], lines[:, ADAPTER_RANK:]):
            twice.append(jnp.concatenate([side, side], axis=1))
        begin += count
    twice = jnp.concatenate(twice, axis=0)
    which = which_ref[...]
    parity = jnp.where(lax.broadcasted_iota(I32, (1, 2 * ADAPTER_RANK), 1) >= ADAPTER_RANK, 1, 0)
    pairs = up_ref.shape[0] // (2 * ADAPTER_RANK)
    wanted = [which == 2 * p + parity for p in range(pairs)]
    delta = None
    for term in split(twice, 3):
        spread = jnp.concatenate([jnp.where(w, term, 0.0).astype(BF16) for w in wanted], axis=1)
        product = jnp.dot(spread, up_ref[...], preferred_element_type=F32)
        delta = product if delta is None else delta + product
    adapters = lax.broadcasted_iota(I32, scale_ref.shape, 1)
    gain = jnp.sum(jnp.where(which == adapters, scale_ref[...], 0.0), axis=1, keepdims=True)
    delta = delta * gain
    begin = 0
    for size, out in zip(sizes, outs):
        out[...] = delta[begin : begin + size, :]
        begin += size


def expand(lines, groups, names, scale, up, sizes):
    columns = up.shape[1]
    return pl.pallas_call(
        functools.partial(expand_kernel, groups, sizes, len(lines)),
        out_shape=[jax.ShapeDtypeStruct((s, columns), F32) for s in sizes],
        compiler_params=PARAMS,
        cost_estimate=LIGHT,
        name="expand",
    )(names, scale, up, *lines)


def merge_kernel(begins, parts, target_ref, *refs):
    blocks, out_ref = refs[parts:-1], refs[-1]
    returned = jnp.concatenate([b[...] for b in blocks], axis=0)
    target = target_ref[...]
    place = jnp.concatenate(
        [
            jnp.where(
                target == begin + lax.broadcasted_iota(I32, (1, block.shape[0]), 1), 1.0, 0.0
            ).astype(BF16)
            for begin, block in zip(begins, blocks)
        ],
        axis=1,
    )
    total = refs[0][...]
    for part in refs[1:parts]:
        total = total + part[...]
    for term in split(returned, 3):
        total = total + jnp.dot(place, term.astype(BF16), preferred_element_type=F32)
    out_ref[...] = total.astype(out_ref.dtype)


def merge(parts, target, begins, blocks, kind):
    return pl.pallas_call(
        functools.partial(merge_kernel, tuple(begins), len(parts)),
        out_shape=jax.ShapeDtypeStruct(parts[0].shape, kind),
        compiler_params=PARAMS,
        cost_estimate=LIGHT,
        name="merge",
    )(target, *parts, *blocks)


def swap(x, axes, size, distance):
    return lax.ppermute(x, axes, [(i, i ^ distance) for i in range(size)])


def up_to_16(count):
    return -(-count // 16) * 16


def local(
    tokens,
    key_value_weight,
    adapter_down_weight,
    adapter_up_weight,
    adapter_scale,
    token_adapter_index,
):
    feature_axes = ("tensor", "sub")
    rows = tokens.shape[0]
    owned = adapter_down_weight.shape[0]
    owners = lax.axis_size("dp")
    sharers = lax.axis_size(feature_axes)
    me = lax.axis_index("dp")
    half = (lax.axis_index(feature_axes) >= sharers // 2).astype(I32)
    cap = up_to_16(owned * TOKEN_LIMIT)

    own = (0, 0, cap)
    if owners == 4:
        usual = up_to_16(cap * 5 // 6)
        most = up_to_16(usual * 4 // 5)
        near = (1, 0, up_to_16(cap // 3))
        far = [
            [(3, 0, most), (2, 0, most), (1, near[2], cap - near[2])],
            [(3, most, usual - most), (2, most, usual - most)],
        ]
        extra = [(3, usual, cap - usual), (2, usual, cap - usual)]
    else:
        usual, near, far = cap, (1, 0, cap), [[(j, 0, cap) for j in range(2, owners)]]
        extra = []

    ids_row = token_adapter_index.reshape(1, rows)
    ids_heard = [ids_row] + [swap(ids_row, "dp", owners, j) for j in range(1, owners)]
    slot, target = route(ids_row, me.reshape(1), owners, owned, cap)
    sent = [near] + [p for s in far for p in s]
    packed = dict(zip(sent, sort_rows(tokens, slot, cap, sent, tuple(ids_heard[1:]))))
    received = {p: swap(packed[p], "dp", owners, p[0]) for p in sent}
    packed |= zip([own] + extra, sort_rows(tokens, slot, cap, [own] + extra, (received[near],)))

    sets = [[own], [near], [own, near]] + far + ([extra] if extra else [])
    here = jnp.stack([me.astype(I32), half])
    names, plans, largest = name_rows(ids_heard, here, owned, sets)

    if owned % 2:
        adapter_up_weight = jnp.pad(adapter_up_weight, ((0, 1), (0, 0), (0, 0)))
    up = adapter_up_weight.reshape(-1, adapter_up_weight.shape[2])
    scale = adapter_scale.reshape(1, owned)

    def exchange(mine, other):
        return [mine] + [
            swap(mine if d < sharers // 2 else other, feature_axes, sharers, d)
            for d in range(1, sharers)
        ]

    def deltas_of(blocks, names, plan, down, up, scale, later_than, cost=LIGHT):
        mine, other = shrink(blocks, names, plan, down, later_than, cost)
        sizes = tuple(b.shape[0] for b in blocks)
        return expand(exchange(mine, other), (mine.shape[0],), names, scale, up, sizes)

    def send_back(pieces, deltas):
        return [swap(d, "dp", owners, p[0]) for p, d in zip(pieces, deltas)]

    def begins(pieces):
        return [b * cap + f for b, f, _ in pieces]

    weights = (adapter_down_weight, up, scale)
    base_part = base_product(tokens, key_value_weight, received[near])
    base = lax.psum_scatter(base_part, feature_axes, scatter_dimension=1, tiled=True)
    first = shrink([packed[own]], names[0], plans[0], adapter_down_weight, (base_part,))
    second = shrink([received[near]], names[1], plans[1], adapter_down_weight, tuple(first[:1]))
    lines = exchange(*(jnp.concatenate(pair, axis=0) for pair in zip(first, second)))
    sizes = (cap, near[2])
    deltas = expand(lines, tuple(c // 2 for c in sizes), names[2], scale, up, sizes)
    returned = [deltas[0]] + send_back([near], deltas[1:])
    done = [own, near]
    for k, pieces in enumerate(far):
        blocks = [received[p] for p in pieces]
        cost = HEAVY if k and pieces is far[-1] else LIGHT
        deltas = deltas_of(blocks, names[3 + k], plans[3 + k], *weights, (deltas[0],), cost)
        returned += send_back(pieces, deltas)
        done += pieces

    def finish(base, target, returned, *_):
        return merge([base], target, begins(done), returned, BF16)

    if not extra:
        return finish(base, target, returned)

    def finish_with_extra(base, target, returned, blocks, names, plan, weights):
        blocks = send_back(extra, blocks)
        deltas = send_back(extra, deltas_of(blocks, names, plan, *weights, ()))
        return merge([base], target, begins(done + extra), returned + deltas, BF16)

    for d in range(1, lax.axis_size("parts")):
        largest = jnp.maximum(largest, swap(largest, "parts", lax.axis_size("parts"), d))
    return lax.cond(
        largest[0, 0] > usual,
        finish_with_extra,
        finish,
        base,
        target,
        returned,
        [packed[p] for p in extra],
        names[-1],
        plans[-1],
        weights,
    )


def solution(mesh):
    return jax.shard_map(
        local,
        mesh=mesh,
        in_specs=(
            P(("parts", "dp"), ("tensor", "sub")),
            P(("tensor", "sub"), None),
            P("dp", None, ("tensor", "sub")),
            P("dp", None, ("tensor", "sub")),
            P("dp"),
            P(("parts", "dp"), None),
        ),
        out_specs=P(("parts", "dp"), ("tensor", "sub")),
        check_vma=False,
    )
```

```python
import functools

import jax
import jax.numpy as jnp
from jax import lax
from jax.experimental import pallas as pl
from jax.experimental.pallas import tpu as pltpu
from jax.sharding import PartitionSpec as P

ADAPTER_RANK = 64
TOKEN_LIMIT = 12
VMEM_LIMIT = 28 * 1024 * 1024
F32 = jnp.float32
BF16 = jnp.bfloat16
I32 = jnp.int32
ANYWHERE = pl.BlockSpec(memory_space=pl.ANY)
COST = pl.CostEstimate(flops=10**9, transcendentals=0, bytes_accessed=1)
PARAMS = pltpu.CompilerParams(vmem_limit_bytes=VMEM_LIMIT)


def up_to_16(count):
    return -(-count // 16) * 16


def owner_of(ids, owners, owned):
    total = jnp.zeros_like(ids)
    for o in range(1, owners):
        total = total + jnp.where(ids >= o * owned, 1, 0)
    return total


def as_column(line):
    size = line.shape[1]
    here = lax.broadcasted_iota(I32, (size, size), 0) == lax.broadcasted_iota(I32, (size, size), 1)
    return jnp.sum(jnp.where(here, line, 0), axis=1, keepdims=True)


def route_kernel(owners, owned, cap, me_ref, row_ref, slot_ref, target_ref):
    rows = row_ref.shape[1]
    id_row = row_ref[...]
    key_row = id_row * rows + lax.broadcasted_iota(I32, (1, rows), 1)
    key_col = as_column(key_row)
    own_row = owner_of(id_row, owners, owned)
    before = (key_col < key_row) & (key_col >= own_row * (owned * rows))
    rank = jnp.sum(jnp.where(before, 1, 0), axis=0, keepdims=True)
    found = (own_row ^ me_ref[0]) * cap + rank
    slot_ref[...] = found
    target_ref[...] = as_column(found)


def route(ids_row, me, owners, owned, cap):
    rows = ids_row.shape[1]
    return pl.pallas_call(
        functools.partial(route_kernel, owners, owned, cap),
        in_specs=[
            pl.BlockSpec(memory_space=pltpu.SMEM),
            pl.BlockSpec(memory_space=pltpu.VMEM),
        ],
        out_shape=[jax.ShapeDtypeStruct((1, rows), I32), jax.ShapeDtypeStruct((rows, 1), I32)],
        compiler_params=PARAMS,
        cost_estimate=COST,
        name="route",
    )(me, ids_row)


def sort_kernel(cap, pieces, waits, slot_ref, tok_ref, *refs):
    outs, place = refs[waits:-1], refs[-1]

    @pl.when(pl.program_id(0) == 0)
    def _():
        begin = 0
        for block, first, count in pieces:
            at = block * cap + first + lax.broadcasted_iota(I32, (count, slot_ref.shape[1]), 0)
            found = jnp.where(at == slot_ref[...], 1.0, 0.0).astype(BF16)
            place[begin : begin + count, :] = found
            begin += count

    moved = jnp.dot(place[...], tok_ref[...], preferred_element_type=F32).astype(BF16)
    begin = 0
    for (_, _, count), out in zip(pieces, outs):
        out[...] = moved[begin : begin + count, :]
        begin += count


def sort_rows(tokens, slot, cap, pieces, later_than=()):
    rows, width = tokens.shape
    step = min(512, width)
    return pl.pallas_call(
        functools.partial(sort_kernel, cap, pieces, len(later_than)),
        grid=(width // step,),
        in_specs=[
            pl.BlockSpec((1, rows), lambda i: (0, 0)),
            pl.BlockSpec((rows, step), lambda i: (0, i)),
        ]
        + [ANYWHERE] * len(later_than),
        out_specs=[pl.BlockSpec((count, step), lambda i: (0, i)) for _, _, count in pieces],
        out_shape=[jax.ShapeDtypeStruct((count, width), BF16) for _, _, count in pieces],
        scratch_shapes=[pltpu.VMEM((sum(c for _, _, c in pieces), rows), BF16)],
        compiler_params=PARAMS,
        cost_estimate=COST,
        name="sort",
    )(slot, tokens, *later_than)


def name_kernel(owners, owned, sets, here_ref, *refs):
    lines, outs, (ends_ref, plan_ref, most_ref) = refs[:owners], refs[owners:-3], refs[-3:]
    me, half = here_ref[0], here_ref[1]
    held = -(-owned // 8) * 8
    owner = lax.broadcasted_iota(I32, (-(-owners // 8) * 8, 1), 0)
    adapter = lax.broadcasted_iota(I32, (held, 1), 0)
    diagonal = adapter == lax.broadcasted_iota(I32, (held, 128), 1)
    used = lax.broadcasted_iota(I32, (1, 128), 1) < owned
    most = jnp.zeros(owner.shape, I32)
    ends = []
    for j, line in enumerate(lines):
        ids = line[...]
        chosen = jnp.where(owner_of(ids, owners, owned) == owner, 1, 0)
        count = jnp.sum(chosen, axis=1, keepdims=True)
        far = (me ^ j ^ owner >= 2) & (owner < owners)
        most = jnp.maximum(most, jnp.where(far, count, 0))
        mine = ids - me * owned
        upto = jnp.sum(jnp.where((mine >= 0) & (mine <= adapter), 1, 0), axis=1, keepdims=True)
        across = jnp.sum(jnp.where(diagonal, upto, 0), axis=0, keepdims=True)
        ends.append(jnp.where(used, across, 1 << 20))
        ends_ref[j : j + 1, :] = ends[j]
    most_ref[...] = jnp.broadcast_to(jnp.max(most, axis=0, keepdims=True), most_ref.shape)
    for k, (pieces, out) in enumerate(zip(sets, outs)):
        begin, low, high = 0, owned - 1, 0
        for block, first, count in pieces:
            at = first + lax.broadcasted_iota(I32, (count, 1), 0)
            names = jnp.sum(jnp.where(ends[block] <= at, 1, 0), axis=1, keepdims=True)
            out[begin : begin + count, :] = names
            low = jnp.minimum(low, jnp.min(names))
            high = jnp.maximum(high, jnp.max(jnp.where(names < owned, names, 0)))
            begin += count
        plan_ref[3 * k] = low
        plan_ref[3 * k + 1] = jnp.maximum(low, high)
        plan_ref[3 * k + 2] = half


def name_rows(lines, here, owned, sets):
    totals = [sum(c for _, _, c in pieces) for pieces in sets]
    on_chip, scalars = (pl.BlockSpec(memory_space=m) for m in (pltpu.VMEM, pltpu.SMEM))
    *names, ends, plan, most = pl.pallas_call(
        functools.partial(name_kernel, len(lines), owned, sets),
        in_specs=[scalars] + [on_chip] * len(lines),
        out_specs=[on_chip] * len(sets) + [on_chip, scalars, on_chip],
        out_shape=[jax.ShapeDtypeStruct((t, 1), I32) for t in totals]
        + [
            jax.ShapeDtypeStruct((len(lines), 128), I32),
            jax.ShapeDtypeStruct((3 * len(sets),), I32),
            jax.ShapeDtypeStruct((1, 128), I32),
        ],
        compiler_params=PARAMS,
        cost_estimate=COST,
        name="name_rows",
    )(here, *lines)
    plans = [plan[3 * k : 3 * k + 3] for k in range(len(sets))]
    return names, ends, plans, most


def base_kernel(tok_ref, weight_ref, _, out_ref):
    out_ref[...] = jnp.dot(tok_ref[...], weight_ref[...], preferred_element_type=F32)


def base_product(tokens, weight, later_than):
    (rows, width), columns = tokens.shape, weight.shape[1]
    step = min(256, columns)
    return pl.pallas_call(
        base_kernel,
        grid=(columns // step,),
        in_specs=[
            pl.BlockSpec((rows, width), lambda i: (0, 0)),
            pl.BlockSpec((width, step), lambda i: (0, i)),
            ANYWHERE,
        ],
        out_specs=pl.BlockSpec((rows, step), lambda i: (0, i)),
        out_shape=jax.ShapeDtypeStruct((rows, columns), F32),
        compiler_params=PARAMS,
        cost_estimate=COST,
        name="base",
    )(tokens, weight, later_than)


def shrink_kernel(pieces, group, fine, plan_ref, ends_ref, which_ref, down_ref, *refs):
    blocks, (mine_ref, other_ref, acc) = refs[: len(pieces)], refs[-3:]
    step, rank2 = pl.program_id(0), 2 * ADAPTER_RANK
    low, high, second = plan_ref[0], plan_ref[1], plan_ref[2] == 1
    begin = (low // group + step) * group

    @pl.when(step == 0)
    def _():
        acc[...] = jnp.zeros_like(acc)

    for f in range(0, group, fine):

        @pl.when((begin + f <= high) & (begin + f + fine > low))
        def _(f=f):
            adapter = begin + f
            windows, spans, at = [], [], 0
            for (block, first, size), rows in zip(pieces, blocks):
                span = min(up_to_16(fine * TOKEN_LIMIT + 15), size)
                ahead = ends_ref[block, jnp.maximum(adapter - 1, 0)]
                start = jnp.where(adapter > 0, ahead, 0) - first
                start = jnp.minimum(jnp.maximum(start, 0), size - span) // 16 * 16
                windows.append(rows[pl.ds(pl.multiple_of(start, 16), span), :])
                spans.append((pl.ds(pl.multiple_of(at + start, 16), span), span))
                at += size
            factors = down_ref[f : f + fine].reshape(fine * rank2, down_ref.shape[2])
            product = lax.dot_general(
                jnp.concatenate(windows, axis=0),
                factors,
                (((1,), (1,)), ((), ())),
                preferred_element_type=F32,
            )
            at = 0
            for here, span in spans:
                which = which_ref[here, :] - adapter
                found = acc[here, :]
                for q in range(fine):
                    part = product[at : at + span, q * rank2 : (q + 1) * rank2]
                    found = found + jnp.where(which == q, part, 0.0)
                acc[here, :] = found
                at += span

    @pl.when(step == pl.num_programs(0) - 1)
    def _():
        total = acc.shape[0]
        upper, lower = acc[: total // 2, :], acc[total // 2 :, :]
        keys = jnp.concatenate([upper[:, :ADAPTER_RANK], lower[:, :ADAPTER_RANK]], axis=1)
        values = jnp.concatenate([upper[:, ADAPTER_RANK:], lower[:, ADAPTER_RANK:]], axis=1)
        mine_ref[...] = jnp.where(second, values, keys)
        other_ref[...] = jnp.where(second, keys, values)


def shrink(pieces, blocks, names, ends, plan, down, later_than=()):
    total = sum(b.shape[0] for b in blocks)
    owned, rank2, width = down.shape
    group = next(g for g in (4, 3, 2, 1) if owned % g == 0)
    fine = next(g for g in (2, 3, 1) if group % g == 0)
    line = jax.ShapeDtypeStruct((total // 2, 2 * ADAPTER_RANK), F32)
    return pl.pallas_call(
        functools.partial(shrink_kernel, pieces, group, fine),
        grid_spec=pltpu.PrefetchScalarGridSpec(
            num_scalar_prefetch=1,
            grid=(owned // group,),
            in_specs=[
                pl.BlockSpec(memory_space=pltpu.SMEM),
                pl.BlockSpec((total, 1), lambda i, p: (0, 0)),
                pl.BlockSpec(
                    (group, rank2, width),
                    lambda i, p: (jnp.minimum(p[0] // group + i, p[1] // group), 0, 0),
                ),
            ]
            + [pl.BlockSpec(b.shape, lambda i, p: (0, 0)) for b in blocks]
            + [ANYWHERE] * len(later_than),
            out_specs=[pl.BlockSpec((total // 2, rank2), lambda i, p: (0, 0))] * 2,
            scratch_shapes=[pltpu.VMEM((total, rank2), F32)],
        ),
        out_shape=[line, line],
        compiler_params=PARAMS,
        cost_estimate=COST,
        name="shrink",
    )(plan, ends, names, down, *blocks, *later_than)


def split(x, terms):
    parts = []
    for _ in range(terms - 1):
        parts.append(x.astype(BF16).astype(F32))
        x = x - parts[-1]
    return parts + [x]


def expand_kernel(groups, sizes, heard, which_ref, scale_ref, up_ref, *refs):
    lines, outs = refs[:heard], refs[heard:]
    total = lines[0][...]
    for line in lines[1:]:
        total = total + line[...]
    twice, begin = [], 0
    for count in groups:
        lines = total[begin : begin + count, :]
        for side in (lines[:, :ADAPTER_RANK], lines[:, ADAPTER_RANK:]):
            twice.append(jnp.concatenate([side, side], axis=1))
        begin += count
    twice = jnp.concatenate(twice, axis=0)
    which = which_ref[...]
    parity = jnp.where(lax.broadcasted_iota(I32, (1, 2 * ADAPTER_RANK), 1) >= ADAPTER_RANK, 1, 0)
    pairs = up_ref.shape[0] // (2 * ADAPTER_RANK)
    wanted = [which == 2 * p + parity for p in range(pairs)]
    delta = None
    for term in split(twice, 3):
        spread = jnp.concatenate([jnp.where(w, term, 0.0).astype(BF16) for w in wanted], axis=1)
        product = jnp.dot(spread, up_ref[...], preferred_element_type=F32)
        delta = product if delta is None else delta + product
    adapters = lax.broadcasted_iota(I32, scale_ref.shape, 1)
    gain = jnp.sum(jnp.where(which == adapters, scale_ref[...], 0.0), axis=1, keepdims=True)
    delta = delta * gain
    begin = 0
    for size, out in zip(sizes, outs):
        out[...] = delta[begin : begin + size, :]
        begin += size


def expand(lines, groups, names, scale, up, sizes):
    columns = up.shape[1]
    return pl.pallas_call(
        functools.partial(expand_kernel, groups, sizes, len(lines)),
        out_shape=[jax.ShapeDtypeStruct((s, columns), F32) for s in sizes],
        compiler_params=PARAMS,
        cost_estimate=COST,
        name="expand",
    )(names, scale, up, *lines)


def merge_kernel(begins, parts, target_ref, *refs):
    blocks, out_ref = refs[parts:-1], refs[-1]
    returned = jnp.concatenate([b[...] for b in blocks], axis=0)
    target = target_ref[...]
    place = jnp.concatenate(
        [
            jnp.where(
                target == begin + lax.broadcasted_iota(I32, (1, block.shape[0]), 1), 1.0, 0.0
            ).astype(BF16)
            for begin, block in zip(begins, blocks)
        ],
        axis=1,
    )
    total = refs[0][...]
    for part in refs[1:parts]:
        total = total + part[...]
    for term in split(returned, 3):
        total = total + jnp.dot(place, term.astype(BF16), preferred_element_type=F32)
    out_ref[...] = total.astype(out_ref.dtype)


def merge(parts, target, begins, blocks, kind):
    return pl.pallas_call(
        functools.partial(merge_kernel, tuple(begins), len(parts)),
        out_shape=jax.ShapeDtypeStruct(parts[0].shape, kind),
        compiler_params=PARAMS,
        cost_estimate=COST,
        name="merge",
    )(target, *parts, *blocks)


def swap(x, axes, size, distance):
    return lax.ppermute(x, axes, [(i, i ^ distance) for i in range(size)])


def local(
    tokens,
    key_value_weight,
    adapter_down_weight,
    adapter_up_weight,
    adapter_scale,
    token_adapter_index,
):
    feature_axes = ("tensor", "sub")
    rows = tokens.shape[0]
    owned = adapter_down_weight.shape[0]
    owners = lax.axis_size("dp")
    sharers = lax.axis_size(feature_axes)
    me = lax.axis_index("dp")
    half = (lax.axis_index(feature_axes) >= sharers // 2).astype(I32)
    cap = up_to_16(owned * TOKEN_LIMIT)

    own, near = (0, 0, cap), (1, 0, cap)
    if owners == 4:
        usual = up_to_16(cap * 5 // 6)
        most = up_to_16(usual * 4 // 5)
        far = [[(3, 0, most), (2, 0, most)], [(3, most, usual - most), (2, most, usual - most)]]
        extra = [(3, usual, cap - usual), (2, usual, cap - usual)]
    else:
        usual, far, extra = cap, [[(j, 0, cap) for j in range(2, owners)]], []

    ids_row = token_adapter_index.reshape(1, rows)
    ids_heard = [ids_row] + [swap(ids_row, "dp", owners, j) for j in range(1, owners)]
    slot, target = route(ids_row, me.reshape(1), owners, owned, cap)
    sent = [p for s in far for p in s] + [near]
    packed = dict(zip(sent, sort_rows(tokens, slot, cap, sent, tuple(ids_heard[1:]))))
    received = {p: swap(packed[p], "dp", owners, p[0]) for p in sent}

    sets = [[own], [near], [own, near]] + far + ([extra] if extra else [])
    here = jnp.stack([me.astype(I32), half])
    names, ends, plans, largest = name_rows(ids_heard, here, owned, sets)

    if owned % 2:
        adapter_up_weight = jnp.pad(adapter_up_weight, ((0, 1), (0, 0), (0, 0)))
    up = adapter_up_weight.reshape(-1, adapter_up_weight.shape[2])
    scale = adapter_scale.reshape(1, owned)

    def exchange(mine, other, steps=2):
        if sharers == 4 and steps == 2:
            mine = mine + swap(other, "tensor", 2, 1)
            return [mine, swap(mine, "sub", 2, 1)]
        return [mine] + [
            swap(mine if d < sharers // 2 else other, feature_axes, sharers, d)
            for d in range(1, sharers)
        ]

    def deltas_of(pieces, blocks, names, ends, plan, down, up, scale, later_than, steps=2):
        mine, other = shrink(pieces, blocks, names, ends, plan, down, later_than)
        sizes = tuple(b.shape[0] for b in blocks)
        lines = exchange(mine, other, steps)
        return expand(lines, (mine.shape[0],), names, scale, up, sizes)

    def send_back(pieces, deltas):
        return [swap(d, "dp", owners, p[0]) for p, d in zip(pieces, deltas)]

    def begins(pieces):
        return [b * cap + f for b, f, _ in pieces]

    weights = (adapter_down_weight, up, scale)
    base_part = base_product(tokens, key_value_weight, packed[near])
    base = lax.psum_scatter(base_part, feature_axes, scatter_dimension=1, tiled=True)
    packed |= zip([own] + extra, sort_rows(tokens, slot, cap, [own] + extra, (base_part,)))
    down = adapter_down_weight
    first = shrink([own], [packed[own]], names[0], ends, plans[0], down)
    second = shrink(
        [near], [received[near]], names[1], ends, plans[1], down, tuple(first[:1])
    )
    lines = exchange(*(jnp.concatenate(pair, axis=0) for pair in zip(first, second)), steps=1)
    deltas = expand(lines, (cap // 2, cap // 2), names[2], scale, up, (cap, cap))
    returned = [deltas[0]] + send_back([near], deltas[1:])
    done = [own, near]
    for k, pieces in enumerate(far):
        blocks = [received[p] for p in pieces]
        deltas = deltas_of(
            pieces, blocks, names[3 + k], ends, plans[3 + k], *weights, (deltas[0],), 1 + (pieces is far[-1])
        )
        returned += send_back(pieces, deltas)
        done += pieces

    def finish(base, target, returned, *_):
        return merge([base], target, begins(done), returned, BF16)

    if not extra:
        return finish(base, target, returned)

    def finish_with_extra(base, target, returned, blocks, names, ends, plan, weights):
        blocks = send_back(extra, blocks)
        deltas = deltas_of(extra, blocks, names, ends, plan, *weights, ())
        deltas = send_back(extra, deltas)
        return merge([base], target, begins(done + extra), returned + deltas, BF16)

    for d in range(1, lax.axis_size("parts")):
        largest = jnp.maximum(largest, swap(largest, "parts", lax.axis_size("parts"), d))
    return lax.cond(
        largest[0, 0] > usual,
        finish_with_extra,
        finish,
        base,
        target,
        returned,
        [packed[p] for p in extra],
        names[-1],
        ends,
        plans[-1],
        weights,
    )


def solution(mesh):
    return jax.shard_map(
        local,
        mesh=mesh,
        in_specs=(
            P(("parts", "dp"), ("tensor", "sub")),
            P(("tensor", "sub"), None),
            P("dp", None, ("tensor", "sub")),
            P("dp", None, ("tensor", "sub")),
            P("dp"),
            P(("parts", "dp"), None),
        ),
        out_specs=P(("parts", "dp"), ("tensor", "sub")),
        check_vma=False,
    )
```

```python
import functools

import jax
import jax.numpy as jnp
from jax import lax
from jax.experimental import pallas as pl
from jax.experimental.pallas import tpu as pltpu
from jax.sharding import PartitionSpec as P

ADAPTER_RANK = 64
TOKEN_LIMIT = 12
VMEM_LIMIT = 28 * 1024 * 1024
F32 = jnp.float32
BF16 = jnp.bfloat16
I32 = jnp.int32
ANYWHERE = pl.BlockSpec(memory_space=pl.ANY)
COST = pl.CostEstimate(flops=10**9, transcendentals=0, bytes_accessed=1)
PARAMS = pltpu.CompilerParams(vmem_limit_bytes=VMEM_LIMIT)


def up_to_16(count):
    return -(-count // 16) * 16


def owner_of(ids, owners, owned):
    total = jnp.zeros_like(ids)
    for o in range(1, owners):
        total = total + jnp.where(ids >= o * owned, 1, 0)
    return total


def as_column(line):
    size = line.shape[1]
    here = lax.broadcasted_iota(I32, (size, size), 0) == lax.broadcasted_iota(I32, (size, size), 1)
    return jnp.sum(jnp.where(here, line, 0), axis=1, keepdims=True)


def route_kernel(owners, owned, cap, me_ref, row_ref, slot_ref, target_ref):
    rows = row_ref.shape[1]
    id_row = row_ref[...]
    key_row = id_row * rows + lax.broadcasted_iota(I32, (1, rows), 1)
    key_col = as_column(key_row)
    own_row = owner_of(id_row, owners, owned)
    before = (key_col < key_row) & (key_col >= own_row * (owned * rows))
    rank = jnp.sum(jnp.where(before, 1, 0), axis=0, keepdims=True)
    found = (own_row ^ me_ref[0]) * cap + rank
    slot_ref[...] = found
    target_ref[...] = as_column(found)


def route(ids_row, me, owners, owned, cap):
    rows = ids_row.shape[1]
    return pl.pallas_call(
        functools.partial(route_kernel, owners, owned, cap),
        in_specs=[
            pl.BlockSpec(memory_space=pltpu.SMEM),
            pl.BlockSpec(memory_space=pltpu.VMEM),
        ],
        out_shape=[jax.ShapeDtypeStruct((1, rows), I32), jax.ShapeDtypeStruct((rows, 1), I32)],
        compiler_params=PARAMS,
        cost_estimate=COST,
        name="route",
    )(me, ids_row)


def sort_kernel(cap, pieces, waits, slot_ref, tok_ref, *refs):
    outs, place = refs[waits:-1], refs[-1]

    @pl.when(pl.program_id(0) == 0)
    def _():
        begin = 0
        for block, first, count in pieces:
            at = block * cap + first + lax.broadcasted_iota(I32, (count, slot_ref.shape[1]), 0)
            found = jnp.where(at == slot_ref[...], 1.0, 0.0).astype(BF16)
            place[begin : begin + count, :] = found
            begin += count

    moved = jnp.dot(place[...], tok_ref[...], preferred_element_type=F32).astype(BF16)
    begin = 0
    for (_, _, count), out in zip(pieces, outs):
        out[...] = moved[begin : begin + count, :]
        begin += count


def sort_rows(tokens, slot, cap, pieces, later_than=()):
    rows, width = tokens.shape
    step = min(512, width)
    return pl.pallas_call(
        functools.partial(sort_kernel, cap, pieces, len(later_than)),
        grid=(width // step,),
        in_specs=[
            pl.BlockSpec((1, rows), lambda i: (0, 0)),
            pl.BlockSpec((rows, step), lambda i: (0, i)),
        ]
        + [ANYWHERE] * len(later_than),
        out_specs=[pl.BlockSpec((count, step), lambda i: (0, i)) for _, _, count in pieces],
        out_shape=[jax.ShapeDtypeStruct((count, width), BF16) for _, _, count in pieces],
        scratch_shapes=[pltpu.VMEM((sum(c for _, _, c in pieces), rows), BF16)],
        compiler_params=PARAMS,
        cost_estimate=COST,
        name="sort",
    )(slot, tokens, *later_than)


def name_kernel(owners, owned, sets, here_ref, *refs):
    lines, outs, (ends_ref, plan_ref, most_ref) = refs[:owners], refs[owners:-3], refs[-3:]
    me, half = here_ref[0], here_ref[1]
    held = -(-owned // 8) * 8
    owner = lax.broadcasted_iota(I32, (-(-owners // 8) * 8, 1), 0)
    adapter = lax.broadcasted_iota(I32, (held, 1), 0)
    diagonal = adapter == lax.broadcasted_iota(I32, (held, 128), 1)
    used = lax.broadcasted_iota(I32, (1, 128), 1) < owned
    most = jnp.zeros(owner.shape, I32)
    ends = []
    for j, line in enumerate(lines):
        ids = line[...]
        chosen = jnp.where(owner_of(ids, owners, owned) == owner, 1, 0)
        count = jnp.sum(chosen, axis=1, keepdims=True)
        far = (me ^ j ^ owner >= 1) & (owner < owners)
        most = jnp.maximum(most, jnp.where(far, count, 0))
        mine = ids - me * owned
        upto = jnp.sum(jnp.where((mine >= 0) & (mine <= adapter), 1, 0), axis=1, keepdims=True)
        across = jnp.sum(jnp.where(diagonal, upto, 0), axis=0, keepdims=True)
        ends.append(jnp.where(used, across, 1 << 20))
        ends_ref[j : j + 1, :] = ends[j]
    most_ref[...] = jnp.broadcast_to(jnp.max(most, axis=0, keepdims=True), most_ref.shape)
    for k, (pieces, out) in enumerate(zip(sets, outs)):
        begin, low, high = 0, owned - 1, 0
        for block, first, count in pieces:
            at = first + lax.broadcasted_iota(I32, (count, 1), 0)
            names = jnp.sum(jnp.where(ends[block] <= at, 1, 0), axis=1, keepdims=True)
            out[begin : begin + count, :] = names
            low = jnp.minimum(low, jnp.min(names))
            high = jnp.maximum(high, jnp.max(jnp.where(names < owned, names, 0)))
            begin += count
        plan_ref[3 * k] = low
        plan_ref[3 * k + 1] = jnp.maximum(low, high)
        plan_ref[3 * k + 2] = half


def name_rows(lines, here, owned, sets):
    totals = [sum(c for _, _, c in pieces) for pieces in sets]
    on_chip, scalars = (pl.BlockSpec(memory_space=m) for m in (pltpu.VMEM, pltpu.SMEM))
    *names, ends, plan, most = pl.pallas_call(
        functools.partial(name_kernel, len(lines), owned, sets),
        in_specs=[scalars] + [on_chip] * len(lines),
        out_specs=[on_chip] * len(sets) + [on_chip, scalars, on_chip],
        out_shape=[jax.ShapeDtypeStruct((t, 1), I32) for t in totals]
        + [
            jax.ShapeDtypeStruct((len(lines), 128), I32),
            jax.ShapeDtypeStruct((3 * len(sets),), I32),
            jax.ShapeDtypeStruct((1, 128), I32),
        ],
        compiler_params=PARAMS,
        cost_estimate=COST,
        name="name_rows",
    )(here, *lines)
    plans = [plan[3 * k : 3 * k + 3] for k in range(len(sets))]
    return names, ends, plans, most


def base_kernel(tok_ref, weight_ref, _, out_ref):
    out_ref[...] = jnp.dot(tok_ref[...], weight_ref[...], preferred_element_type=F32)


def base_product(tokens, weight, later_than):
    (rows, width), columns = tokens.shape, weight.shape[1]
    step = min(256, columns)
    return pl.pallas_call(
        base_kernel,
        grid=(columns // step,),
        in_specs=[
            pl.BlockSpec((rows, width), lambda i: (0, 0)),
            pl.BlockSpec((width, step), lambda i: (0, i)),
            ANYWHERE,
        ],
        out_specs=pl.BlockSpec((rows, step), lambda i: (0, i)),
        out_shape=jax.ShapeDtypeStruct((rows, columns), F32),
        compiler_params=PARAMS,
        cost_estimate=COST,
        name="base",
    )(tokens, weight, later_than)


def shrink_kernel(pieces, group, fine, plan_ref, ends_ref, which_ref, down_ref, *refs):
    blocks, (mine_ref, other_ref, acc) = refs[: len(pieces)], refs[-3:]
    step, rank2 = pl.program_id(0), 2 * ADAPTER_RANK
    low, high, second = plan_ref[0], plan_ref[1], plan_ref[2] == 1
    begin = (low // group + step) * group

    @pl.when(step == 0)
    def _():
        acc[...] = jnp.zeros_like(acc)

    for f in range(0, group, fine):

        @pl.when((begin + f <= high) & (begin + f + fine > low))
        def _(f=f):
            adapter = begin + f
            windows, spans, at = [], [], 0
            for (block, first, size), rows in zip(pieces, blocks):
                span = min(up_to_16(fine * TOKEN_LIMIT + 15), size)
                ahead = ends_ref[block, jnp.maximum(adapter - 1, 0)]
                start = jnp.where(adapter > 0, ahead, 0) - first
                start = jnp.minimum(jnp.maximum(start, 0), size - span) // 16 * 16
                windows.append(rows[pl.ds(pl.multiple_of(start, 16), span), :])
                spans.append((pl.ds(pl.multiple_of(at + start, 16), span), span))
                at += size
            factors = down_ref[f : f + fine].reshape(fine * rank2, down_ref.shape[2])
            product = lax.dot_general(
                jnp.concatenate(windows, axis=0),
                factors,
                (((1,), (1,)), ((), ())),
                preferred_element_type=F32,
            )
            at = 0
            for here, span in spans:
                which = which_ref[here, :] - adapter
                found = acc[here, :]
                for q in range(fine):
                    part = product[at : at + span, q * rank2 : (q + 1) * rank2]
                    found = found + jnp.where(which == q, part, 0.0)
                acc[here, :] = found
                at += span

    @pl.when(step == pl.num_programs(0) - 1)
    def _():
        total = acc.shape[0]
        upper, lower = acc[: total // 2, :], acc[total // 2 :, :]
        keys = jnp.concatenate([upper[:, :ADAPTER_RANK], lower[:, :ADAPTER_RANK]], axis=1)
        values = jnp.concatenate([upper[:, ADAPTER_RANK:], lower[:, ADAPTER_RANK:]], axis=1)
        mine_ref[...] = jnp.where(second, values, keys)
        other_ref[...] = jnp.where(second, keys, values)


def shrink(pieces, blocks, names, ends, plan, down, later_than=()):
    total = sum(b.shape[0] for b in blocks)
    owned, rank2, width = down.shape
    group = next(g for g in (4, 3, 2, 1) if owned % g == 0)
    fine = next(g for g in (2, 3, 1) if group % g == 0)
    line = jax.ShapeDtypeStruct((total // 2, 2 * ADAPTER_RANK), F32)
    return pl.pallas_call(
        functools.partial(shrink_kernel, pieces, group, fine),
        grid_spec=pltpu.PrefetchScalarGridSpec(
            num_scalar_prefetch=1,
            grid=(owned // group,),
            in_specs=[
                pl.BlockSpec(memory_space=pltpu.SMEM),
                pl.BlockSpec((total, 1), lambda i, p: (0, 0)),
                pl.BlockSpec(
                    (group, rank2, width),
                    lambda i, p: (jnp.minimum(p[0] // group + i, p[1] // group), 0, 0),
                ),
            ]
            + [pl.BlockSpec(b.shape, lambda i, p: (0, 0)) for b in blocks]
            + [ANYWHERE] * len(later_than),
            out_specs=[pl.BlockSpec((total // 2, rank2), lambda i, p: (0, 0))] * 2,
            scratch_shapes=[pltpu.VMEM((total, rank2), F32)],
        ),
        out_shape=[line, line],
        compiler_params=PARAMS,
        cost_estimate=COST,
        name="shrink",
    )(plan, ends, names, down, *blocks, *later_than)


def split(x, terms):
    parts = []
    for _ in range(terms - 1):
        parts.append(x.astype(BF16).astype(F32))
        x = x - parts[-1]
    return parts + [x]


def expand_kernel(groups, sizes, heard, which_ref, scale_ref, up_ref, *refs):
    lines, outs = refs[:heard], refs[heard:]
    total = lines[0][...]
    for line in lines[1:]:
        total = total + line[...]
    twice, begin = [], 0
    for count in groups:
        lines = total[begin : begin + count, :]
        for side in (lines[:, :ADAPTER_RANK], lines[:, ADAPTER_RANK:]):
            twice.append(jnp.concatenate([side, side], axis=1))
        begin += count
    twice = jnp.concatenate(twice, axis=0)
    which = which_ref[...]
    parity = jnp.where(lax.broadcasted_iota(I32, (1, 2 * ADAPTER_RANK), 1) >= ADAPTER_RANK, 1, 0)
    pairs = up_ref.shape[0] // (2 * ADAPTER_RANK)
    wanted = [which == 2 * p + parity for p in range(pairs)]
    delta = None
    for term in split(twice, 3):
        spread = jnp.concatenate([jnp.where(w, term, 0.0).astype(BF16) for w in wanted], axis=1)
        product = jnp.dot(spread, up_ref[...], preferred_element_type=F32)
        delta = product if delta is None else delta + product
    adapters = lax.broadcasted_iota(I32, scale_ref.shape, 1)
    gain = jnp.sum(jnp.where(which == adapters, scale_ref[...], 0.0), axis=1, keepdims=True)
    delta = delta * gain
    begin = 0
    for size, out in zip(sizes, outs):
        piece = delta[begin : begin + size, :]
        if out.dtype == F32:
            out[...] = piece
        else:
            code_rows(piece, out)
        begin += size


def code_rows(x, out_ref):
    rows, columns = x.shape
    largest = jnp.maximum(jnp.max(jnp.abs(x), axis=1, keepdims=True), 2.0**-105)
    power = jnp.floor(jnp.log2(largest)) - 14.0
    power = power + jnp.where(largest * power_of_two(-power) > 32767.0, 1.0, 0.0)
    coded = jnp.round(x * power_of_two(-power))
    coded = jnp.minimum(jnp.maximum(coded, -32767.0), 32767.0)
    out_ref[:rows, :] = coded.astype(I32).astype(jnp.int16)
    down = lax.broadcasted_iota(I32, (rows, columns), 0)
    across = lax.broadcasted_iota(I32, (rows, columns), 1)
    line = jnp.sum(jnp.where(down == across, power, 0.0), axis=0, keepdims=True)
    line = jnp.broadcast_to(line, (16, columns)).astype(I32)
    out_ref[rows:, :] = line.astype(jnp.int16)


def power_of_two(power):
    return jnp.exp2(power).astype(BF16).astype(F32)


def expand(lines, groups, names, scale, up, sizes, kept=0):
    columns = up.shape[1]
    shapes = [
        jax.ShapeDtypeStruct((s, columns), F32)
        if i < kept
        else jax.ShapeDtypeStruct((s + 16, columns), jnp.int16)
        for i, s in enumerate(sizes)
    ]
    return pl.pallas_call(
        functools.partial(expand_kernel, groups, sizes, len(lines)),
        out_shape=shapes,
        compiler_params=PARAMS,
        cost_estimate=COST,
        name="expand",
    )(names, scale, up, *lines)


def place_kernel(begin, target_ref, rows_ref, out_ref):
    at = begin + lax.broadcasted_iota(I32, (1, rows_ref.shape[0]), 1)
    place = jnp.where(target_ref[...] == at, 1.0, 0.0).astype(BF16)
    total = None
    for term in split(rows_ref[...], 3):
        moved = jnp.dot(place, term.astype(BF16), preferred_element_type=F32)
        total = moved if total is None else total + moved
    out_ref[...] = total


def place_rows(target, begin, rows):
    return pl.pallas_call(
        functools.partial(place_kernel, begin),
        out_shape=jax.ShapeDtypeStruct((target.shape[0], rows.shape[1]), F32),
        compiler_params=PARAMS,
        cost_estimate=COST,
        name="place",
    )(target, rows)


def merge_kernel(begins, parts, target_ref, *refs):
    blocks, out_ref = refs[parts:-1], refs[-1]
    spots, powers, highs, lows = [], [], [], []
    for begin, block in zip(begins, blocks):
        count = block.shape[0] - 16
        spots.append(begin + lax.broadcasted_iota(I32, (1, count), 1))
        powers.append(block[count:, :].astype(I32)[:1, :count])
        coded = block[:count, :].astype(I32)
        high = (coded + 128) >> 8
        highs.append(high.astype(F32).astype(BF16))
        lows.append((coded - high * 256).astype(F32).astype(BF16))
    spot, power = jnp.concatenate(spots, axis=1), jnp.concatenate(powers, axis=1)
    place = jnp.where(target_ref[...] == spot, jnp.exp2(power.astype(F32)), 0.0).astype(BF16)
    total = jnp.dot(place, jnp.concatenate(highs, axis=0), preferred_element_type=F32) * 256.0
    total = total + jnp.dot(place, jnp.concatenate(lows, axis=0), preferred_element_type=F32)
    for part in refs[:parts]:
        total = total + part[...]
    out_ref[...] = total.astype(out_ref.dtype)


def merge(parts, target, begins, blocks, kind):
    return pl.pallas_call(
        functools.partial(merge_kernel, tuple(begins), len(parts)),
        out_shape=jax.ShapeDtypeStruct(parts[0].shape, kind),
        compiler_params=PARAMS,
        cost_estimate=COST,
        name="merge",
    )(target, *parts, *blocks)


def swap(x, axes, size, distance):
    return lax.ppermute(x, axes, [(i, i ^ distance) for i in range(size)])


def local(
    tokens,
    key_value_weight,
    adapter_down_weight,
    adapter_up_weight,
    adapter_scale,
    token_adapter_index,
):
    feature_axes = ("tensor", "sub")
    rows = tokens.shape[0]
    owned = adapter_down_weight.shape[0]
    owners = lax.axis_size("dp")
    sharers = lax.axis_size(feature_axes)
    me = lax.axis_index("dp")
    half = (lax.axis_index(feature_axes) >= sharers // 2).astype(I32)
    cap = up_to_16(owned * TOKEN_LIMIT)

    own, near = (0, 0, cap), (1, 0, cap)
    if owners == 4:
        usual = up_to_16(cap * 5 // 6)
        near = (1, 0, usual)
        most = up_to_16(usual * 4 // 5)
        far = [[(3, 0, most), (2, 0, most)], [(3, most, usual - most), (2, most, usual - most)]]
        extra = [(j, usual, cap - usual) for j in (3, 2, 1)]
    else:
        usual, far, extra = cap, [[(j, 0, cap) for j in range(2, owners)]], []

    ids_row = token_adapter_index.reshape(1, rows)
    ids_heard = [ids_row] + [swap(ids_row, "dp", owners, j) for j in range(1, owners)]
    slot, target = route(ids_row, me.reshape(1), owners, owned, cap)
    sent = [p for s in far for p in s] + [near]
    packed = dict(zip(sent, sort_rows(tokens, slot, cap, sent, tuple(ids_heard[1:]))))
    base_part = base_product(tokens, key_value_weight, packed[near])
    base = lax.psum_scatter(base_part, feature_axes, scatter_dimension=1, tiled=True)
    received = {p: swap(packed[p], "dp", owners, p[0]) for p in sent}

    sets = [[own], [near], [own, near]] + far + ([extra] if extra else [])
    here = jnp.stack([me.astype(I32), half])
    names, ends, plans, largest = name_rows(ids_heard, here, owned, sets)

    if owned % 2:
        adapter_up_weight = jnp.pad(adapter_up_weight, ((0, 1), (0, 0), (0, 0)))
    up = adapter_up_weight.reshape(-1, adapter_up_weight.shape[2])
    scale = adapter_scale.reshape(1, owned)

    def exchange(mine, other, steps=2):
        if sharers == 4 and steps == 2:
            mine = mine + swap(other, "tensor", 2, 1)
            return [mine, swap(mine, "sub", 2, 1)]
        return [mine] + [
            swap(mine if d < sharers // 2 else other, feature_axes, sharers, d)
            for d in range(1, sharers)
        ]

    def deltas_of(pieces, blocks, names, ends, plan, down, up, scale, later_than, steps=2):
        mine, other = shrink(pieces, blocks, names, ends, plan, down, later_than)
        sizes = tuple(b.shape[0] for b in blocks)
        lines = exchange(mine, other, steps)
        return expand(lines, (mine.shape[0],), names, scale, up, sizes)

    def send_back(pieces, deltas):
        return [swap(d, "dp", owners, p[0]) for p, d in zip(pieces, deltas)]

    def begins(pieces):
        return [b * cap + f for b, f, _ in pieces]

    weights = (adapter_down_weight, up, scale)
    packed |= zip([own] + extra, sort_rows(tokens, slot, cap, [own] + extra, (base_part,)))
    down = adapter_down_weight
    first = shrink([own], [packed[own]], names[0], ends, plans[0], down)
    second = shrink(
        [near], [received[near]], names[1], ends, plans[1], down, tuple(first[:1])
    )
    lines = exchange(*(jnp.concatenate(pair, axis=0) for pair in zip(first, second)), steps=1)
    sizes = (own[2], near[2])
    deltas = expand(lines, tuple(c // 2 for c in sizes), names[2], scale, up, sizes, kept=1)
    parts = [base, place_rows(target, own[0] * cap, deltas[0])]
    returned = send_back([near], deltas[1:])
    done = [near]
    for k, pieces in enumerate(far):
        blocks = [received[p] for p in pieces]
        deltas = deltas_of(
            pieces, blocks, names[3 + k], ends, plans[3 + k], *weights, (deltas[0], parts[1]), 1 + (pieces is far[-1])
        )
        returned += send_back(pieces, deltas)
        done += pieces

    def finish(parts, target, returned, *_):
        return merge(parts, target, begins(done), returned, BF16)

    if not extra:
        return finish(parts, target, returned)

    def finish_with_extra(parts, target, returned, blocks, names, ends, plan, weights):
        blocks = send_back(extra, blocks)
        deltas = deltas_of(extra, blocks, names, ends, plan, *weights, ())
        deltas = send_back(extra, deltas)
        return merge(parts, target, begins(done + extra), returned + deltas, BF16)

    for d in range(1, lax.axis_size("parts")):
        largest = jnp.maximum(largest, swap(largest, "parts", lax.axis_size("parts"), d))
    return lax.cond(
        largest[0, 0] > usual,
        finish_with_extra,
        finish,
        parts,
        target,
        returned,
        [packed[p] for p in extra],
        names[-1],
        ends,
        plans[-1],
        weights,
    )


def solution(mesh):
    return jax.shard_map(
        local,
        mesh=mesh,
        in_specs=(
            P(("parts", "dp"), ("tensor", "sub")),
            P(("tensor", "sub"), None),
            P("dp", None, ("tensor", "sub")),
            P("dp", None, ("tensor", "sub")),
            P("dp"),
            P(("parts", "dp"), None),
        ),
        out_specs=P(("parts", "dp"), ("tensor", "sub")),
        check_vma=False,
    )
```

```python
import functools

import jax
import jax.numpy as jnp
from jax import lax
from jax.experimental import pallas as pl
from jax.experimental.pallas import tpu as pltpu
from jax.sharding import PartitionSpec as P

ADAPTER_RANK = 64
TOKEN_LIMIT = 12
VMEM_LIMIT = 28 * 1024 * 1024
F32 = jnp.float32
BF16 = jnp.bfloat16
I32 = jnp.int32
ANYWHERE = pl.BlockSpec(memory_space=pl.ANY)
COST = pl.CostEstimate(flops=10**9, transcendentals=0, bytes_accessed=1)
PARAMS = pltpu.CompilerParams(vmem_limit_bytes=VMEM_LIMIT)


def up_to_16(count):
    return -(-count // 16) * 16


def owner_of(ids, owners, owned):
    total = jnp.zeros_like(ids)
    for o in range(1, owners):
        total = total + jnp.where(ids >= o * owned, 1, 0)
    return total


def as_column(line):
    size = line.shape[1]
    here = lax.broadcasted_iota(I32, (size, size), 0) == lax.broadcasted_iota(I32, (size, size), 1)
    return jnp.sum(jnp.where(here, line, 0), axis=1, keepdims=True)


def route_kernel(owners, owned, cap, me_ref, row_ref, slot_ref, target_ref):
    rows = row_ref.shape[1]
    id_row = row_ref[...]
    key_row = id_row * rows + lax.broadcasted_iota(I32, (1, rows), 1)
    key_col = as_column(key_row)
    own_row = owner_of(id_row, owners, owned)
    before = (key_col < key_row) & (key_col >= own_row * (owned * rows))
    rank = jnp.sum(jnp.where(before, 1, 0), axis=0, keepdims=True)
    found = (own_row ^ me_ref[0]) * cap + rank
    slot_ref[...] = found
    target_ref[...] = as_column(found)


def route(ids_row, me, owners, owned, cap):
    rows = ids_row.shape[1]
    return pl.pallas_call(
        functools.partial(route_kernel, owners, owned, cap),
        in_specs=[
            pl.BlockSpec(memory_space=pltpu.SMEM),
            pl.BlockSpec(memory_space=pltpu.VMEM),
        ],
        out_shape=[jax.ShapeDtypeStruct((1, rows), I32), jax.ShapeDtypeStruct((rows, 1), I32)],
        compiler_params=PARAMS,
        cost_estimate=COST,
        name="route",
    )(me, ids_row)


def sort_kernel(cap, pieces, waits, slot_ref, tok_ref, *refs):
    outs, place = refs[waits:-1], refs[-1]

    @pl.when(pl.program_id(0) == 0)
    def _():
        begin = 0
        for block, first, count in pieces:
            at = block * cap + first + lax.broadcasted_iota(I32, (count, slot_ref.shape[1]), 0)
            found = jnp.where(at == slot_ref[...], 1.0, 0.0).astype(BF16)
            place[begin : begin + count, :] = found
            begin += count

    moved = jnp.dot(place[...], tok_ref[...], preferred_element_type=F32).astype(BF16)
    begin = 0
    for (_, _, count), out in zip(pieces, outs):
        out[...] = moved[begin : begin + count, :]
        begin += count


def sort_rows(tokens, slot, cap, pieces, later_than=()):
    rows, width = tokens.shape
    step = min(512, width)
    return pl.pallas_call(
        functools.partial(sort_kernel, cap, pieces, len(later_than)),
        grid=(width // step,),
        in_specs=[
            pl.BlockSpec((1, rows), lambda i: (0, 0)),
            pl.BlockSpec((rows, step), lambda i: (0, i)),
        ]
        + [ANYWHERE] * len(later_than),
        out_specs=[pl.BlockSpec((count, step), lambda i: (0, i)) for _, _, count in pieces],
        out_shape=[jax.ShapeDtypeStruct((count, width), BF16) for _, _, count in pieces],
        scratch_shapes=[pltpu.VMEM((sum(c for _, _, c in pieces), rows), BF16)],
        compiler_params=PARAMS,
        cost_estimate=COST,
        name="sort",
    )(slot, tokens, *later_than)


def name_kernel(owners, owned, sets, here_ref, *refs):
    lines, outs, (ends_ref, plan_ref, most_ref) = refs[:owners], refs[owners:-3], refs[-3:]
    me, half = here_ref[0], here_ref[1]
    held = -(-owned // 8) * 8
    owner = lax.broadcasted_iota(I32, (-(-owners // 8) * 8, 1), 0)
    adapter = lax.broadcasted_iota(I32, (held, 1), 0)
    diagonal = adapter == lax.broadcasted_iota(I32, (held, 128), 1)
    used = lax.broadcasted_iota(I32, (1, 128), 1) < owned
    most = jnp.zeros(owner.shape, I32)
    ends = []
    for j, line in enumerate(lines):
        ids = line[...]
        chosen = jnp.where(owner_of(ids, owners, owned) == owner, 1, 0)
        count = jnp.sum(chosen, axis=1, keepdims=True)
        far = (me ^ j ^ owner >= 1) & (owner < owners)
        most = jnp.maximum(most, jnp.where(far, count, 0))
        mine = ids - me * owned
        upto = jnp.sum(jnp.where((mine >= 0) & (mine <= adapter), 1, 0), axis=1, keepdims=True)
        across = jnp.sum(jnp.where(diagonal, upto, 0), axis=0, keepdims=True)
        ends.append(jnp.where(used, across, 1 << 20))
        ends_ref[j : j + 1, :] = ends[j]
    most_ref[...] = jnp.broadcast_to(jnp.max(most, axis=0, keepdims=True), most_ref.shape)
    for k, (pieces, out) in enumerate(zip(sets, outs)):
        begin, low, high = 0, owned - 1, 0
        for block, first, count in pieces:
            at = first + lax.broadcasted_iota(I32, (count, 1), 0)
            names = jnp.sum(jnp.where(ends[block] <= at, 1, 0), axis=1, keepdims=True)
            out[begin : begin + count, :] = names
            low = jnp.minimum(low, jnp.min(names))
            high = jnp.maximum(high, jnp.max(jnp.where(names < owned, names, 0)))
            begin += count
        plan_ref[3 * k] = low
        plan_ref[3 * k + 1] = jnp.maximum(low, high)
        plan_ref[3 * k + 2] = half


def name_rows(lines, here, owned, sets):
    totals = [sum(c for _, _, c in pieces) for pieces in sets]
    on_chip, scalars = (pl.BlockSpec(memory_space=m) for m in (pltpu.VMEM, pltpu.SMEM))
    *names, ends, plan, most = pl.pallas_call(
        functools.partial(name_kernel, len(lines), owned, sets),
        in_specs=[scalars] + [on_chip] * len(lines),
        out_specs=[on_chip] * len(sets) + [on_chip, scalars, on_chip],
        out_shape=[jax.ShapeDtypeStruct((t, 1), I32) for t in totals]
        + [
            jax.ShapeDtypeStruct((len(lines), 128), I32),
            jax.ShapeDtypeStruct((3 * len(sets),), I32),
            jax.ShapeDtypeStruct((1, 128), I32),
        ],
        compiler_params=PARAMS,
        cost_estimate=COST,
        name="name_rows",
    )(here, *lines)
    plans = [plan[3 * k : 3 * k + 3] for k in range(len(sets))]
    return names, ends, plans, most


def base_kernel(tok_ref, weight_ref, _, out_ref):
    out_ref[...] = jnp.dot(tok_ref[...], weight_ref[...], preferred_element_type=F32)


def base_product(tokens, weight, later_than):
    (rows, width), columns = tokens.shape, weight.shape[1]
    step = min(256, columns)
    return pl.pallas_call(
        base_kernel,
        grid=(columns // step,),
        in_specs=[
            pl.BlockSpec((rows, width), lambda i: (0, 0)),
            pl.BlockSpec((width, step), lambda i: (0, i)),
            ANYWHERE,
        ],
        out_specs=pl.BlockSpec((rows, step), lambda i: (0, i)),
        out_shape=jax.ShapeDtypeStruct((rows, columns), F32),
        compiler_params=PARAMS,
        cost_estimate=COST,
        name="base",
    )(tokens, weight, later_than)


def shrink_kernel(pieces, group, fine, plan_ref, ends_ref, which_ref, down_ref, *refs):
    blocks, (mine_ref, other_ref, acc) = refs[: len(pieces)], refs[-3:]
    step, rank2 = pl.program_id(0), 2 * ADAPTER_RANK
    low, high, second = plan_ref[0], plan_ref[1], plan_ref[2] == 1
    begin = (low // group + step) * group

    @pl.when(step == 0)
    def _():
        acc[...] = jnp.zeros_like(acc)

    for f in range(0, group, fine):

        @pl.when((begin + f <= high) & (begin + f + fine > low))
        def _(f=f):
            adapter = begin + f
            windows, spans, at = [], [], 0
            for (block, first, size), rows in zip(pieces, blocks):
                span = min(up_to_16(fine * TOKEN_LIMIT + 15), size)
                ahead = ends_ref[block, jnp.maximum(adapter - 1, 0)]
                start = jnp.where(adapter > 0, ahead, 0) - first
                start = jnp.minimum(jnp.maximum(start, 0), size - span) // 16 * 16
                windows.append(rows[pl.ds(pl.multiple_of(start, 16), span), :])
                spans.append((pl.ds(pl.multiple_of(at + start, 16), span), span))
                at += size
            factors = down_ref[f : f + fine].reshape(fine * rank2, down_ref.shape[2])
            product = lax.dot_general(
                jnp.concatenate(windows, axis=0),
                factors,
                (((1,), (1,)), ((), ())),
                preferred_element_type=F32,
            )
            at = 0
            for here, span in spans:
                which = which_ref[here, :] - adapter
                found = acc[here, :]
                for q in range(fine):
                    part = product[at : at + span, q * rank2 : (q + 1) * rank2]
                    found = found + jnp.where(which == q, part, 0.0)
                acc[here, :] = found
                at += span

    @pl.when(step == pl.num_programs(0) - 1)
    def _():
        total = acc.shape[0]
        upper, lower = acc[: total // 2, :], acc[total // 2 :, :]
        keys = jnp.concatenate([upper[:, :ADAPTER_RANK], lower[:, :ADAPTER_RANK]], axis=1)
        values = jnp.concatenate([upper[:, ADAPTER_RANK:], lower[:, ADAPTER_RANK:]], axis=1)
        mine_ref[...] = jnp.where(second, values, keys)
        other_ref[...] = jnp.where(second, keys, values)


def shrink(pieces, blocks, names, ends, plan, down, later_than=()):
    total = sum(b.shape[0] for b in blocks)
    owned, rank2, width = down.shape
    group = next(g for g in (4, 3, 2, 1) if owned % g == 0)
    fine = next(g for g in (2, 3, 1) if group % g == 0)
    line = jax.ShapeDtypeStruct((total // 2, 2 * ADAPTER_RANK), F32)
    return pl.pallas_call(
        functools.partial(shrink_kernel, pieces, group, fine),
        grid_spec=pltpu.PrefetchScalarGridSpec(
            num_scalar_prefetch=1,
            grid=(owned // group,),
            in_specs=[
                pl.BlockSpec(memory_space=pltpu.SMEM),
                pl.BlockSpec((total, 1), lambda i, p: (0, 0)),
                pl.BlockSpec(
                    (group, rank2, width),
                    lambda i, p: (jnp.minimum(p[0] // group + i, p[1] // group), 0, 0),
                ),
            ]
            + [pl.BlockSpec(b.shape, lambda i, p: (0, 0)) for b in blocks]
            + [ANYWHERE] * len(later_than),
            out_specs=[pl.BlockSpec((total // 2, rank2), lambda i, p: (0, 0))] * 2,
            scratch_shapes=[pltpu.VMEM((total, rank2), F32)],
        ),
        out_shape=[line, line],
        compiler_params=PARAMS,
        cost_estimate=COST,
        name="shrink",
    )(plan, ends, names, down, *blocks, *later_than)


def split(x, terms):
    parts = []
    for _ in range(terms - 1):
        parts.append(x.astype(BF16).astype(F32))
        x = x - parts[-1]
    return parts + [x]


def expand_kernel(groups, sizes, heard, which_ref, scale_ref, up_ref, *refs):
    lines, outs = refs[:heard], refs[heard:]
    total = lines[0][...]
    for line in lines[1:]:
        total = total + line[...]
    twice, begin = [], 0
    for count in groups:
        lines = total[begin : begin + count, :]
        for side in (lines[:, :ADAPTER_RANK], lines[:, ADAPTER_RANK:]):
            twice.append(jnp.concatenate([side, side], axis=1))
        begin += count
    twice = jnp.concatenate(twice, axis=0)
    which = which_ref[...]
    parity = jnp.where(lax.broadcasted_iota(I32, (1, 2 * ADAPTER_RANK), 1) >= ADAPTER_RANK, 1, 0)
    pairs = up_ref.shape[0] // (2 * ADAPTER_RANK)
    wanted = [which == 2 * p + parity for p in range(pairs)]
    delta = None
    for term in split(twice, 3):
        spread = jnp.concatenate([jnp.where(w, term, 0.0).astype(BF16) for w in wanted], axis=1)
        product = jnp.dot(spread, up_ref[...], preferred_element_type=F32)
        delta = product if delta is None else delta + product
    adapters = lax.broadcasted_iota(I32, scale_ref.shape, 1)
    gain = jnp.sum(jnp.where(which == adapters, scale_ref[...], 0.0), axis=1, keepdims=True)
    delta = delta * gain
    begin = 0
    for size, out in zip(sizes, outs):
        piece = delta[begin : begin + size, :]
        if out.dtype == F32:
            out[...] = piece
        else:
            code_rows(piece, out)
        begin += size


def code_rows(x, out_ref):
    rows, columns = x.shape
    largest = jnp.maximum(jnp.max(jnp.abs(x), axis=1, keepdims=True), 2.0**-105)
    power = jnp.floor(jnp.log2(largest)) - 14.0
    power = power + jnp.where(largest * power_of_two(-power) > 32767.0, 1.0, 0.0)
    coded = jnp.round(x * power_of_two(-power))
    coded = jnp.minimum(jnp.maximum(coded, -32767.0), 32767.0)
    out_ref[:rows, :] = coded.astype(I32).astype(jnp.int16)
    down = lax.broadcasted_iota(I32, (rows, columns), 0)
    across = lax.broadcasted_iota(I32, (rows, columns), 1)
    line = jnp.sum(jnp.where(down == across, power, 0.0), axis=0, keepdims=True)
    line = jnp.broadcast_to(line, (16, columns)).astype(I32)
    out_ref[rows:, :] = line.astype(jnp.int16)


def power_of_two(power):
    return jnp.exp2(power).astype(BF16).astype(F32)


def expand(lines, groups, names, scale, up, sizes, kept=0):
    columns = up.shape[1]
    shapes = [
        jax.ShapeDtypeStruct((s, columns), F32)
        if i < kept
        else jax.ShapeDtypeStruct((s + 16, columns), jnp.int16)
        for i, s in enumerate(sizes)
    ]
    return pl.pallas_call(
        functools.partial(expand_kernel, groups, sizes, len(lines)),
        out_shape=shapes,
        compiler_params=PARAMS,
        cost_estimate=COST,
        name="expand",
    )(names, scale, up, *lines)


def place_kernel(begin, target_ref, rows_ref, out_ref):
    at = begin + lax.broadcasted_iota(I32, (1, rows_ref.shape[0]), 1)
    place = jnp.where(target_ref[...] == at, 1.0, 0.0).astype(BF16)
    total = None
    for term in split(rows_ref[...], 3):
        moved = jnp.dot(place, term.astype(BF16), preferred_element_type=F32)
        total = moved if total is None else total + moved
    out_ref[...] = total


def place_rows(target, begin, rows):
    return pl.pallas_call(
        functools.partial(place_kernel, begin),
        out_shape=jax.ShapeDtypeStruct((target.shape[0], rows.shape[1]), F32),
        compiler_params=PARAMS,
        cost_estimate=COST,
        name="place",
    )(target, rows)


def merge_kernel(begins, parts, target_ref, *refs):
    blocks, out_ref = refs[parts:-1], refs[-1]
    spots, powers, highs, lows = [], [], [], []
    for begin, block in zip(begins, blocks):
        count = block.shape[0] - 16
        spots.append(begin + lax.broadcasted_iota(I32, (1, count), 1))
        powers.append(block[count:, :].astype(I32)[:1, :count])
        coded = block[:count, :].astype(I32)
        high = (coded + 128) >> 8
        highs.append(high.astype(F32).astype(BF16))
        lows.append((coded - high * 256).astype(F32).astype(BF16))
    spot, power = jnp.concatenate(spots, axis=1), jnp.concatenate(powers, axis=1)
    place = jnp.where(target_ref[...] == spot, jnp.exp2(power.astype(F32)), 0.0).astype(BF16)
    total = jnp.dot(place, jnp.concatenate(highs, axis=0), preferred_element_type=F32) * 256.0
    total = total + jnp.dot(place, jnp.concatenate(lows, axis=0), preferred_element_type=F32)
    for part in refs[:parts]:
        total = total + part[...]
    out_ref[...] = total.astype(out_ref.dtype)


def merge(parts, target, begins, blocks, kind):
    return pl.pallas_call(
        functools.partial(merge_kernel, tuple(begins), len(parts)),
        out_shape=jax.ShapeDtypeStruct(parts[0].shape, kind),
        compiler_params=PARAMS,
        cost_estimate=COST,
        name="merge",
    )(target, *parts, *blocks)


def swap(x, axes, size, distance):
    return lax.ppermute(x, axes, [(i, i ^ distance) for i in range(size)])


def local(
    tokens,
    key_value_weight,
    adapter_down_weight,
    adapter_up_weight,
    adapter_scale,
    token_adapter_index,
):
    feature_axes = ("tensor", "sub")
    rows = tokens.shape[0]
    owned = adapter_down_weight.shape[0]
    owners = lax.axis_size("dp")
    sharers = lax.axis_size(feature_axes)
    me = lax.axis_index("dp")
    half = (lax.axis_index(feature_axes) >= sharers // 2).astype(I32)
    cap = up_to_16(owned * TOKEN_LIMIT)

    own, near = (0, 0, cap), (1, 0, cap)
    if owners == 4:
        usual = up_to_16(cap * 5 // 6)
        near = (1, 0, usual)
        far, last = [(3, 0, usual)], [(2, 0, usual)]
        extra = [(j, usual, cap - usual) for j in (3, 2, 1)]
    else:
        usual, far, last, extra = cap, [], [(j, 0, cap) for j in range(2, owners)], []

    ids_row = token_adapter_index.reshape(1, rows)
    ids_heard = [ids_row] + [swap(ids_row, "dp", owners, j) for j in range(1, owners)]
    slot, target = route(ids_row, me.reshape(1), owners, owned, cap)
    sent = far + [near]
    packed = dict(zip(sent, sort_rows(tokens, slot, cap, sent, tuple(ids_heard[1:]))))
    received = {p: swap(packed[p], "dp", owners, p[0]) for p in sent}
    base_part = base_product(tokens, key_value_weight, packed[near])
    base = lax.psum_scatter(base_part, feature_axes, scatter_dimension=1, tiled=True)
    packed |= zip([own] + extra, sort_rows(tokens, slot, cap, [own] + extra, (base_part,)))
    packed |= zip(last, sort_rows(tokens, slot, cap, last, (received[near],)))
    received |= {p: swap(packed[p], "dp", owners, p[0]) for p in last}

    early = [own, near] + far
    sets = [[p] for p in early] + [early, last] + ([extra] if extra else [])
    here = jnp.stack([me.astype(I32), half])
    names, ends, plans, largest = name_rows(ids_heard, here, owned, sets)

    if owned % 2:
        adapter_up_weight = jnp.pad(adapter_up_weight, ((0, 1), (0, 0), (0, 0)))
    up = adapter_up_weight.reshape(-1, adapter_up_weight.shape[2])
    scale = adapter_scale.reshape(1, owned)

    def exchange(mine, other, steps=2):
        if sharers == 4 and steps == 2:
            mine = mine + swap(other, "tensor", 2, 1)
            return [mine, swap(mine, "sub", 2, 1)]
        return [mine] + [
            swap(mine if d < sharers // 2 else other, feature_axes, sharers, d)
            for d in range(1, sharers)
        ]

    def deltas_of(pieces, blocks, names, ends, plan, down, up, scale, later_than, steps=2):
        mine, other = shrink(pieces, blocks, names, ends, plan, down, later_than)
        sizes = tuple(b.shape[0] for b in blocks)
        lines = exchange(mine, other, steps)
        return expand(lines, (mine.shape[0],), names, scale, up, sizes)

    def send_back(pieces, deltas):
        return [swap(d, "dp", owners, p[0]) for p, d in zip(pieces, deltas)]

    def begins(pieces):
        return [b * cap + f for b, f, _ in pieces]

    weights = (adapter_down_weight, up, scale)
    packed |= zip([own] + extra, sort_rows(tokens, slot, cap, [own] + extra, (base_part,)))
    shares, waits = [], ()
    for k, p in enumerate(early):
        rows_here = received.get(p, packed[p])
        shares.append(
            shrink([p], [rows_here], names[k], ends, plans[k], adapter_down_weight, waits)
        )
        waits = (shares[-1][0], packed[last[0]])
    lines = exchange(*(jnp.concatenate(pair, axis=0) for pair in zip(*shares)), steps=1)
    sizes = tuple(p[2] for p in early)
    here = len(early)
    deltas = expand(lines, tuple(c // 2 for c in sizes), names[here], scale, up, sizes, kept=1)
    parts = [base, place_rows(target, own[0] * cap, deltas[0])]
    returned = send_back(early[1:], deltas[1:])
    blocks = [received[p] for p in last]
    deltas = deltas_of(
        last, blocks, names[here + 1], ends, plans[here + 1], *weights, (deltas[0], parts[1])
    )
    returned += send_back(last, deltas)
    done = early[1:] + last

    def finish(parts, target, returned, *_):
        return merge(parts, target, begins(done), returned, BF16)

    if not extra:
        return finish(parts, target, returned)

    def finish_with_extra(parts, target, returned, blocks, names, ends, plan, weights):
        blocks = send_back(extra, blocks)
        deltas = deltas_of(extra, blocks, names, ends, plan, *weights, ())
        deltas = send_back(extra, deltas)
        return merge(parts, target, begins(done + extra), returned + deltas, BF16)

    for d in range(1, lax.axis_size("parts")):
        largest = jnp.maximum(largest, swap(largest, "parts", lax.axis_size("parts"), d))
    return lax.cond(
        largest[0, 0] > usual,
        finish_with_extra,
        finish,
        parts,
        target,
        returned,
        [packed[p] for p in extra],
        names[-1],
        ends,
        plans[-1],
        weights,
    )


def solution(mesh):
    return jax.shard_map(
        local,
        mesh=mesh,
        in_specs=(
            P(("parts", "dp"), ("tensor", "sub")),
            P(("tensor", "sub"), None),
            P("dp", None, ("tensor", "sub")),
            P("dp", None, ("tensor", "sub")),
            P("dp"),
            P(("parts", "dp"), None),
        ),
        out_specs=P(("parts", "dp"), ("tensor", "sub")),
        check_vma=False,
    )
```

```python
import functools

import jax
import jax.numpy as jnp
from jax import lax
from jax.experimental import pallas as pl
from jax.experimental.pallas import tpu as pltpu
from jax.sharding import PartitionSpec as P

ADAPTER_RANK = 64
TOKEN_LIMIT = 12
VMEM_LIMIT = 28 * 1024 * 1024
F32 = jnp.float32
BF16 = jnp.bfloat16
I32 = jnp.int32
ANYWHERE = pl.BlockSpec(memory_space=pl.ANY)
COST = pl.CostEstimate(flops=1, transcendentals=0, bytes_accessed=1)
PARAMS = pltpu.CompilerParams(vmem_limit_bytes=VMEM_LIMIT)


def up_to_16(count):
    return -(-count // 16) * 16


def owner_of(ids, owners, owned):
    total = jnp.zeros_like(ids)
    for o in range(1, owners):
        total = total + jnp.where(ids >= o * owned, 1, 0)
    return total


def as_column(line):
    size = line.shape[1]
    here = lax.broadcasted_iota(I32, (size, size), 0) == lax.broadcasted_iota(I32, (size, size), 1)
    return jnp.sum(jnp.where(here, line, 0), axis=1, keepdims=True)


def route_kernel(owners, owned, cap, me_ref, row_ref, slot_ref, target_ref):
    rows = row_ref.shape[1]
    id_row = row_ref[...]
    key_row = id_row * rows + lax.broadcasted_iota(I32, (1, rows), 1)
    key_col = as_column(key_row)
    own_row = owner_of(id_row, owners, owned)
    before = (key_col < key_row) & (key_col >= own_row * (owned * rows))
    rank = jnp.sum(jnp.where(before, 1, 0), axis=0, keepdims=True)
    found = (own_row ^ me_ref[0]) * cap + rank
    slot_ref[...] = found
    target_ref[...] = as_column(found)


def route(ids_row, me, owners, owned, cap):
    rows = ids_row.shape[1]
    return pl.pallas_call(
        functools.partial(route_kernel, owners, owned, cap),
        in_specs=[
            pl.BlockSpec(memory_space=pltpu.SMEM),
            pl.BlockSpec(memory_space=pltpu.VMEM),
        ],
        out_shape=[jax.ShapeDtypeStruct((1, rows), I32), jax.ShapeDtypeStruct((rows, 1), I32)],
        compiler_params=PARAMS,
        cost_estimate=COST,
        name="route",
    )(me, ids_row)


def sort_kernel(cap, pieces, waits, slot_ref, tok_ref, *refs):
    outs, place = refs[waits:-1], refs[-1]

    @pl.when(pl.program_id(0) == 0)
    def _():
        begin = 0
        for block, first, count in pieces:
            at = block * cap + first + lax.broadcasted_iota(I32, (count, slot_ref.shape[1]), 0)
            found = jnp.where(at == slot_ref[...], 1.0, 0.0).astype(BF16)
            place[begin : begin + count, :] = found
            begin += count

    moved = jnp.dot(place[...], tok_ref[...], preferred_element_type=F32).astype(BF16)
    begin = 0
    for (_, _, count), out in zip(pieces, outs):
        out[...] = moved[begin : begin + count, :]
        begin += count


def sort_rows(tokens, slot, cap, pieces, later_than=()):
    rows, width = tokens.shape
    step = min(512, width)
    return pl.pallas_call(
        functools.partial(sort_kernel, cap, pieces, len(later_than)),
        grid=(width // step,),
        in_specs=[
            pl.BlockSpec((1, rows), lambda i: (0, 0)),
            pl.BlockSpec((rows, step), lambda i: (0, i)),
        ]
        + [ANYWHERE] * len(later_than),
        out_specs=[pl.BlockSpec((count, step), lambda i: (0, i)) for _, _, count in pieces],
        out_shape=[jax.ShapeDtypeStruct((count, width), BF16) for _, _, count in pieces],
        scratch_shapes=[pltpu.VMEM((sum(c for _, _, c in pieces), rows), BF16)],
        compiler_params=PARAMS,
        cost_estimate=COST,
        name="sort",
    )(slot, tokens, *later_than)


def name_kernel(owners, owned, sets, here_ref, *refs):
    lines, outs, (ends_ref, plan_ref, most_ref) = refs[:owners], refs[owners:-3], refs[-3:]
    me, half = here_ref[0], here_ref[1]
    held = -(-owned // 8) * 8
    owner = lax.broadcasted_iota(I32, (-(-owners // 8) * 8, 1), 0)
    adapter = lax.broadcasted_iota(I32, (held, 1), 0)
    diagonal = adapter == lax.broadcasted_iota(I32, (held, 128), 1)
    used = lax.broadcasted_iota(I32, (1, 128), 1) < owned
    most = jnp.zeros(owner.shape, I32)
    ends = []
    for j, line in enumerate(lines):
        ids = line[...]
        chosen = jnp.where(owner_of(ids, owners, owned) == owner, 1, 0)
        count = jnp.sum(chosen, axis=1, keepdims=True)
        far = (me ^ j ^ owner >= 1) & (owner < owners)
        most = jnp.maximum(most, jnp.where(far, count, 0))
        mine = ids - me * owned
        upto = jnp.sum(jnp.where((mine >= 0) & (mine <= adapter), 1, 0), axis=1, keepdims=True)
        across = jnp.sum(jnp.where(diagonal, upto, 0), axis=0, keepdims=True)
        ends.append(jnp.where(used, across, 1 << 20))
        ends_ref[j : j + 1, :] = ends[j]
    most_ref[...] = jnp.broadcast_to(jnp.max(most, axis=0, keepdims=True), most_ref.shape)
    for k, (pieces, out) in enumerate(zip(sets, outs)):
        begin, low, high = 0, owned - 1, 0
        for block, first, count in pieces:
            at = first + lax.broadcasted_iota(I32, (count, 1), 0)
            names = jnp.sum(jnp.where(ends[block] <= at, 1, 0), axis=1, keepdims=True)
            out[begin : begin + count, :] = names
            low = jnp.minimum(low, jnp.min(names))
            high = jnp.maximum(high, jnp.max(jnp.where(names < owned, names, 0)))
            begin += count
        plan_ref[3 * k] = low
        plan_ref[3 * k + 1] = jnp.maximum(low, high)
        plan_ref[3 * k + 2] = half


def name_rows(lines, here, owned, sets):
    totals = [sum(c for _, _, c in pieces) for pieces in sets]
    on_chip, scalars = (pl.BlockSpec(memory_space=m) for m in (pltpu.VMEM, pltpu.SMEM))
    *names, ends, plan, most = pl.pallas_call(
        functools.partial(name_kernel, len(lines), owned, sets),
        in_specs=[scalars] + [on_chip] * len(lines),
        out_specs=[on_chip] * len(sets) + [on_chip, scalars, on_chip],
        out_shape=[jax.ShapeDtypeStruct((t, 1), I32) for t in totals]
        + [
            jax.ShapeDtypeStruct((len(lines), 128), I32),
            jax.ShapeDtypeStruct((3 * len(sets),), I32),
            jax.ShapeDtypeStruct((1, 128), I32),
        ],
        compiler_params=PARAMS,
        cost_estimate=COST,
        name="name_rows",
    )(here, *lines)
    plans = [plan[3 * k : 3 * k + 3] for k in range(len(sets))]
    return names, ends, plans, most


def base_kernel(tok_ref, weight_ref, _, out_ref):
    out_ref[...] = jnp.dot(tok_ref[...], weight_ref[...], preferred_element_type=F32)


def base_product(tokens, weight, later_than):
    (rows, width), columns = tokens.shape, weight.shape[1]
    step = min(256, columns)
    return pl.pallas_call(
        base_kernel,
        grid=(columns // step,),
        in_specs=[
            pl.BlockSpec((rows, width), lambda i: (0, 0)),
            pl.BlockSpec((width, step), lambda i: (0, i)),
            ANYWHERE,
        ],
        out_specs=pl.BlockSpec((rows, step), lambda i: (0, i)),
        out_shape=pltpu.HBM((rows, columns), F32),
        compiler_params=PARAMS,
        cost_estimate=COST,
        name="base",
    )(tokens, weight, later_than)


def shrink_kernel(pieces, group, fine, plan_ref, ends_ref, which_ref, down_ref, *refs):
    blocks, (mine_ref, other_ref, acc) = refs[: len(pieces)], refs[-3:]
    step, rank2 = pl.program_id(0), 2 * ADAPTER_RANK
    low, high, second = plan_ref[0], plan_ref[1], plan_ref[2] == 1
    begin = (low // group + step) * group

    @pl.when(step == 0)
    def _():
        acc[...] = jnp.zeros_like(acc)

    for f in range(0, group, fine):

        @pl.when((begin + f <= high) & (begin + f + fine > low))
        def _(f=f):
            adapter = begin + f
            windows, spans, at = [], [], 0
            for (block, first, size), rows in zip(pieces, blocks):
                span = min(up_to_16(fine * TOKEN_LIMIT + 15), size)
                ahead = ends_ref[block, jnp.maximum(adapter - 1, 0)]
                start = jnp.where(adapter > 0, ahead, 0) - first
                start = jnp.minimum(jnp.maximum(start, 0), size - span) // 16 * 16
                windows.append(rows[pl.ds(pl.multiple_of(start, 16), span), :])
                spans.append((pl.ds(pl.multiple_of(at + start, 16), span), span))
                at += size
            factors = down_ref[f : f + fine].reshape(fine * rank2, down_ref.shape[2])
            product = lax.dot_general(
                jnp.concatenate(windows, axis=0),
                factors,
                (((1,), (1,)), ((), ())),
                preferred_element_type=F32,
            )
            at = 0
            for here, span in spans:
                which = which_ref[here, :] - adapter
                found = acc[here, :]
                for q in range(fine):
                    part = product[at : at + span, q * rank2 : (q + 1) * rank2]
                    found = found + jnp.where(which == q, part, 0.0)
                acc[here, :] = found
                at += span

    @pl.when(step == pl.num_programs(0) - 1)
    def _():
        total = acc.shape[0]
        upper, lower = acc[: total // 2, :], acc[total // 2 :, :]
        keys = jnp.concatenate([upper[:, :ADAPTER_RANK], lower[:, :ADAPTER_RANK]], axis=1)
        values = jnp.concatenate([upper[:, ADAPTER_RANK:], lower[:, ADAPTER_RANK:]], axis=1)
        mine_ref[...] = jnp.where(second, values, keys)
        other_ref[...] = jnp.where(second, keys, values)


def shrink(pieces, blocks, names, ends, plan, down, later_than=()):
    total = sum(b.shape[0] for b in blocks)
    owned, rank2, width = down.shape
    group = next(g for g in (4, 3, 2, 1) if owned % g == 0)
    fine = next(g for g in (2, 3, 1) if group % g == 0)
    line = jax.ShapeDtypeStruct((total // 2, 2 * ADAPTER_RANK), F32)
    return pl.pallas_call(
        functools.partial(shrink_kernel, pieces, group, fine),
        grid_spec=pltpu.PrefetchScalarGridSpec(
            num_scalar_prefetch=1,
            grid=(owned // group,),
            in_specs=[
                pl.BlockSpec(memory_space=pltpu.SMEM),
                pl.BlockSpec((total, 1), lambda i, p: (0, 0)),
                pl.BlockSpec(
                    (group, rank2, width),
                    lambda i, p: (jnp.minimum(p[0] // group + i, p[1] // group), 0, 0),
                ),
            ]
            + [pl.BlockSpec(b.shape, lambda i, p: (0, 0)) for b in blocks]
            + [ANYWHERE] * len(later_than),
            out_specs=[pl.BlockSpec((total // 2, rank2), lambda i, p: (0, 0))] * 2,
            scratch_shapes=[pltpu.VMEM((total, rank2), F32)],
        ),
        out_shape=[line, line],
        compiler_params=PARAMS,
        cost_estimate=COST,
        name="shrink",
    )(plan, ends, names, down, *blocks, *later_than)


def split(x, terms):
    parts = []
    for _ in range(terms - 1):
        parts.append(x.astype(BF16).astype(F32))
        x = x - parts[-1]
    return parts + [x]


def expand_kernel(groups, sizes, heard, waits, which_ref, scale_ref, up_ref, *refs):
    lines, outs = refs[:heard], refs[heard + waits :]
    total = lines[0][...]
    for line in lines[1:]:
        total = total + line[...]
    twice, begin = [], 0
    for count in groups:
        lines = total[begin : begin + count, :]
        for side in (lines[:, :ADAPTER_RANK], lines[:, ADAPTER_RANK:]):
            twice.append(jnp.concatenate([side, side], axis=1))
        begin += count
    twice = jnp.concatenate(twice, axis=0)
    which = which_ref[...]
    parity = jnp.where(lax.broadcasted_iota(I32, (1, 2 * ADAPTER_RANK), 1) >= ADAPTER_RANK, 1, 0)
    pairs = up_ref.shape[0] // (2 * ADAPTER_RANK)
    wanted = [which == 2 * p + parity for p in range(pairs)]
    delta = None
    for term in split(twice, 3):
        spread = jnp.concatenate([jnp.where(w, term, 0.0).astype(BF16) for w in wanted], axis=1)
        product = jnp.dot(spread, up_ref[...], preferred_element_type=F32)
        delta = product if delta is None else delta + product
    adapters = lax.broadcasted_iota(I32, scale_ref.shape, 1)
    gain = jnp.sum(jnp.where(which == adapters, scale_ref[...], 0.0), axis=1, keepdims=True)
    delta = delta * gain
    begin = 0
    for size, out in zip(sizes, outs):
        piece = delta[begin : begin + size, :]
        if out.dtype == F32:
            out[...] = piece
        else:
            code_rows(piece, out)
        begin += size


def code_rows(x, out_ref):
    rows, columns = x.shape
    largest = jnp.maximum(jnp.max(jnp.abs(x), axis=1, keepdims=True), 2.0**-105)
    power = jnp.floor(jnp.log2(largest)) - 14.0
    power = power + jnp.where(largest * power_of_two(-power) > 32767.0, 1.0, 0.0)
    coded = jnp.round(x * power_of_two(-power))
    coded = jnp.minimum(jnp.maximum(coded, -32767.0), 32767.0)
    out_ref[:rows, :] = coded.astype(I32).astype(jnp.int16)
    down = lax.broadcasted_iota(I32, (rows, columns), 0)
    across = lax.broadcasted_iota(I32, (rows, columns), 1)
    line = jnp.sum(jnp.where(down == across, power, 0.0), axis=0, keepdims=True)
    line = jnp.broadcast_to(line, (16, columns)).astype(I32)
    out_ref[rows:, :] = line.astype(jnp.int16)


def power_of_two(power):
    return jnp.exp2(power).astype(BF16).astype(F32)


def expand(lines, groups, names, scale, up, sizes, kept=0, later_than=()):
    columns = up.shape[1]
    shapes = [
        jax.ShapeDtypeStruct((s, columns), F32)
        if i < kept
        else jax.ShapeDtypeStruct((s + 16, columns), jnp.int16)
        for i, s in enumerate(sizes)
    ]
    return pl.pallas_call(
        functools.partial(expand_kernel, groups, sizes, len(lines), len(later_than)),
        in_specs=[pl.BlockSpec(memory_space=pltpu.VMEM)] * (3 + len(lines))
        + [ANYWHERE] * len(later_than),
        out_shape=shapes,
        compiler_params=PARAMS,
        cost_estimate=COST,
        name="expand",
    )(names, scale, up, *lines, *later_than)


def place_kernel(begin, target_ref, rows_ref, out_ref):
    at = begin + lax.broadcasted_iota(I32, (1, rows_ref.shape[0]), 1)
    place = jnp.where(target_ref[...] == at, 1.0, 0.0).astype(BF16)
    total = None
    for term in split(rows_ref[...], 3):
        moved = jnp.dot(place, term.astype(BF16), preferred_element_type=F32)
        total = moved if total is None else total + moved
    out_ref[...] = total


def place_rows(target, begin, rows):
    return pl.pallas_call(
        functools.partial(place_kernel, begin),
        out_shape=jax.ShapeDtypeStruct((target.shape[0], rows.shape[1]), F32),
        compiler_params=PARAMS,
        cost_estimate=COST,
        name="place",
    )(target, rows)


def merge_kernel(begins, parts, target_ref, *refs):
    blocks, out_ref = refs[parts:-1], refs[-1]
    spots, powers, highs, lows = [], [], [], []
    for begin, block in zip(begins, blocks):
        count = block.shape[0] - 16
        spots.append(begin + lax.broadcasted_iota(I32, (1, count), 1))
        powers.append(block[count:, :].astype(I32)[:1, :count])
        coded = block[:count, :].astype(I32)
        high = (coded + 128) >> 8
        highs.append(high.astype(F32).astype(BF16))
        lows.append((coded - high * 256).astype(F32).astype(BF16))
    spot, power = jnp.concatenate(spots, axis=1), jnp.concatenate(powers, axis=1)
    place = jnp.where(target_ref[...] == spot, jnp.exp2(power.astype(F32)), 0.0).astype(BF16)
    total = jnp.dot(place, jnp.concatenate(highs, axis=0), preferred_element_type=F32) * 256.0
    total = total + jnp.dot(place, jnp.concatenate(lows, axis=0), preferred_element_type=F32)
    for part in refs[:parts]:
        total = total + part[...]
    out_ref[...] = total.astype(out_ref.dtype)


def merge(parts, target, begins, blocks, kind):
    return pl.pallas_call(
        functools.partial(merge_kernel, tuple(begins), len(parts)),
        out_shape=jax.ShapeDtypeStruct(parts[0].shape, kind),
        compiler_params=PARAMS,
        cost_estimate=COST,
        name="merge",
    )(target, *parts, *blocks)


def swap(x, axes, size, distance):
    return lax.ppermute(x, axes, [(i, i ^ distance) for i in range(size)])


def local(
    tokens,
    key_value_weight,
    adapter_down_weight,
    adapter_up_weight,
    adapter_scale,
    token_adapter_index,
):
    feature_axes = ("tensor", "sub")
    rows = tokens.shape[0]
    owned = adapter_down_weight.shape[0]
    owners = lax.axis_size("dp")
    sharers = lax.axis_size(feature_axes)
    me = lax.axis_index("dp")
    half = (lax.axis_index(feature_axes) >= sharers // 2).astype(I32)
    cap = up_to_16(owned * TOKEN_LIMIT)

    own, near = (0, 0, cap), (1, 0, cap)
    if owners == 4:
        usual = up_to_16(cap * 5 // 6)
        near = (1, 0, usual)
        first = up_to_16(usual * 3 // 5)
        far, last = [(3, 0, usual)], [[(2, 0, first)], [(2, first, usual - first)]]
        extra = [(j, usual, cap - usual) for j in (3, 2, 1)]
    else:
        usual, far, last, extra = cap, [], [[(j, 0, cap) for j in range(2, owners)]], []

    ids_row = token_adapter_index.reshape(1, rows)
    ids_heard = [ids_row] + [swap(ids_row, "dp", owners, j) for j in range(1, owners)]
    slot, target = route(ids_row, me.reshape(1), owners, owned, cap)
    sent = far + [near]
    packed = dict(zip(sent, sort_rows(tokens, slot, cap, sent, tuple(ids_heard[1:]))))
    received = {p: swap(packed[p], "dp", owners, p[0]) for p in sent}
    base_part = base_product(tokens, key_value_weight, packed[near])
    base = lax.psum_scatter(base_part, feature_axes, scatter_dimension=1, tiled=True)
    packed |= zip([own] + extra, sort_rows(tokens, slot, cap, [own] + extra, (base_part,)))
    gated = [p for pieces in last for p in pieces]
    packed |= zip(gated, sort_rows(tokens, slot, cap, gated, (received[near],)))
    received |= {p: swap(packed[p], "dp", owners, p[0]) for p in gated}

    early = [own, near] + far
    sets = [[p] for p in early] + [early] + last + ([extra] if extra else [])
    here = jnp.stack([me.astype(I32), half])
    names, ends, plans, largest = name_rows(ids_heard, here, owned, sets)

    if owned % 2:
        adapter_up_weight = jnp.pad(adapter_up_weight, ((0, 1), (0, 0), (0, 0)))
    up = adapter_up_weight.reshape(-1, adapter_up_weight.shape[2])
    scale = adapter_scale.reshape(1, owned)

    def exchange(mine, other, steps=2):
        if sharers == 4 and steps == 2:
            mine = mine + swap(other, "tensor", 2, 1)
            return [mine, swap(mine, "sub", 2, 1)]
        return [mine] + [
            swap(mine if d < sharers // 2 else other, feature_axes, sharers, d)
            for d in range(1, sharers)
        ]

    def deltas_of(pieces, blocks, names, ends, plan, down, up, scale, later_than):
        mine, other = shrink(pieces, blocks, names, ends, plan, down, later_than)
        sizes = tuple(b.shape[0] for b in blocks)
        lines = exchange(mine, other)
        return expand(lines, (mine.shape[0],), names, scale, up, sizes)

    def send_back(pieces, deltas):
        return [swap(d, "dp", owners, p[0]) for p, d in zip(pieces, deltas)]

    def begins(pieces):
        return [b * cap + f for b, f, _ in pieces]

    weights = (adapter_down_weight, up, scale)
    packed |= zip([own] + extra, sort_rows(tokens, slot, cap, [own] + extra, (base_part,)))
    shares, waits = [], ()
    for k, p in enumerate(early):
        rows_here = received.get(p, packed[p])
        shares.append(
            shrink([p], [rows_here], names[k], ends, plans[k], adapter_down_weight, waits)
        )
        waits = (shares[-1][0], packed[gated[0]])
    lines = exchange(*(jnp.concatenate(pair, axis=0) for pair in zip(*shares)), steps=1)
    sizes = tuple(p[2] for p in early)
    here = len(early)
    deltas = expand(lines, tuple(c // 2 for c in sizes), names[here], scale, up, sizes, kept=1)
    parts = [base, place_rows(target, own[0] * cap, deltas[0])]
    returned = send_back(early[1:], deltas[1:])
    done = early[1:]
    for k, pieces in enumerate(last):
        blocks = [received[p] for p in pieces]
        waits = (deltas[0], parts[1])
        deltas = deltas_of(
            pieces, blocks, names[here + 1 + k], ends, plans[here + 1 + k], *weights, waits
        )
        returned += send_back(pieces, deltas)
        done += pieces

    def finish(parts, target, returned, *_):
        return merge(parts, target, begins(done), returned, BF16)

    if not extra:
        return finish(parts, target, returned)

    def finish_with_extra(parts, target, returned, blocks, names, ends, plan, weights):
        blocks = send_back(extra, blocks)
        deltas = deltas_of(extra, blocks, names, ends, plan, *weights, ())
        deltas = send_back(extra, deltas)
        return merge(parts, target, begins(done + extra), returned + deltas, BF16)

    for d in range(1, lax.axis_size("parts")):
        largest = jnp.maximum(largest, swap(largest, "parts", lax.axis_size("parts"), d))
    return lax.cond(
        largest[0, 0] > usual,
        finish_with_extra,
        finish,
        parts,
        target,
        returned,
        [packed[p] for p in extra],
        names[-1],
        ends,
        plans[-1],
        weights,
    )


def solution(mesh):
    return jax.shard_map(
        local,
        mesh=mesh,
        in_specs=(
            P(("parts", "dp"), ("tensor", "sub")),
            P(("tensor", "sub"), None),
            P("dp", None, ("tensor", "sub")),
            P("dp", None, ("tensor", "sub")),
            P("dp"),
            P(("parts", "dp"), None),
        ),
        out_specs=P(("parts", "dp"), ("tensor", "sub")),
        check_vma=False,
    )
```

```python
import functools

import jax
import jax.numpy as jnp
from jax import lax
from jax.experimental import pallas as pl
from jax.experimental.pallas import tpu as pltpu
from jax.sharding import PartitionSpec as P

ADAPTER_RANK = 64
TOKEN_LIMIT = 12
VMEM_LIMIT = 16 * 1024 * 1024
F32 = jnp.float32
BF16 = jnp.bfloat16
I32 = jnp.int32
ANYWHERE = pl.BlockSpec(memory_space=pl.ANY)
COST = pl.CostEstimate(flops=1, transcendentals=0, bytes_accessed=1)
PARAMS = pltpu.CompilerParams(vmem_limit_bytes=VMEM_LIMIT)


def up_to_16(count):
    return -(-count // 16) * 16


def owner_of(ids, owners, owned):
    total = jnp.zeros_like(ids)
    for o in range(1, owners):
        total = total + jnp.where(ids >= o * owned, 1, 0)
    return total


def as_column(line):
    size = line.shape[1]
    here = lax.broadcasted_iota(I32, (size, size), 0) == lax.broadcasted_iota(I32, (size, size), 1)
    return jnp.sum(jnp.where(here, line, 0), axis=1, keepdims=True)


def route_kernel(owners, owned, cap, me_ref, row_ref, slot_ref, target_ref):
    rows = row_ref.shape[1]
    id_row = row_ref[...]
    key_row = id_row * rows + lax.broadcasted_iota(I32, (1, rows), 1)
    key_col = as_column(key_row)
    own_row = owner_of(id_row, owners, owned)
    before = (key_col < key_row) & (key_col >= own_row * (owned * rows))
    rank = jnp.sum(jnp.where(before, 1, 0), axis=0, keepdims=True)
    found = (own_row ^ me_ref[0]) * cap + rank
    slot_ref[...] = found
    target_ref[...] = as_column(found)


def route(ids_row, me, owners, owned, cap):
    rows = ids_row.shape[1]
    return pl.pallas_call(
        functools.partial(route_kernel, owners, owned, cap),
        in_specs=[
            pl.BlockSpec(memory_space=pltpu.SMEM),
            pl.BlockSpec(memory_space=pltpu.VMEM),
        ],
        out_shape=[jax.ShapeDtypeStruct((1, rows), I32), jax.ShapeDtypeStruct((rows, 1), I32)],
        compiler_params=PARAMS,
        cost_estimate=COST,
        name="route",
    )(me, ids_row)


def sort_kernel(cap, pieces, waits, slot_ref, tok_ref, *refs):
    outs, place = refs[waits:-1], refs[-1]

    @pl.when(pl.program_id(0) == 0)
    def _():
        begin = 0
        for block, first, count in pieces:
            at = block * cap + first + lax.broadcasted_iota(I32, (count, slot_ref.shape[1]), 0)
            found = jnp.where(at == slot_ref[...], 1.0, 0.0).astype(BF16)
            place[begin : begin + count, :] = found
            begin += count

    moved = jnp.dot(place[...], tok_ref[...], preferred_element_type=F32).astype(BF16)
    begin = 0
    for (_, _, count), out in zip(pieces, outs):
        out[...] = moved[begin : begin + count, :]
        begin += count


def sort_rows(tokens, slot, cap, pieces, later_than=()):
    rows, width = tokens.shape
    step = min(512, width)
    return pl.pallas_call(
        functools.partial(sort_kernel, cap, pieces, len(later_than)),
        grid=(width // step,),
        in_specs=[
            pl.BlockSpec((1, rows), lambda i: (0, 0)),
            pl.BlockSpec((rows, step), lambda i: (0, i)),
        ]
        + [ANYWHERE] * len(later_than),
        out_specs=[pl.BlockSpec((count, step), lambda i: (0, i)) for _, _, count in pieces],
        out_shape=[jax.ShapeDtypeStruct((count, width), BF16) for _, _, count in pieces],
        scratch_shapes=[pltpu.VMEM((sum(c for _, _, c in pieces), rows), BF16)],
        compiler_params=PARAMS,
        cost_estimate=COST,
        name="sort",
    )(slot, tokens, *later_than)


def name_kernel(owners, owned, sets, here_ref, *refs):
    lines, outs, (ends_ref, plan_ref, most_ref) = refs[:owners], refs[owners:-3], refs[-3:]
    me, half = here_ref[0], here_ref[1]
    held = -(-owned // 8) * 8
    owner = lax.broadcasted_iota(I32, (-(-owners // 8) * 8, 1), 0)
    adapter = lax.broadcasted_iota(I32, (held, 1), 0)
    diagonal = adapter == lax.broadcasted_iota(I32, (held, 128), 1)
    used = lax.broadcasted_iota(I32, (1, 128), 1) < owned
    most = jnp.zeros(owner.shape, I32)
    ends = []
    for j, line in enumerate(lines):
        ids = line[...]
        chosen = jnp.where(owner_of(ids, owners, owned) == owner, 1, 0)
        count = jnp.sum(chosen, axis=1, keepdims=True)
        far = (me ^ j ^ owner >= 1) & (owner < owners)
        most = jnp.maximum(most, jnp.where(far, count, 0))
        mine = ids - me * owned
        upto = jnp.sum(jnp.where((mine >= 0) & (mine <= adapter), 1, 0), axis=1, keepdims=True)
        across = jnp.sum(jnp.where(diagonal, upto, 0), axis=0, keepdims=True)
        ends.append(jnp.where(used, across, 1 << 20))
        ends_ref[j : j + 1, :] = ends[j]
    most_ref[...] = jnp.broadcast_to(jnp.max(most, axis=0, keepdims=True), most_ref.shape)
    for k, (pieces, out) in enumerate(zip(sets, outs)):
        begin, low, high = 0, owned - 1, 0
        for block, first, count in pieces:
            at = first + lax.broadcasted_iota(I32, (count, 1), 0)
            names = jnp.sum(jnp.where(ends[block] <= at, 1, 0), axis=1, keepdims=True)
            out[begin : begin + count, :] = names
            low = jnp.minimum(low, jnp.min(names))
            high = jnp.maximum(high, jnp.max(jnp.where(names < owned, names, 0)))
            begin += count
        plan_ref[3 * k] = low
        plan_ref[3 * k + 1] = jnp.maximum(low, high)
        plan_ref[3 * k + 2] = half


def name_rows(lines, here, owned, sets):
    totals = [sum(c for _, _, c in pieces) for pieces in sets]
    on_chip, scalars = (pl.BlockSpec(memory_space=m) for m in (pltpu.VMEM, pltpu.SMEM))
    *names, ends, plan, most = pl.pallas_call(
        functools.partial(name_kernel, len(lines), owned, sets),
        in_specs=[scalars] + [on_chip] * len(lines),
        out_specs=[on_chip] * len(sets) + [on_chip, scalars, on_chip],
        out_shape=[jax.ShapeDtypeStruct((t, 1), I32) for t in totals]
        + [
            jax.ShapeDtypeStruct((len(lines), 128), I32),
            jax.ShapeDtypeStruct((3 * len(sets),), I32),
            jax.ShapeDtypeStruct((1, 128), I32),
        ],
        compiler_params=PARAMS,
        cost_estimate=COST,
        name="name_rows",
    )(here, *lines)
    plans = [plan[3 * k : 3 * k + 3] for k in range(len(sets))]
    return names, ends, plans, most


def base_kernel(tok_ref, weight_ref, _, out_ref, done_ref):
    done_ref[...] = jnp.zeros_like(done_ref)
    out_ref[...] = jnp.dot(tok_ref[...], weight_ref[...], preferred_element_type=F32)


def base_product(tokens, weight, later_than):
    (rows, width), columns = tokens.shape, weight.shape[1]
    step = min(256, columns)
    return pl.pallas_call(
        base_kernel,
        grid=(columns // step,),
        in_specs=[
            pl.BlockSpec((rows, width), lambda i: (0, 0)),
            pl.BlockSpec((width, step), lambda i: (0, i)),
            ANYWHERE,
        ],
        out_specs=[
            pl.BlockSpec((rows, step), lambda i: (0, i)),
            pl.BlockSpec((8, 128), lambda i: (0, 0)),
        ],
        out_shape=[
            jax.ShapeDtypeStruct((rows, columns), F32),
            jax.ShapeDtypeStruct((8, 128), F32),
        ],
        compiler_params=PARAMS,
        cost_estimate=COST,
        name="base",
    )(tokens, weight, later_than)


def shrink_kernel(pieces, group, fine, plan_ref, ends_ref, which_ref, down_ref, *refs):
    blocks, (mine_ref, other_ref, acc) = refs[: len(pieces)], refs[-3:]
    step, rank2 = pl.program_id(0), 2 * ADAPTER_RANK
    low, high, second = plan_ref[0], plan_ref[1], plan_ref[2] == 1
    begin = (low // group + step) * group

    @pl.when(step == 0)
    def _():
        acc[...] = jnp.zeros_like(acc)

    for f in range(0, group, fine):

        @pl.when((begin + f <= high) & (begin + f + fine > low))
        def _(f=f):
            adapter = begin + f
            windows, spans, at = [], [], 0
            for (block, first, size), rows in zip(pieces, blocks):
                span = min(up_to_16(fine * TOKEN_LIMIT + 15), size)
                ahead = ends_ref[block, jnp.maximum(adapter - 1, 0)]
                start = jnp.where(adapter > 0, ahead, 0) - first
                start = jnp.minimum(jnp.maximum(start, 0), size - span) // 16 * 16
                windows.append(rows[pl.ds(pl.multiple_of(start, 16), span), :])
                spans.append((pl.ds(pl.multiple_of(at + start, 16), span), span))
                at += size
            factors = down_ref[f : f + fine].reshape(fine * rank2, down_ref.shape[2])
            product = lax.dot_general(
                jnp.concatenate(windows, axis=0),
                factors,
                (((1,), (1,)), ((), ())),
                preferred_element_type=F32,
            )
            at = 0
            for here, span in spans:
                which = which_ref[here, :] - adapter
                found = acc[here, :]
                for q in range(fine):
                    part = product[at : at + span, q * rank2 : (q + 1) * rank2]
                    found = found + jnp.where(which == q, part, 0.0)
                acc[here, :] = found
                at += span

    @pl.when(step == pl.num_programs(0) - 1)
    def _():
        total = acc.shape[0]
        upper, lower = acc[: total // 2, :], acc[total // 2 :, :]
        keys = jnp.concatenate([upper[:, :ADAPTER_RANK], lower[:, :ADAPTER_RANK]], axis=1)
        values = jnp.concatenate([upper[:, ADAPTER_RANK:], lower[:, ADAPTER_RANK:]], axis=1)
        mine_ref[...] = jnp.where(second, values, keys)
        other_ref[...] = jnp.where(second, keys, values)


def shrink(pieces, blocks, names, ends, plan, down, later_than=()):
    total = sum(b.shape[0] for b in blocks)
    owned, rank2, width = down.shape
    group = next(g for g in (4, 3, 2, 1) if owned % g == 0)
    fine = next(g for g in (2, 3, 1) if group % g == 0)
    line = jax.ShapeDtypeStruct((total // 2, 2 * ADAPTER_RANK), F32)
    return pl.pallas_call(
        functools.partial(shrink_kernel, pieces, group, fine),
        grid_spec=pltpu.PrefetchScalarGridSpec(
            num_scalar_prefetch=1,
            grid=(owned // group,),
            in_specs=[
                pl.BlockSpec(memory_space=pltpu.SMEM),
                pl.BlockSpec((total, 1), lambda i, p: (0, 0)),
                pl.BlockSpec(
                    (group, rank2, width),
                    lambda i, p: (jnp.minimum(p[0] // group + i, p[1] // group), 0, 0),
                ),
            ]
            + [pl.BlockSpec(b.shape, lambda i, p: (0, 0)) for b in blocks]
            + [ANYWHERE] * len(later_than),
            out_specs=[pl.BlockSpec((total // 2, rank2), lambda i, p: (0, 0))] * 2,
            scratch_shapes=[pltpu.VMEM((total, rank2), F32)],
        ),
        out_shape=[line, line],
        compiler_params=PARAMS,
        cost_estimate=COST,
        name="shrink",
    )(plan, ends, names, down, *blocks, *later_than)


def split(x, terms):
    parts = []
    for _ in range(terms - 1):
        parts.append(x.astype(BF16).astype(F32))
        x = x - parts[-1]
    return parts + [x]


def expand_kernel(groups, sizes, heard, waits, which_ref, scale_ref, up_ref, *refs):
    lines, outs = refs[:heard], refs[heard + waits :]
    total = lines[0][...]
    for line in lines[1:]:
        total = total + line[...]
    twice, begin = [], 0
    for count in groups:
        lines = total[begin : begin + count, :]
        for side in (lines[:, :ADAPTER_RANK], lines[:, ADAPTER_RANK:]):
            twice.append(jnp.concatenate([side, side], axis=1))
        begin += count
    twice = jnp.concatenate(twice, axis=0)
    which = which_ref[...]
    parity = jnp.where(lax.broadcasted_iota(I32, (1, 2 * ADAPTER_RANK), 1) >= ADAPTER_RANK, 1, 0)
    pairs = up_ref.shape[0] // (2 * ADAPTER_RANK)
    wanted = [which == 2 * p + parity for p in range(pairs)]
    delta = None
    for term in split(twice, 3):
        spread = jnp.concatenate([jnp.where(w, term, 0.0).astype(BF16) for w in wanted], axis=1)
        product = jnp.dot(spread, up_ref[...], preferred_element_type=F32)
        delta = product if delta is None else delta + product
    adapters = lax.broadcasted_iota(I32, scale_ref.shape, 1)
    gain = jnp.sum(jnp.where(which == adapters, scale_ref[...], 0.0), axis=1, keepdims=True)
    delta = delta * gain
    begin = 0
    for size, out in zip(sizes, outs):
        piece = delta[begin : begin + size, :]
        if out.dtype == F32:
            out[...] = piece
        else:
            code_rows(piece, out)
        begin += size


def code_rows(x, out_ref):
    rows, columns = x.shape
    largest = jnp.maximum(jnp.max(jnp.abs(x), axis=1, keepdims=True), 2.0**-105)
    power = jnp.floor(jnp.log2(largest)) - 14.0
    power = power + jnp.where(largest * power_of_two(-power) > 32767.0, 1.0, 0.0)
    coded = jnp.round(x * power_of_two(-power))
    coded = jnp.minimum(jnp.maximum(coded, -32767.0), 32767.0)
    out_ref[:rows, :] = coded.astype(I32).astype(jnp.int16)
    down = lax.broadcasted_iota(I32, (rows, columns), 0)
    across = lax.broadcasted_iota(I32, (rows, columns), 1)
    line = jnp.sum(jnp.where(down == across, power, 0.0), axis=0, keepdims=True)
    line = jnp.broadcast_to(line, (16, columns)).astype(I32)
    out_ref[rows:, :] = line.astype(jnp.int16)


def power_of_two(power):
    return jnp.exp2(power).astype(BF16).astype(F32)


def expand(lines, groups, names, scale, up, sizes, kept=0, later_than=()):
    columns = up.shape[1]
    shapes = [
        jax.ShapeDtypeStruct((s, columns), F32)
        if i < kept
        else jax.ShapeDtypeStruct((s + 16, columns), jnp.int16)
        for i, s in enumerate(sizes)
    ]
    return pl.pallas_call(
        functools.partial(expand_kernel, groups, sizes, len(lines), len(later_than)),
        in_specs=[pl.BlockSpec(memory_space=pltpu.VMEM)] * (3 + len(lines))
        + [ANYWHERE] * len(later_than),
        out_shape=shapes,
        compiler_params=PARAMS,
        cost_estimate=COST,
        name="expand",
    )(names, scale, up, *lines, *later_than)


def place_kernel(begin, target_ref, rows_ref, out_ref):
    at = begin + lax.broadcasted_iota(I32, (1, rows_ref.shape[0]), 1)
    place = jnp.where(target_ref[...] == at, 1.0, 0.0).astype(BF16)
    total = None
    for term in split(rows_ref[...], 3):
        moved = jnp.dot(place, term.astype(BF16), preferred_element_type=F32)
        total = moved if total is None else total + moved
    out_ref[...] = total


def place_rows(target, begin, rows):
    return pl.pallas_call(
        functools.partial(place_kernel, begin),
        out_shape=jax.ShapeDtypeStruct((target.shape[0], rows.shape[1]), F32),
        compiler_params=PARAMS,
        cost_estimate=COST,
        name="place",
    )(target, rows)


def merge_kernel(begins, parts, target_ref, *refs):
    blocks, out_ref = refs[parts:-1], refs[-1]
    spots, powers, highs, lows = [], [], [], []
    for begin, block in zip(begins, blocks):
        count = block.shape[0] - 16
        spots.append(begin + lax.broadcasted_iota(I32, (1, count), 1))
        powers.append(block[count:, :].astype(I32)[:1, :count])
        coded = block[:count, :].astype(I32)
        high = (coded + 128) >> 8
        highs.append(high.astype(F32).astype(BF16))
        lows.append((coded - high * 256).astype(F32).astype(BF16))
    spot, power = jnp.concatenate(spots, axis=1), jnp.concatenate(powers, axis=1)
    place = jnp.where(target_ref[...] == spot, jnp.exp2(power.astype(F32)), 0.0).astype(BF16)
    total = jnp.dot(place, jnp.concatenate(highs, axis=0), preferred_element_type=F32) * 256.0
    total = total + jnp.dot(place, jnp.concatenate(lows, axis=0), preferred_element_type=F32)
    for part in refs[:parts]:
        total = total + part[...]
    out_ref[...] = total.astype(out_ref.dtype)


def merge(parts, target, begins, blocks, kind):
    return pl.pallas_call(
        functools.partial(merge_kernel, tuple(begins), len(parts)),
        out_shape=jax.ShapeDtypeStruct(parts[0].shape, kind),
        compiler_params=PARAMS,
        cost_estimate=COST,
        name="merge",
    )(target, *parts, *blocks)


def swap(x, axes, size, distance):
    return lax.ppermute(x, axes, [(i, i ^ distance) for i in range(size)])


def local(
    tokens,
    key_value_weight,
    adapter_down_weight,
    adapter_up_weight,
    adapter_scale,
    token_adapter_index,
):
    feature_axes = ("tensor", "sub")
    rows = tokens.shape[0]
    owned = adapter_down_weight.shape[0]
    owners = lax.axis_size("dp")
    sharers = lax.axis_size(feature_axes)
    me = lax.axis_index("dp")
    half = (lax.axis_index(feature_axes) >= sharers // 2).astype(I32)
    cap = up_to_16(owned * TOKEN_LIMIT)

    own, near = (0, 0, cap), (1, 0, cap)
    if owners == 4:
        usual = up_to_16(cap * 5 // 6)
        near = (1, 0, usual)
        first = up_to_16(usual * 3 // 5)
        far, last = [(3, 0, usual)], [[(2, 0, first)], [(2, first, usual - first)]]
        extra = [(j, usual, cap - usual) for j in (3, 2, 1)]
    else:
        usual, far, last, extra = cap, [], [[(j, 0, cap) for j in range(2, owners)]], []

    ids_row = token_adapter_index.reshape(1, rows)
    ids_heard = [ids_row] + [swap(ids_row, "dp", owners, j) for j in range(1, owners)]
    slot, target = route(ids_row, me.reshape(1), owners, owned, cap)
    sent = far + [near]
    packed = dict(zip(sent, sort_rows(tokens, slot, cap, sent, tuple(ids_heard[1:]))))
    received = {p: swap(packed[p], "dp", owners, p[0]) for p in sent}
    base_part, base_done = base_product(tokens, key_value_weight, packed[near])
    base = lax.psum_scatter(base_part, feature_axes, scatter_dimension=1, tiled=True)
    packed |= zip([own] + extra, sort_rows(tokens, slot, cap, [own] + extra, (base_done,)))
    gated = [p for pieces in last for p in pieces]
    packed |= zip(gated, sort_rows(tokens, slot, cap, gated, (received[near],)))
    received |= {p: swap(packed[p], "dp", owners, p[0]) for p in gated}

    early = [own, near] + far
    sets = [[p] for p in early] + [early] + last + ([extra] if extra else [])
    here = jnp.stack([me.astype(I32), half])
    names, ends, plans, largest = name_rows(ids_heard, here, owned, sets)

    if owned % 2:
        adapter_up_weight = jnp.pad(adapter_up_weight, ((0, 1), (0, 0), (0, 0)))
    up = adapter_up_weight.reshape(-1, adapter_up_weight.shape[2])
    scale = adapter_scale.reshape(1, owned)

    def exchange(mine, other, steps=2):
        if sharers == 4 and steps == 2:
            mine = mine + swap(other, "tensor", 2, 1)
            return [mine, swap(mine, "sub", 2, 1)]
        return [mine] + [
            swap(mine if d < sharers // 2 else other, feature_axes, sharers, d)
            for d in range(1, sharers)
        ]

    def deltas_of(pieces, blocks, names, ends, plan, down, up, scale, later_than):
        mine, other = shrink(pieces, blocks, names, ends, plan, down, later_than)
        sizes = tuple(b.shape[0] for b in blocks)
        lines = exchange(mine, other)
        return expand(lines, (mine.shape[0],), names, scale, up, sizes)

    def send_back(pieces, deltas):
        return [swap(d, "dp", owners, p[0]) for p, d in zip(pieces, deltas)]

    def begins(pieces):
        return [b * cap + f for b, f, _ in pieces]

    weights = (adapter_down_weight, up, scale)
    packed |= zip([own] + extra, sort_rows(tokens, slot, cap, [own] + extra, (base_done,)))
    for d in range(1, lax.axis_size("parts")):
        largest = jnp.maximum(largest, swap(largest, "parts", lax.axis_size("parts"), d))
    shares, waits = [], ()
    for k, p in enumerate(early):
        rows_here = received.get(p, packed[p])
        shares.append(
            shrink([p], [rows_here], names[k], ends, plans[k], adapter_down_weight, waits)
        )
        waits = (shares[-1][0], packed[gated[0]])
    lines = exchange(*(jnp.concatenate(pair, axis=0) for pair in zip(*shares)), steps=1)
    sizes = tuple(p[2] for p in early)
    here = len(early)
    deltas = expand(lines, tuple(c // 2 for c in sizes), names[here], scale, up, sizes, kept=1)
    parts = [base, place_rows(target, own[0] * cap, deltas[0])]
    returned = send_back(early[1:], deltas[1:])
    done = early[1:]
    for k, pieces in enumerate(last):
        blocks = [received[p] for p in pieces]
        waits = (deltas[0], parts[1], largest)
        deltas = deltas_of(
            pieces, blocks, names[here + 1 + k], ends, plans[here + 1 + k], *weights, waits
        )
        returned += send_back(pieces, deltas)
        done += pieces

    def finish(parts, target, returned, *_):
        return merge(parts, target, begins(done), returned, BF16)

    if not extra:
        return finish(parts, target, returned)

    def finish_with_extra(parts, target, returned, blocks, names, ends, plan, weights):
        blocks = send_back(extra, blocks)
        deltas = deltas_of(extra, blocks, names, ends, plan, *weights, ())
        deltas = send_back(extra, deltas)
        return merge(parts, target, begins(done + extra), returned + deltas, BF16)

    return lax.cond(
        largest[0, 0] > usual,
        finish_with_extra,
        finish,
        parts,
        target,
        returned,
        [packed[p] for p in extra],
        names[-1],
        ends,
        plans[-1],
        weights,
    )


def solution(mesh):
    return jax.shard_map(
        local,
        mesh=mesh,
        in_specs=(
            P(("parts", "dp"), ("tensor", "sub")),
            P(("tensor", "sub"), None),
            P("dp", None, ("tensor", "sub")),
            P("dp", None, ("tensor", "sub")),
            P("dp"),
            P(("parts", "dp"), None),
        ),
        out_specs=P(("parts", "dp"), ("tensor", "sub")),
        check_vma=False,
    )
```

```python
import functools

import jax
import jax.numpy as jnp
from jax import lax
from jax.experimental import pallas as pl
from jax.experimental.pallas import tpu as pltpu
from jax.sharding import PartitionSpec as P

ADAPTER_RANK = 64
TOKEN_LIMIT = 12
VMEM_LIMIT = 28 * 1024 * 1024
F32 = jnp.float32
BF16 = jnp.bfloat16
I32 = jnp.int32
ANYWHERE = pl.BlockSpec(memory_space=pl.ANY)
COST = pl.CostEstimate(flops=1, transcendentals=0, bytes_accessed=1)
HEAD = pl.CostEstimate(flops=10**9, transcendentals=0, bytes_accessed=1)
PARAMS = pltpu.CompilerParams(vmem_limit_bytes=VMEM_LIMIT)


def up_to_16(count):
    return -(-count // 16) * 16


def owner_of(ids, owners, owned):
    total = jnp.zeros_like(ids)
    for o in range(1, owners):
        total = total + jnp.where(ids >= o * owned, 1, 0)
    return total


def as_column(line):
    size = line.shape[1]
    here = lax.broadcasted_iota(I32, (size, size), 0) == lax.broadcasted_iota(I32, (size, size), 1)
    return jnp.sum(jnp.where(here, line, 0), axis=1, keepdims=True)


def route_kernel(owners, owned, cap, me_ref, row_ref, slot_ref, target_ref):
    rows = row_ref.shape[1]
    id_row = row_ref[...]
    key_row = id_row * rows + lax.broadcasted_iota(I32, (1, rows), 1)
    key_col = as_column(key_row)
    own_row = owner_of(id_row, owners, owned)
    before = (key_col < key_row) & (key_col >= own_row * (owned * rows))
    rank = jnp.sum(jnp.where(before, 1, 0), axis=0, keepdims=True)
    found = (own_row ^ me_ref[0]) * cap + rank
    slot_ref[...] = found
    target_ref[...] = as_column(found)


def route(ids_row, me, owners, owned, cap):
    rows = ids_row.shape[1]
    return pl.pallas_call(
        functools.partial(route_kernel, owners, owned, cap),
        in_specs=[
            pl.BlockSpec(memory_space=pltpu.SMEM),
            pl.BlockSpec(memory_space=pltpu.VMEM),
        ],
        out_shape=[jax.ShapeDtypeStruct((1, rows), I32), jax.ShapeDtypeStruct((rows, 1), I32)],
        compiler_params=PARAMS,
        cost_estimate=HEAD,
        name="route",
    )(me, ids_row)


def sort_kernel(cap, pieces, waits, slot_ref, tok_ref, *refs):
    outs, place = refs[waits:-1], refs[-1]

    @pl.when(pl.program_id(0) == 0)
    def _():
        begin = 0
        for block, first, count in pieces:
            at = block * cap + first + lax.broadcasted_iota(I32, (count, slot_ref.shape[1]), 0)
            found = jnp.where(at == slot_ref[...], 1.0, 0.0).astype(BF16)
            place[begin : begin + count, :] = found
            begin += count

    moved = jnp.dot(place[...], tok_ref[...], preferred_element_type=F32).astype(BF16)
    begin = 0
    for (_, _, count), out in zip(pieces, outs):
        out[...] = moved[begin : begin + count, :]
        begin += count


def sort_rows(tokens, slot, cap, pieces, later_than=()):
    rows, width = tokens.shape
    step = min(512, width)
    return pl.pallas_call(
        functools.partial(sort_kernel, cap, pieces, len(later_than)),
        grid=(width // step,),
        in_specs=[
            pl.BlockSpec((1, rows), lambda i: (0, 0)),
            pl.BlockSpec((rows, step), lambda i: (0, i)),
        ]
        + [ANYWHERE] * len(later_than),
        out_specs=[pl.BlockSpec((count, step), lambda i: (0, i)) for _, _, count in pieces],
        out_shape=[jax.ShapeDtypeStruct((count, width), BF16) for _, _, count in pieces],
        scratch_shapes=[pltpu.VMEM((sum(c for _, _, c in pieces), rows), BF16)],
        compiler_params=PARAMS,
        cost_estimate=HEAD,
        name="sort",
    )(slot, tokens, *later_than)


def name_kernel(owners, owned, sets, here_ref, *refs):
    lines, outs, (ends_ref, plan_ref, most_ref) = refs[:owners], refs[owners:-3], refs[-3:]
    me, half = here_ref[0], here_ref[1]
    held = -(-owned // 8) * 8
    owner = lax.broadcasted_iota(I32, (-(-owners // 8) * 8, 1), 0)
    adapter = lax.broadcasted_iota(I32, (held, 1), 0)
    diagonal = adapter == lax.broadcasted_iota(I32, (held, 128), 1)
    used = lax.broadcasted_iota(I32, (1, 128), 1) < owned
    most = jnp.zeros(owner.shape, I32)
    ends = []
    for j, line in enumerate(lines):
        ids = line[...]
        chosen = jnp.where(owner_of(ids, owners, owned) == owner, 1, 0)
        count = jnp.sum(chosen, axis=1, keepdims=True)
        far = (me ^ j ^ owner >= 1) & (owner < owners)
        most = jnp.maximum(most, jnp.where(far, count, 0))
        mine = ids - me * owned
        upto = jnp.sum(jnp.where((mine >= 0) & (mine <= adapter), 1, 0), axis=1, keepdims=True)
        across = jnp.sum(jnp.where(diagonal, upto, 0), axis=0, keepdims=True)
        ends.append(jnp.where(used, across, 1 << 20))
        ends_ref[j : j + 1, :] = ends[j]
    most_ref[...] = jnp.broadcast_to(jnp.max(most, axis=0, keepdims=True), most_ref.shape)
    for k, (pieces, out) in enumerate(zip(sets, outs)):
        begin, low, high = 0, owned - 1, 0
        for block, first, count in pieces:
            at = first + lax.broadcasted_iota(I32, (count, 1), 0)
            names = jnp.sum(jnp.where(ends[block] <= at, 1, 0), axis=1, keepdims=True)
            out[begin : begin + count, :] = names
            low = jnp.minimum(low, jnp.min(names))
            high = jnp.maximum(high, jnp.max(jnp.where(names < owned, names, 0)))
            begin += count
        plan_ref[3 * k] = low
        plan_ref[3 * k + 1] = jnp.maximum(low, high)
        plan_ref[3 * k + 2] = half


def name_rows(lines, here, owned, sets):
    totals = [sum(c for _, _, c in pieces) for pieces in sets]
    on_chip, scalars = (pl.BlockSpec(memory_space=m) for m in (pltpu.VMEM, pltpu.SMEM))
    *names, ends, plan, most = pl.pallas_call(
        functools.partial(name_kernel, len(lines), owned, sets),
        in_specs=[scalars] + [on_chip] * len(lines),
        out_specs=[on_chip] * len(sets) + [on_chip, scalars, on_chip],
        out_shape=[jax.ShapeDtypeStruct((t, 1), I32) for t in totals]
        + [
            jax.ShapeDtypeStruct((len(lines), 128), I32),
            jax.ShapeDtypeStruct((3 * len(sets),), I32),
            jax.ShapeDtypeStruct((1, 128), I32),
        ],
        compiler_params=PARAMS,
        cost_estimate=COST,
        name="name_rows",
    )(here, *lines)
    plans = [plan[3 * k : 3 * k + 3] for k in range(len(sets))]
    return names, ends, plans, most


def base_kernel(tok_ref, weight_ref, _, out_ref, done_ref):
    done_ref[...] = jnp.zeros_like(done_ref)
    out_ref[...] = jnp.dot(tok_ref[...], weight_ref[...], preferred_element_type=F32)


def base_product(tokens, weight, later_than):
    (rows, width), columns = tokens.shape, weight.shape[1]
    step = min(256, columns)
    return pl.pallas_call(
        base_kernel,
        grid=(columns // step,),
        in_specs=[
            pl.BlockSpec((rows, width), lambda i: (0, 0)),
            pl.BlockSpec((width, step), lambda i: (0, i)),
            ANYWHERE,
        ],
        out_specs=[
            pl.BlockSpec((rows, step), lambda i: (0, i)),
            pl.BlockSpec((8, 128), lambda i: (0, 0)),
        ],
        out_shape=[
            jax.ShapeDtypeStruct((rows, columns), F32),
            jax.ShapeDtypeStruct((8, 128), F32),
        ],
        compiler_params=PARAMS,
        cost_estimate=HEAD,
        name="base",
    )(tokens, weight, later_than)


def shrink_kernel(pieces, group, fine, plan_ref, ends_ref, which_ref, down_ref, *refs):
    blocks, (mine_ref, other_ref, acc) = refs[: len(pieces)], refs[-3:]
    step, rank2 = pl.program_id(0), 2 * ADAPTER_RANK
    low, high, second = plan_ref[0], plan_ref[1], plan_ref[2] == 1
    begin = (low // group + step) * group

    @pl.when(step == 0)
    def _():
        acc[...] = jnp.zeros_like(acc)

    for f in range(0, group, fine):

        @pl.when((begin + f <= high) & (begin + f + fine > low))
        def _(f=f):
            adapter = begin + f
            windows, spans, at = [], [], 0
            for (block, first, size), rows in zip(pieces, blocks):
                span = min(up_to_16(fine * TOKEN_LIMIT + 15), size)
                ahead = ends_ref[block, jnp.maximum(adapter - 1, 0)]
                start = jnp.where(adapter > 0, ahead, 0) - first
                start = jnp.minimum(jnp.maximum(start, 0), size - span) // 16 * 16
                windows.append(rows[pl.ds(pl.multiple_of(start, 16), span), :])
                spans.append((pl.ds(pl.multiple_of(at + start, 16), span), span))
                at += size
            factors = down_ref[f : f + fine].reshape(fine * rank2, down_ref.shape[2])
            product = lax.dot_general(
                jnp.concatenate(windows, axis=0),
                factors,
                (((1,), (1,)), ((), ())),
                preferred_element_type=F32,
            )
            at = 0
            for here, span in spans:
                which = which_ref[here, :] - adapter
                found = acc[here, :]
                for q in range(fine):
                    part = product[at : at + span, q * rank2 : (q + 1) * rank2]
                    found = found + jnp.where(which == q, part, 0.0)
                acc[here, :] = found
                at += span

    @pl.when(step == pl.num_programs(0) - 1)
    def _():
        total = acc.shape[0]
        upper, lower = acc[: total // 2, :], acc[total // 2 :, :]
        keys = jnp.concatenate([upper[:, :ADAPTER_RANK], lower[:, :ADAPTER_RANK]], axis=1)
        values = jnp.concatenate([upper[:, ADAPTER_RANK:], lower[:, ADAPTER_RANK:]], axis=1)
        mine_ref[...] = jnp.where(second, values, keys)
        other_ref[...] = jnp.where(second, keys, values)


def shrink(pieces, blocks, names, ends, plan, down, later_than=()):
    total = sum(b.shape[0] for b in blocks)
    owned, rank2, width = down.shape
    group = next(g for g in (4, 3, 2, 1) if owned % g == 0)
    fine = next(g for g in (2, 3, 1) if group % g == 0)
    line = jax.ShapeDtypeStruct((total // 2, 2 * ADAPTER_RANK), F32)
    return pl.pallas_call(
        functools.partial(shrink_kernel, pieces, group, fine),
        grid_spec=pltpu.PrefetchScalarGridSpec(
            num_scalar_prefetch=1,
            grid=(owned // group,),
            in_specs=[
                pl.BlockSpec(memory_space=pltpu.SMEM),
                pl.BlockSpec((total, 1), lambda i, p: (0, 0)),
                pl.BlockSpec(
                    (group, rank2, width),
                    lambda i, p: (jnp.minimum(p[0] // group + i, p[1] // group), 0, 0),
                ),
            ]
            + [pl.BlockSpec(b.shape, lambda i, p: (0, 0)) for b in blocks]
            + [ANYWHERE] * len(later_than),
            out_specs=[pl.BlockSpec((total // 2, rank2), lambda i, p: (0, 0))] * 2,
            scratch_shapes=[pltpu.VMEM((total, rank2), F32)],
        ),
        out_shape=[line, line],
        compiler_params=PARAMS,
        cost_estimate=COST,
        name="shrink",
    )(plan, ends, names, down, *blocks, *later_than)


def split(x, terms):
    parts = []
    for _ in range(terms - 1):
        parts.append(x.astype(BF16).astype(F32))
        x = x - parts[-1]
    return parts + [x]


def expand_kernel(groups, sizes, heard, waits, which_ref, scale_ref, up_ref, *refs):
    lines, outs = refs[:heard], refs[heard + waits :]
    total = lines[0][...]
    for line in lines[1:]:
        total = total + line[...]
    twice, begin = [], 0
    for count in groups:
        lines = total[begin : begin + count, :]
        for side in (lines[:, :ADAPTER_RANK], lines[:, ADAPTER_RANK:]):
            twice.append(jnp.concatenate([side, side], axis=1))
        begin += count
    twice = jnp.concatenate(twice, axis=0)
    which = which_ref[...]
    parity = jnp.where(lax.broadcasted_iota(I32, (1, 2 * ADAPTER_RANK), 1) >= ADAPTER_RANK, 1, 0)
    pairs = up_ref.shape[0] // (2 * ADAPTER_RANK)
    wanted = [which == 2 * p + parity for p in range(pairs)]
    delta = None
    for term in split(twice, 3):
        spread = jnp.concatenate([jnp.where(w, term, 0.0).astype(BF16) for w in wanted], axis=1)
        product = jnp.dot(spread, up_ref[...], preferred_element_type=F32)
        delta = product if delta is None else delta + product
    adapters = lax.broadcasted_iota(I32, scale_ref.shape, 1)
    gain = jnp.sum(jnp.where(which == adapters, scale_ref[...], 0.0), axis=1, keepdims=True)
    delta = delta * gain
    begin = 0
    for size, out in zip(sizes, outs):
        piece = delta[begin : begin + size, :]
        if out.dtype == F32:
            out[...] = piece
        else:
            code_rows(piece, out)
        begin += size


def code_rows(x, out_ref):
    rows, columns = x.shape
    largest = jnp.maximum(jnp.max(jnp.abs(x), axis=1, keepdims=True), 2.0**-105)
    power = jnp.floor(jnp.log2(largest)) - 14.0
    power = power + jnp.where(largest * power_of_two(-power) > 32767.0, 1.0, 0.0)
    coded = jnp.round(x * power_of_two(-power))
    coded = jnp.minimum(jnp.maximum(coded, -32767.0), 32767.0)
    out_ref[:rows, :] = coded.astype(I32).astype(jnp.int16)
    down = lax.broadcasted_iota(I32, (rows, columns), 0)
    across = lax.broadcasted_iota(I32, (rows, columns), 1)
    line = jnp.sum(jnp.where(down == across, power, 0.0), axis=0, keepdims=True)
    line = jnp.broadcast_to(line, (16, columns)).astype(I32)
    out_ref[rows:, :] = line.astype(jnp.int16)


def power_of_two(power):
    return jnp.exp2(power).astype(BF16).astype(F32)


def expand(lines, groups, names, scale, up, sizes, kept=0, later_than=()):
    columns = up.shape[1]
    shapes = [
        jax.ShapeDtypeStruct((s, columns), F32)
        if i < kept
        else jax.ShapeDtypeStruct((s + 16, columns), jnp.int16)
        for i, s in enumerate(sizes)
    ]
    return pl.pallas_call(
        functools.partial(expand_kernel, groups, sizes, len(lines), len(later_than)),
        in_specs=[pl.BlockSpec(memory_space=pltpu.VMEM)] * (3 + len(lines))
        + [ANYWHERE] * len(later_than),
        out_shape=shapes,
        compiler_params=PARAMS,
        cost_estimate=COST,
        name="expand",
    )(names, scale, up, *lines, *later_than)


def place_kernel(begin, target_ref, rows_ref, out_ref):
    at = begin + lax.broadcasted_iota(I32, (1, rows_ref.shape[0]), 1)
    place = jnp.where(target_ref[...] == at, 1.0, 0.0).astype(BF16)
    total = None
    for term in split(rows_ref[...], 3):
        moved = jnp.dot(place, term.astype(BF16), preferred_element_type=F32)
        total = moved if total is None else total + moved
    out_ref[...] = total


def place_rows(target, begin, rows):
    return pl.pallas_call(
        functools.partial(place_kernel, begin),
        out_shape=jax.ShapeDtypeStruct((target.shape[0], rows.shape[1]), F32),
        compiler_params=PARAMS,
        cost_estimate=COST,
        name="place",
    )(target, rows)


def merge_kernel(begins, parts, target_ref, *refs):
    blocks, out_ref = refs[parts:-1], refs[-1]
    spots, powers, highs, lows = [], [], [], []
    for begin, block in zip(begins, blocks):
        count = block.shape[0] - 16
        spots.append(begin + lax.broadcasted_iota(I32, (1, count), 1))
        powers.append(block[count:, :].astype(I32)[:1, :count])
        coded = block[:count, :].astype(I32)
        high = (coded + 128) >> 8
        highs.append(high.astype(F32).astype(BF16))
        lows.append((coded - high * 256).astype(F32).astype(BF16))
    spot, power = jnp.concatenate(spots, axis=1), jnp.concatenate(powers, axis=1)
    place = jnp.where(target_ref[...] == spot, jnp.exp2(power.astype(F32)), 0.0).astype(BF16)
    total = jnp.dot(place, jnp.concatenate(highs, axis=0), preferred_element_type=F32) * 256.0
    total = total + jnp.dot(place, jnp.concatenate(lows, axis=0), preferred_element_type=F32)
    for part in refs[:parts]:
        total = total + part[...]
    out_ref[...] = total.astype(out_ref.dtype)


def merge(parts, target, begins, blocks, kind):
    return pl.pallas_call(
        functools.partial(merge_kernel, tuple(begins), len(parts)),
        out_shape=jax.ShapeDtypeStruct(parts[0].shape, kind),
        compiler_params=PARAMS,
        cost_estimate=COST,
        name="merge",
    )(target, *parts, *blocks)


def swap(x, axes, size, distance):
    return lax.ppermute(x, axes, [(i, i ^ distance) for i in range(size)])


def local(
    tokens,
    key_value_weight,
    adapter_down_weight,
    adapter_up_weight,
    adapter_scale,
    token_adapter_index,
):
    feature_axes = ("tensor", "sub")
    rows = tokens.shape[0]
    owned = adapter_down_weight.shape[0]
    owners = lax.axis_size("dp")
    sharers = lax.axis_size(feature_axes)
    me = lax.axis_index("dp")
    half = (lax.axis_index(feature_axes) >= sharers // 2).astype(I32)
    cap = up_to_16(owned * TOKEN_LIMIT)

    own, near = (0, 0, cap), (1, 0, cap)
    if owners == 4:
        usual = up_to_16(cap * 5 // 6)
        near = (1, 0, usual)
        first = up_to_16(usual * 3 // 5)
        far, last = [(3, 0, usual)], [[(2, 0, first)], [(2, first, usual - first)]]
        extra = [(j, usual, cap - usual) for j in (3, 2, 1)]
    else:
        usual, far, last, extra = cap, [], [[(j, 0, cap) for j in range(2, owners)]], []

    ids_row = token_adapter_index.reshape(1, rows)
    ids_heard = [ids_row] + [swap(ids_row, "dp", owners, j) for j in range(1, owners)]
    slot, target = route(ids_row, me.reshape(1), owners, owned, cap)
    sent = far + [near]
    packed = dict(zip(sent, sort_rows(tokens, slot, cap, sent, tuple(ids_heard[1:]))))
    received = {p: swap(packed[p], "dp", owners, p[0]) for p in sent}
    base_part, base_done = base_product(tokens, key_value_weight, packed[near])
    base = lax.psum_scatter(base_part, feature_axes, scatter_dimension=1, tiled=True)
    packed |= zip([own] + extra, sort_rows(tokens, slot, cap, [own] + extra, (base_done,)))
    gated = [p for pieces in last for p in pieces]

    early = [own, near] + far
    sets = [[p] for p in early] + [early] + last + ([extra] if extra else [])
    here = jnp.stack([me.astype(I32), half])
    names, ends, plans, largest = name_rows(ids_heard, here, owned, sets)

    if owned % 2:
        adapter_up_weight = jnp.pad(adapter_up_weight, ((0, 1), (0, 0), (0, 0)))
    up = adapter_up_weight.reshape(-1, adapter_up_weight.shape[2])
    scale = adapter_scale.reshape(1, owned)

    def exchange(mine, other, steps=2):
        if sharers == 4 and steps == 2:
            mine = mine + swap(other, "tensor", 2, 1)
            return [mine, swap(mine, "sub", 2, 1)]
        return [mine] + [
            swap(mine if d < sharers // 2 else other, feature_axes, sharers, d)
            for d in range(1, sharers)
        ]

    def deltas_of(pieces, blocks, names, ends, plan, down, up, scale, later_than):
        mine, other = shrink(pieces, blocks, names, ends, plan, down, later_than)
        sizes = tuple(b.shape[0] for b in blocks)
        lines = exchange(mine, other)
        return expand(lines, (mine.shape[0],), names, scale, up, sizes)

    def send_back(pieces, deltas):
        return [swap(d, "dp", owners, p[0]) for p, d in zip(pieces, deltas)]

    def begins(pieces):
        return [b * cap + f for b, f, _ in pieces]

    weights = (adapter_down_weight, up, scale)
    packed |= zip([own] + extra, sort_rows(tokens, slot, cap, [own] + extra, (base_done,)))
    for d in range(1, lax.axis_size("parts")):
        largest = jnp.maximum(largest, swap(largest, "parts", lax.axis_size("parts"), d))
    down = adapter_down_weight
    shares = [shrink([own], [packed[own]], names[0], ends, plans[0], down)]
    packed |= zip(gated, sort_rows(tokens, slot, cap, gated, (shares[0][0],)))
    received |= {p: swap(packed[p], "dp", owners, p[0]) for p in gated}
    waits = (packed[gated[0]],)
    for k, p in enumerate(early[1:], 1):
        shares.append(shrink([p], [received[p]], names[k], ends, plans[k], down, waits))
        waits = (shares[-1][0],)
    lines = exchange(*(jnp.concatenate(pair, axis=0) for pair in zip(*shares)), steps=1)
    sizes = tuple(p[2] for p in early)
    here = len(early)
    deltas = expand(lines, tuple(c // 2 for c in sizes), names[here], scale, up, sizes, kept=1)
    parts = [base, place_rows(target, own[0] * cap, deltas[0])]
    returned = send_back(early[1:], deltas[1:])
    done = early[1:]
    for k, pieces in enumerate(last):
        blocks = [received[p] for p in pieces]
        waits = (deltas[0], parts[1], largest)
        deltas = deltas_of(
            pieces, blocks, names[here + 1 + k], ends, plans[here + 1 + k], *weights, waits
        )
        returned += send_back(pieces, deltas)
        done += pieces

    def finish(parts, target, returned, *_):
        return merge(parts, target, begins(done), returned, BF16)

    if not extra:
        return finish(parts, target, returned)

    def finish_with_extra(parts, target, returned, blocks, names, ends, plan, weights):
        blocks = send_back(extra, blocks)
        deltas = deltas_of(extra, blocks, names, ends, plan, *weights, ())
        deltas = send_back(extra, deltas)
        return merge(parts, target, begins(done + extra), returned + deltas, BF16)

    return lax.cond(
        largest[0, 0] > usual,
        finish_with_extra,
        finish,
        parts,
        target,
        returned,
        [packed[p] for p in extra],
        names[-1],
        ends,
        plans[-1],
        weights,
    )


def solution(mesh):
    return jax.shard_map(
        local,
        mesh=mesh,
        in_specs=(
            P(("parts", "dp"), ("tensor", "sub")),
            P(("tensor", "sub"), None),
            P("dp", None, ("tensor", "sub")),
            P("dp", None, ("tensor", "sub")),
            P("dp"),
            P(("parts", "dp"), None),
        ),
        out_specs=P(("parts", "dp"), ("tensor", "sub")),
        check_vma=False,
    )
```

```python
import functools

import jax
import jax.numpy as jnp
from jax import lax
from jax.experimental import pallas as pl
from jax.experimental.pallas import tpu as pltpu
from jax.sharding import PartitionSpec as P

ADAPTER_RANK = 64
TOKEN_LIMIT = 12
VMEM_LIMIT = 28 * 1024 * 1024
F32 = jnp.float32
BF16 = jnp.bfloat16
I32 = jnp.int32
ANYWHERE = pl.BlockSpec(memory_space=pl.ANY)
COST = pl.CostEstimate(flops=1, transcendentals=0, bytes_accessed=1)
HEAD = pl.CostEstimate(flops=10**9, transcendentals=0, bytes_accessed=1)
PARAMS = pltpu.CompilerParams(vmem_limit_bytes=VMEM_LIMIT)


def up_to_16(count):
    return -(-count // 16) * 16


def owner_of(ids, owners, owned):
    total = jnp.zeros_like(ids)
    for o in range(1, owners):
        total = total + jnp.where(ids >= o * owned, 1, 0)
    return total


def as_column(line):
    size = line.shape[1]
    here = lax.broadcasted_iota(I32, (size, size), 0) == lax.broadcasted_iota(I32, (size, size), 1)
    return jnp.sum(jnp.where(here, line, 0), axis=1, keepdims=True)


def route_kernel(owners, owned, cap, me_ref, row_ref, slot_ref, target_ref):
    rows = row_ref.shape[1]
    id_row = row_ref[...]
    key_row = id_row * rows + lax.broadcasted_iota(I32, (1, rows), 1)
    key_col = as_column(key_row)
    own_row = owner_of(id_row, owners, owned)
    before = (key_col < key_row) & (key_col >= own_row * (owned * rows))
    rank = jnp.sum(jnp.where(before, 1, 0), axis=0, keepdims=True)
    found = (own_row ^ me_ref[0]) * cap + rank
    slot_ref[...] = found
    target_ref[...] = as_column(found)


def route(ids_row, me, owners, owned, cap):
    rows = ids_row.shape[1]
    return pl.pallas_call(
        functools.partial(route_kernel, owners, owned, cap),
        in_specs=[
            pl.BlockSpec(memory_space=pltpu.SMEM),
            pl.BlockSpec(memory_space=pltpu.VMEM),
        ],
        out_shape=[jax.ShapeDtypeStruct((1, rows), I32), jax.ShapeDtypeStruct((rows, 1), I32)],
        compiler_params=PARAMS,
        cost_estimate=HEAD,
        name="route",
    )(me, ids_row)


def sort_kernel(cap, pieces, waits, slot_ref, tok_ref, *refs):
    outs, place = refs[waits:-1], refs[-1]

    @pl.when(pl.program_id(0) == 0)
    def _():
        begin = 0
        for block, first, count in pieces:
            at = block * cap + first + lax.broadcasted_iota(I32, (count, slot_ref.shape[1]), 0)
            found = jnp.where(at == slot_ref[...], 1.0, 0.0).astype(BF16)
            place[begin : begin + count, :] = found
            begin += count

    moved = jnp.dot(place[...], tok_ref[...], preferred_element_type=F32).astype(BF16)
    begin = 0
    for (_, _, count), out in zip(pieces, outs):
        out[...] = moved[begin : begin + count, :]
        begin += count


def sort_rows(tokens, slot, cap, pieces, later_than=()):
    rows, width = tokens.shape
    step = min(512, width)
    return pl.pallas_call(
        functools.partial(sort_kernel, cap, pieces, len(later_than)),
        grid=(width // step,),
        in_specs=[
            pl.BlockSpec((1, rows), lambda i: (0, 0)),
            pl.BlockSpec((rows, step), lambda i: (0, i)),
        ]
        + [ANYWHERE] * len(later_than),
        out_specs=[pl.BlockSpec((count, step), lambda i: (0, i)) for _, _, count in pieces],
        out_shape=[jax.ShapeDtypeStruct((count, width), BF16) for _, _, count in pieces],
        scratch_shapes=[pltpu.VMEM((sum(c for _, _, c in pieces), rows), BF16)],
        compiler_params=PARAMS,
        cost_estimate=HEAD,
        name="sort",
    )(slot, tokens, *later_than)


def name_kernel(owners, owned, sets, here_ref, *refs):
    lines, outs, (ends_ref, plan_ref, most_ref) = refs[:owners], refs[owners:-3], refs[-3:]
    me, half = here_ref[0], here_ref[1]
    held = -(-owned // 8) * 8
    owner = lax.broadcasted_iota(I32, (-(-owners // 8) * 8, 1), 0)
    adapter = lax.broadcasted_iota(I32, (held, 1), 0)
    diagonal = adapter == lax.broadcasted_iota(I32, (held, 128), 1)
    used = lax.broadcasted_iota(I32, (1, 128), 1) < owned
    most = jnp.zeros(owner.shape, I32)
    ends = []
    for j, line in enumerate(lines):
        ids = line[...]
        chosen = jnp.where(owner_of(ids, owners, owned) == owner, 1, 0)
        count = jnp.sum(chosen, axis=1, keepdims=True)
        far = (me ^ j ^ owner >= 1) & (owner < owners)
        most = jnp.maximum(most, jnp.where(far, count, 0))
        mine = ids - me * owned
        upto = jnp.sum(jnp.where((mine >= 0) & (mine <= adapter), 1, 0), axis=1, keepdims=True)
        across = jnp.sum(jnp.where(diagonal, upto, 0), axis=0, keepdims=True)
        ends.append(jnp.where(used, across, 1 << 20))
        ends_ref[j : j + 1, :] = ends[j]
    most_ref[...] = jnp.broadcast_to(jnp.max(most, axis=0, keepdims=True), most_ref.shape)
    for k, (pieces, out) in enumerate(zip(sets, outs)):
        begin, low, high = 0, owned - 1, 0
        for block, first, count in pieces:
            at = first + lax.broadcasted_iota(I32, (count, 1), 0)
            names = jnp.sum(jnp.where(ends[block] <= at, 1, 0), axis=1, keepdims=True)
            out[begin : begin + count, :] = names
            low = jnp.minimum(low, jnp.min(names))
            high = jnp.maximum(high, jnp.max(jnp.where(names < owned, names, 0)))
            begin += count
        plan_ref[3 * k] = low
        plan_ref[3 * k + 1] = jnp.maximum(low, high)
        plan_ref[3 * k + 2] = half


def name_rows(lines, here, owned, sets):
    totals = [sum(c for _, _, c in pieces) for pieces in sets]
    on_chip, scalars = (pl.BlockSpec(memory_space=m) for m in (pltpu.VMEM, pltpu.SMEM))
    *names, ends, plan, most = pl.pallas_call(
        functools.partial(name_kernel, len(lines), owned, sets),
        in_specs=[scalars] + [on_chip] * len(lines),
        out_specs=[on_chip] * len(sets) + [on_chip, scalars, on_chip],
        out_shape=[jax.ShapeDtypeStruct((t, 1), I32) for t in totals]
        + [
            jax.ShapeDtypeStruct((len(lines), 128), I32),
            jax.ShapeDtypeStruct((3 * len(sets),), I32),
            jax.ShapeDtypeStruct((1, 128), I32),
        ],
        compiler_params=PARAMS,
        cost_estimate=COST,
        name="name_rows",
    )(here, *lines)
    plans = [plan[3 * k : 3 * k + 3] for k in range(len(sets))]
    return names, ends, plans, most


def base_kernel(tok_ref, weight_ref, _, out_ref, done_ref):
    done_ref[...] = jnp.zeros_like(done_ref)
    out_ref[...] = jnp.dot(tok_ref[...], weight_ref[...], preferred_element_type=F32)


def base_product(tokens, weight, later_than):
    (rows, width), columns = tokens.shape, weight.shape[1]
    step = min(256, columns)
    return pl.pallas_call(
        base_kernel,
        grid=(columns // step,),
        in_specs=[
            pl.BlockSpec((rows, width), lambda i: (0, 0)),
            pl.BlockSpec((width, step), lambda i: (0, i)),
            ANYWHERE,
        ],
        out_specs=[
            pl.BlockSpec((rows, step), lambda i: (0, i)),
            pl.BlockSpec((8, 128), lambda i: (0, 0)),
        ],
        out_shape=[
            jax.ShapeDtypeStruct((rows, columns), F32),
            jax.ShapeDtypeStruct((8, 128), F32),
        ],
        compiler_params=PARAMS,
        cost_estimate=HEAD,
        name="base",
    )(tokens, weight, later_than)


def shrink_kernel(pieces, group, fine, plan_ref, ends_ref, which_ref, down_ref, *refs):
    blocks, (mine_ref, other_ref, acc) = refs[: len(pieces)], refs[-3:]
    step, rank2 = pl.program_id(0), 2 * ADAPTER_RANK
    low, high, second = plan_ref[0], plan_ref[1], plan_ref[2] == 1
    begin = (low // group + step) * group

    @pl.when(step == 0)
    def _():
        acc[...] = jnp.zeros_like(acc)

    for f in range(0, group, fine):

        @pl.when((begin + f <= high) & (begin + f + fine > low))
        def _(f=f):
            adapter = begin + f
            windows, spans, at = [], [], 0
            for (block, first, size), rows in zip(pieces, blocks):
                span = min(up_to_16(fine * TOKEN_LIMIT + 15), size)
                ahead = ends_ref[block, jnp.maximum(adapter - 1, 0)]
                start = jnp.where(adapter > 0, ahead, 0) - first
                start = jnp.minimum(jnp.maximum(start, 0), size - span) // 16 * 16
                windows.append(rows[pl.ds(pl.multiple_of(start, 16), span), :])
                spans.append((pl.ds(pl.multiple_of(at + start, 16), span), span))
                at += size
            factors = down_ref[f : f + fine].reshape(fine * rank2, down_ref.shape[2])
            product = lax.dot_general(
                jnp.concatenate(windows, axis=0),
                factors,
                (((1,), (1,)), ((), ())),
                preferred_element_type=F32,
            )
            at = 0
            for here, span in spans:
                which = which_ref[here, :] - adapter
                found = acc[here, :]
                for q in range(fine):
                    part = product[at : at + span, q * rank2 : (q + 1) * rank2]
                    found = found + jnp.where(which == q, part, 0.0)
                acc[here, :] = found
                at += span

    @pl.when(step == pl.num_programs(0) - 1)
    def _():
        total = acc.shape[0]
        upper, lower = acc[: total // 2, :], acc[total // 2 :, :]
        keys = jnp.concatenate([upper[:, :ADAPTER_RANK], lower[:, :ADAPTER_RANK]], axis=1)
        values = jnp.concatenate([upper[:, ADAPTER_RANK:], lower[:, ADAPTER_RANK:]], axis=1)
        mine_ref[...] = jnp.where(second, values, keys)
        other_ref[...] = jnp.where(second, keys, values)


def shrink(pieces, blocks, names, ends, plan, down, later_than=()):
    total = sum(b.shape[0] for b in blocks)
    owned, rank2, width = down.shape
    group = next(g for g in (4, 3, 2, 1) if owned % g == 0)
    fine = next(g for g in (2, 3, 1) if group % g == 0)
    line = jax.ShapeDtypeStruct((total // 2, 2 * ADAPTER_RANK), F32)
    return pl.pallas_call(
        functools.partial(shrink_kernel, pieces, group, fine),
        grid_spec=pltpu.PrefetchScalarGridSpec(
            num_scalar_prefetch=1,
            grid=(owned // group,),
            in_specs=[
                pl.BlockSpec(memory_space=pltpu.SMEM),
                pl.BlockSpec((total, 1), lambda i, p: (0, 0)),
                pl.BlockSpec(
                    (group, rank2, width),
                    lambda i, p: (jnp.minimum(p[0] // group + i, p[1] // group), 0, 0),
                ),
            ]
            + [pl.BlockSpec(b.shape, lambda i, p: (0, 0)) for b in blocks]
            + [ANYWHERE] * len(later_than),
            out_specs=[pl.BlockSpec((total // 2, rank2), lambda i, p: (0, 0))] * 2,
            scratch_shapes=[pltpu.VMEM((total, rank2), F32)],
        ),
        out_shape=[line, line],
        compiler_params=PARAMS,
        cost_estimate=COST,
        name="shrink",
    )(plan, ends, names, down, *blocks, *later_than)


def split(x, terms):
    parts = []
    for _ in range(terms - 1):
        parts.append(x.astype(BF16).astype(F32))
        x = x - parts[-1]
    return parts + [x]


def expand_kernel(groups, sizes, heard, waits, which_ref, scale_ref, up_ref, *refs):
    lines, outs = refs[:heard], refs[heard + waits :]
    total = lines[0][...]
    for line in lines[1:]:
        total = total + line[...]
    twice, begin = [], 0
    for count in groups:
        lines = total[begin : begin + count, :]
        for side in (lines[:, :ADAPTER_RANK], lines[:, ADAPTER_RANK:]):
            twice.append(jnp.concatenate([side, side], axis=1))
        begin += count
    twice = jnp.concatenate(twice, axis=0)
    which = which_ref[...]
    parity = jnp.where(lax.broadcasted_iota(I32, (1, 2 * ADAPTER_RANK), 1) >= ADAPTER_RANK, 1, 0)
    pairs = up_ref.shape[0] // (2 * ADAPTER_RANK)
    wanted = [which == 2 * p + parity for p in range(pairs)]
    delta = None
    for term in split(twice, 3):
        spread = jnp.concatenate([jnp.where(w, term, 0.0).astype(BF16) for w in wanted], axis=1)
        product = jnp.dot(spread, up_ref[...], preferred_element_type=F32)
        delta = product if delta is None else delta + product
    adapters = lax.broadcasted_iota(I32, scale_ref.shape, 1)
    gain = jnp.sum(jnp.where(which == adapters, scale_ref[...], 0.0), axis=1, keepdims=True)
    delta = delta * gain
    begin = 0
    for size, out in zip(sizes, outs):
        piece = delta[begin : begin + size, :]
        if out.dtype == F32:
            out[...] = piece
        else:
            code_rows(piece, out)
        begin += size


def code_rows(x, out_ref):
    rows, columns = x.shape
    largest = jnp.maximum(jnp.max(jnp.abs(x), axis=1, keepdims=True), 2.0**-105)
    power = jnp.floor(jnp.log2(largest)) - 14.0
    power = power + jnp.where(largest * power_of_two(-power) > 32767.0, 1.0, 0.0)
    coded = jnp.round(x * power_of_two(-power))
    coded = jnp.minimum(jnp.maximum(coded, -32767.0), 32767.0)
    out_ref[:rows, :] = coded.astype(I32).astype(jnp.int16)
    down = lax.broadcasted_iota(I32, (rows, columns), 0)
    across = lax.broadcasted_iota(I32, (rows, columns), 1)
    line = jnp.sum(jnp.where(down == across, power, 0.0), axis=0, keepdims=True)
    line = jnp.broadcast_to(line, (16, columns)).astype(I32)
    out_ref[rows:, :] = line.astype(jnp.int16)


def power_of_two(power):
    return jnp.exp2(power).astype(BF16).astype(F32)


def expand(lines, groups, names, scale, up, sizes, kept=0, later_than=()):
    columns = up.shape[1]
    shapes = [
        jax.ShapeDtypeStruct((s, columns), F32)
        if i < kept
        else jax.ShapeDtypeStruct((s + 16, columns), jnp.int16)
        for i, s in enumerate(sizes)
    ]
    return pl.pallas_call(
        functools.partial(expand_kernel, groups, sizes, len(lines), len(later_than)),
        in_specs=[pl.BlockSpec(memory_space=pltpu.VMEM)] * (3 + len(lines))
        + [ANYWHERE] * len(later_than),
        out_shape=shapes,
        compiler_params=PARAMS,
        cost_estimate=COST,
        name="expand",
    )(names, scale, up, *lines, *later_than)


def place_kernel(begin, target_ref, rows_ref, out_ref):
    at = begin + lax.broadcasted_iota(I32, (1, rows_ref.shape[0]), 1)
    place = jnp.where(target_ref[...] == at, 1.0, 0.0).astype(BF16)
    total = None
    for term in split(rows_ref[...], 3):
        moved = jnp.dot(place, term.astype(BF16), preferred_element_type=F32)
        total = moved if total is None else total + moved
    out_ref[...] = total


def place_rows(target, begin, rows):
    return pl.pallas_call(
        functools.partial(place_kernel, begin),
        out_shape=jax.ShapeDtypeStruct((target.shape[0], rows.shape[1]), F32),
        compiler_params=PARAMS,
        cost_estimate=COST,
        name="place",
    )(target, rows)


def merge_kernel(begins, parts, target_ref, *refs):
    blocks, out_ref = refs[parts:-1], refs[-1]
    spots, powers, highs, lows = [], [], [], []
    for begin, block in zip(begins, blocks):
        count = block.shape[0] - 16
        spots.append(begin + lax.broadcasted_iota(I32, (1, count), 1))
        powers.append(block[count:, :].astype(I32)[:1, :count])
        coded = block[:count, :].astype(I32)
        high = (coded + 128) >> 8
        highs.append(high.astype(F32).astype(BF16))
        lows.append((coded - high * 256).astype(F32).astype(BF16))
    spot, power = jnp.concatenate(spots, axis=1), jnp.concatenate(powers, axis=1)
    place = jnp.where(target_ref[...] == spot, jnp.exp2(power.astype(F32)), 0.0).astype(BF16)
    total = jnp.dot(place, jnp.concatenate(highs, axis=0), preferred_element_type=F32) * 256.0
    total = total + jnp.dot(place, jnp.concatenate(lows, axis=0), preferred_element_type=F32)
    for part in refs[:parts]:
        total = total + part[...]
    out_ref[...] = total.astype(out_ref.dtype)


def merge(parts, target, begins, blocks, kind):
    return pl.pallas_call(
        functools.partial(merge_kernel, tuple(begins), len(parts)),
        out_shape=jax.ShapeDtypeStruct(parts[0].shape, kind),
        compiler_params=PARAMS,
        cost_estimate=COST,
        name="merge",
    )(target, *parts, *blocks)


def swap(x, axes, size, distance):
    return lax.ppermute(x, axes, [(i, i ^ distance) for i in range(size)])


def local(
    tokens,
    key_value_weight,
    adapter_down_weight,
    adapter_up_weight,
    adapter_scale,
    token_adapter_index,
):
    feature_axes = ("tensor", "sub")
    rows = tokens.shape[0]
    owned = adapter_down_weight.shape[0]
    owners = lax.axis_size("dp")
    sharers = lax.axis_size(feature_axes)
    me = lax.axis_index("dp")
    half = (lax.axis_index(feature_axes) >= sharers // 2).astype(I32)
    cap = up_to_16(owned * TOKEN_LIMIT)

    own, near = (0, 0, cap), (1, 0, cap)
    if owners == 4:
        usual = up_to_16(cap * 5 // 6)
        near = (1, 0, usual)
        first = up_to_16(usual * 3 // 5)
        far, last = [(3, 0, usual)], [[(2, 0, first)], [(2, first, usual - first)]]
        extra = [(j, usual, cap - usual) for j in (3, 2, 1)]
    else:
        usual, far, last, extra = cap, [], [[(j, 0, cap) for j in range(2, owners)]], []

    ids_row = token_adapter_index.reshape(1, rows)
    ids_heard = [ids_row] + [swap(ids_row, "dp", owners, j) for j in range(1, owners)]
    slot, target = route(ids_row, me.reshape(1), owners, owned, cap)
    packed = dict(zip([near], sort_rows(tokens, slot, cap, [near], tuple(ids_heard[1:]))))
    base_part, base_done = base_product(tokens, key_value_weight, packed[near])
    base = lax.psum_scatter(base_part, feature_axes, scatter_dimension=1, tiled=True)
    received = {near: swap(packed[near], "dp", owners, near[0])}
    if far:
        packed |= zip(far, sort_rows(tokens, slot, cap, far, (base_done,)))
        received |= {p: swap(packed[p], "dp", owners, p[0]) for p in far}
    packed |= zip([own] + extra, sort_rows(tokens, slot, cap, [own] + extra, (packed[(far or [near])[0]],)))
    gated = [p for pieces in last for p in pieces]

    early = [own, near] + far
    sets = [[p] for p in early] + [early] + last + ([extra] if extra else [])
    here = jnp.stack([me.astype(I32), half])
    names, ends, plans, largest = name_rows(ids_heard, here, owned, sets)

    if owned % 2:
        adapter_up_weight = jnp.pad(adapter_up_weight, ((0, 1), (0, 0), (0, 0)))
    up = adapter_up_weight.reshape(-1, adapter_up_weight.shape[2])
    scale = adapter_scale.reshape(1, owned)

    def exchange(mine, other, steps=2):
        if sharers == 4 and steps == 2:
            mine = mine + swap(other, "tensor", 2, 1)
            return [mine, swap(mine, "sub", 2, 1)]
        return [mine] + [
            swap(mine if d < sharers // 2 else other, feature_axes, sharers, d)
            for d in range(1, sharers)
        ]

    def deltas_of(pieces, blocks, names, ends, plan, down, up, scale, later_than, sooner=()):
        mine, other = shrink(pieces, blocks, names, ends, plan, down, later_than)
        sizes = tuple(b.shape[0] for b in blocks)
        lines = exchange(mine, other)
        groups = (mine.shape[0],)
        return expand(lines, groups, names, scale, up, sizes, later_than=sooner)

    def send_back(pieces, deltas):
        return [swap(d, "dp", owners, p[0]) for p, d in zip(pieces, deltas)]

    def begins(pieces):
        return [b * cap + f for b, f, _ in pieces]

    weights = (adapter_down_weight, up, scale)
    packed |= zip([own] + extra, sort_rows(tokens, slot, cap, [own] + extra, (packed[(far or [near])[0]],)))
    for d in range(1, lax.axis_size("parts")):
        largest = jnp.maximum(largest, swap(largest, "parts", lax.axis_size("parts"), d))
    down = adapter_down_weight
    shares = [shrink([own], [packed[own]], names[0], ends, plans[0], down)]
    packed |= zip(gated, sort_rows(tokens, slot, cap, gated, (shares[0][0],)))
    received |= {p: swap(packed[p], "dp", owners, p[0]) for p in gated}
    waits = (packed[gated[0]], largest)
    for k, p in enumerate(early[1:], 1):
        shares.append(shrink([p], [received[p]], names[k], ends, plans[k], down, waits))
        waits = (shares[-1][0],)
    lines = exchange(*(jnp.concatenate(pair, axis=0) for pair in zip(*shares)), steps=1)
    sizes = tuple(p[2] for p in early)
    here = len(early)
    deltas = expand(lines, tuple(c // 2 for c in sizes), names[here], scale, up, sizes, kept=1)
    parts = [base, place_rows(target, own[0] * cap, deltas[0])]
    returned = send_back(early[1:], deltas[1:])
    done = early[1:]
    for k, pieces in enumerate(last):
        blocks = [received[p] for p in pieces]
        waits = (deltas[0], parts[1])
        sooner = tuple(returned[-1:]) if k else ()
        deltas = deltas_of(
            pieces, blocks, names[here + 1 + k], ends, plans[here + 1 + k], *weights, waits, sooner
        )
        returned += send_back(pieces, deltas)
        done += pieces

    def finish(parts, target, returned, *_):
        return merge(parts, target, begins(done), returned, BF16)

    if not extra:
        return finish(parts, target, returned)

    def finish_with_extra(parts, target, returned, blocks, names, ends, plan, weights):
        blocks = send_back(extra, blocks)
        deltas = deltas_of(extra, blocks, names, ends, plan, *weights, ())
        deltas = send_back(extra, deltas)
        return merge(parts, target, begins(done + extra), returned + deltas, BF16)

    return lax.cond(
        largest[0, 0] > usual,
        finish_with_extra,
        finish,
        parts,
        target,
        returned,
        [packed[p] for p in extra],
        names[-1],
        ends,
        plans[-1],
        weights,
    )


def solution(mesh):
    return jax.shard_map(
        local,
        mesh=mesh,
        in_specs=(
            P(("parts", "dp"), ("tensor", "sub")),
            P(("tensor", "sub"), None),
            P("dp", None, ("tensor", "sub")),
            P("dp", None, ("tensor", "sub")),
            P("dp"),
            P(("parts", "dp"), None),
        ),
        out_specs=P(("parts", "dp"), ("tensor", "sub")),
        check_vma=False,
    )
```

```python
import functools

import jax
import jax.numpy as jnp
from jax import lax
from jax.experimental import pallas as pl
from jax.experimental.pallas import tpu as pltpu
from jax.sharding import PartitionSpec as P

ADAPTER_RANK = 64
TOKEN_LIMIT = 12
VMEM_LIMIT = 28 * 1024 * 1024
F32 = jnp.float32
BF16 = jnp.bfloat16
I32 = jnp.int32
ANYWHERE = pl.BlockSpec(memory_space=pl.ANY)
COST = pl.CostEstimate(flops=1, transcendentals=0, bytes_accessed=1)
HEAD = pl.CostEstimate(flops=10**9, transcendentals=0, bytes_accessed=1)
PARAMS = pltpu.CompilerParams(vmem_limit_bytes=VMEM_LIMIT)


def up_to_16(count):
    return -(-count // 16) * 16


def owner_of(ids, owners, owned):
    total = jnp.zeros_like(ids)
    for o in range(1, owners):
        total = total + jnp.where(ids >= o * owned, 1, 0)
    return total


def as_column(line):
    size = line.shape[1]
    here = lax.broadcasted_iota(I32, (size, size), 0) == lax.broadcasted_iota(I32, (size, size), 1)
    return jnp.sum(jnp.where(here, line, 0), axis=1, keepdims=True)


def route_kernel(owners, owned, cap, me_ref, row_ref, slot_ref, target_ref):
    rows = row_ref.shape[1]
    id_row = row_ref[...]
    key_row = id_row * rows + lax.broadcasted_iota(I32, (1, rows), 1)
    key_col = as_column(key_row)
    own_row = owner_of(id_row, owners, owned)
    before = (key_col < key_row) & (key_col >= own_row * (owned * rows))
    rank = jnp.sum(jnp.where(before, 1, 0), axis=0, keepdims=True)
    found = (own_row ^ me_ref[0]) * cap + rank
    slot_ref[...] = found
    target_ref[...] = as_column(found)


def route(ids_row, me, owners, owned, cap):
    rows = ids_row.shape[1]
    return pl.pallas_call(
        functools.partial(route_kernel, owners, owned, cap),
        in_specs=[
            pl.BlockSpec(memory_space=pltpu.SMEM),
            pl.BlockSpec(memory_space=pltpu.VMEM),
        ],
        out_shape=[jax.ShapeDtypeStruct((1, rows), I32), jax.ShapeDtypeStruct((rows, 1), I32)],
        compiler_params=PARAMS,
        cost_estimate=HEAD,
        name="route",
    )(me, ids_row)


def sort_kernel(cap, pieces, waits, slot_ref, tok_ref, *refs):
    outs, place = refs[waits:-1], refs[-1]

    @pl.when(pl.program_id(0) == 0)
    def _():
        begin = 0
        for block, first, count in pieces:
            at = block * cap + first + lax.broadcasted_iota(I32, (count, slot_ref.shape[1]), 0)
            found = jnp.where(at == slot_ref[...], 1.0, 0.0).astype(BF16)
            place[begin : begin + count, :] = found
            begin += count

    moved = jnp.dot(place[...], tok_ref[...], preferred_element_type=F32).astype(BF16)
    begin = 0
    for (_, _, count), out in zip(pieces, outs):
        out[...] = moved[begin : begin + count, :]
        begin += count


def sort_rows(tokens, slot, cap, pieces, later_than=()):
    rows, width = tokens.shape
    step = min(512, width)
    return pl.pallas_call(
        functools.partial(sort_kernel, cap, pieces, len(later_than)),
        grid=(width // step,),
        in_specs=[
            pl.BlockSpec((1, rows), lambda i: (0, 0)),
            pl.BlockSpec((rows, step), lambda i: (0, i)),
        ]
        + [ANYWHERE] * len(later_than),
        out_specs=[pl.BlockSpec((count, step), lambda i: (0, i)) for _, _, count in pieces],
        out_shape=[jax.ShapeDtypeStruct((count, width), BF16) for _, _, count in pieces],
        scratch_shapes=[pltpu.VMEM((sum(c for _, _, c in pieces), rows), BF16)],
        compiler_params=PARAMS,
        cost_estimate=HEAD,
        name="sort",
    )(slot, tokens, *later_than)


def name_kernel(owners, owned, sets, here_ref, *refs):
    lines, outs, (ends_ref, plan_ref, most_ref) = refs[:owners], refs[owners:-3], refs[-3:]
    me, half = here_ref[0], here_ref[1]
    held = -(-owned // 8) * 8
    owner = lax.broadcasted_iota(I32, (-(-owners // 8) * 8, 1), 0)
    adapter = lax.broadcasted_iota(I32, (held, 1), 0)
    diagonal = adapter == lax.broadcasted_iota(I32, (held, 128), 1)
    used = lax.broadcasted_iota(I32, (1, 128), 1) < owned
    most = jnp.zeros(owner.shape, I32)
    ends = []
    for j, line in enumerate(lines):
        ids = line[...]
        chosen = jnp.where(owner_of(ids, owners, owned) == owner, 1, 0)
        count = jnp.sum(chosen, axis=1, keepdims=True)
        far = (me ^ j ^ owner >= 1) & (owner < owners)
        most = jnp.maximum(most, jnp.where(far, count, 0))
        mine = ids - me * owned
        upto = jnp.sum(jnp.where((mine >= 0) & (mine <= adapter), 1, 0), axis=1, keepdims=True)
        across = jnp.sum(jnp.where(diagonal, upto, 0), axis=0, keepdims=True)
        ends.append(jnp.where(used, across, 1 << 20))
        ends_ref[j : j + 1, :] = ends[j]
    most_ref[...] = jnp.broadcast_to(jnp.max(most, axis=0, keepdims=True), most_ref.shape)
    for k, (pieces, out) in enumerate(zip(sets, outs)):
        begin, low, high = 0, owned - 1, 0
        for block, first, count in pieces:
            at = first + lax.broadcasted_iota(I32, (count, 1), 0)
            names = jnp.sum(jnp.where(ends[block] <= at, 1, 0), axis=1, keepdims=True)
            out[begin : begin + count, :] = names
            low = jnp.minimum(low, jnp.min(names))
            high = jnp.maximum(high, jnp.max(jnp.where(names < owned, names, 0)))
            begin += count
        plan_ref[3 * k] = low
        plan_ref[3 * k + 1] = jnp.maximum(low, high)
        plan_ref[3 * k + 2] = half


def name_rows(lines, here, owned, sets):
    totals = [sum(c for _, _, c in pieces) for pieces in sets]
    on_chip, scalars = (pl.BlockSpec(memory_space=m) for m in (pltpu.VMEM, pltpu.SMEM))
    *names, ends, plan, most = pl.pallas_call(
        functools.partial(name_kernel, len(lines), owned, sets),
        in_specs=[scalars] + [on_chip] * len(lines),
        out_specs=[on_chip] * len(sets) + [on_chip, scalars, on_chip],
        out_shape=[jax.ShapeDtypeStruct((t, 1), I32) for t in totals]
        + [
            jax.ShapeDtypeStruct((len(lines), 128), I32),
            jax.ShapeDtypeStruct((3 * len(sets),), I32),
            jax.ShapeDtypeStruct((1, 128), I32),
        ],
        compiler_params=PARAMS,
        cost_estimate=COST,
        name="name_rows",
    )(here, *lines)
    plans = [plan[3 * k : 3 * k + 3] for k in range(len(sets))]
    return names, ends, plans, most


def base_kernel(tok_ref, weight_ref, _, out_ref):
    out_ref[...] = jnp.dot(tok_ref[...], weight_ref[...], preferred_element_type=F32)


def base_product(tokens, weight, later_than):
    (rows, width), columns = tokens.shape, weight.shape[1]
    step = min(256, columns)
    return pl.pallas_call(
        base_kernel,
        grid=(columns // step,),
        in_specs=[
            pl.BlockSpec((rows, width), lambda i: (0, 0)),
            pl.BlockSpec((width, step), lambda i: (0, i)),
            ANYWHERE,
        ],
        out_specs=pl.BlockSpec((rows, step), lambda i: (0, i)),
        out_shape=jax.ShapeDtypeStruct((rows, columns), F32),
        compiler_params=PARAMS,
        cost_estimate=HEAD,
        name="base",
    )(tokens, weight, later_than)


def shrink_kernel(pieces, group, fine, plan_ref, ends_ref, which_ref, down_ref, *refs):
    blocks, (mine_ref, other_ref, acc) = refs[: len(pieces)], refs[-3:]
    step, rank2 = pl.program_id(0), 2 * ADAPTER_RANK
    low, high, second = plan_ref[0], plan_ref[1], plan_ref[2] == 1
    begin = (low // group + step) * group

    @pl.when(step == 0)
    def _():
        acc[...] = jnp.zeros_like(acc)

    for f in range(0, group, fine):

        @pl.when((begin + f <= high) & (begin + f + fine > low))
        def _(f=f):
            adapter = begin + f
            windows, spans, at = [], [], 0
            for (block, first, size), rows in zip(pieces, blocks):
                span = min(up_to_16(fine * TOKEN_LIMIT + 15), size)
                ahead = ends_ref[block, jnp.maximum(adapter - 1, 0)]
                start = jnp.where(adapter > 0, ahead, 0) - first
                start = jnp.minimum(jnp.maximum(start, 0), size - span) // 16 * 16
                windows.append(rows[pl.ds(pl.multiple_of(start, 16), span), :])
                spans.append((pl.ds(pl.multiple_of(at + start, 16), span), span))
                at += size
            factors = down_ref[f : f + fine].reshape(fine * rank2, down_ref.shape[2])
            product = lax.dot_general(
                jnp.concatenate(windows, axis=0),
                factors,
                (((1,), (1,)), ((), ())),
                preferred_element_type=F32,
            )
            at = 0
            for here, span in spans:
                which = which_ref[here, :] - adapter
                found = acc[here, :]
                for q in range(fine):
                    part = product[at : at + span, q * rank2 : (q + 1) * rank2]
                    found = found + jnp.where(which == q, part, 0.0)
                acc[here, :] = found
                at += span

    @pl.when(step == pl.num_programs(0) - 1)
    def _():
        total = acc.shape[0]
        upper, lower = acc[: total // 2, :], acc[total // 2 :, :]
        keys = jnp.concatenate([upper[:, :ADAPTER_RANK], lower[:, :ADAPTER_RANK]], axis=1)
        values = jnp.concatenate([upper[:, ADAPTER_RANK:], lower[:, ADAPTER_RANK:]], axis=1)
        mine_ref[...] = jnp.where(second, values, keys)
        other_ref[...] = jnp.where(second, keys, values)


def shrink(pieces, blocks, names, ends, plan, down, later_than=()):
    total = sum(b.shape[0] for b in blocks)
    owned, rank2, width = down.shape
    group = next(g for g in (4, 3, 2, 1) if owned % g == 0)
    fine = next(g for g in (2, 3, 1) if group % g == 0)
    line = jax.ShapeDtypeStruct((total // 2, 2 * ADAPTER_RANK), F32)
    return pl.pallas_call(
        functools.partial(shrink_kernel, pieces, group, fine),
        grid_spec=pltpu.PrefetchScalarGridSpec(
            num_scalar_prefetch=1,
            grid=(owned // group,),
            in_specs=[
                pl.BlockSpec(memory_space=pltpu.SMEM),
                pl.BlockSpec((total, 1), lambda i, p: (0, 0)),
                pl.BlockSpec(
                    (group, rank2, width),
                    lambda i, p: (jnp.minimum(p[0] // group + i, p[1] // group), 0, 0),
                ),
            ]
            + [pl.BlockSpec(b.shape, lambda i, p: (0, 0)) for b in blocks]
            + [ANYWHERE] * len(later_than),
            out_specs=[pl.BlockSpec((total // 2, rank2), lambda i, p: (0, 0))] * 2,
            scratch_shapes=[pltpu.VMEM((total, rank2), F32)],
        ),
        out_shape=[line, line],
        compiler_params=PARAMS,
        cost_estimate=COST,
        name="shrink",
    )(plan, ends, names, down, *blocks, *later_than)


def split(x, terms):
    parts = []
    for _ in range(terms - 1):
        parts.append(x.astype(BF16).astype(F32))
        x = x - parts[-1]
    return parts + [x]


def expand_kernel(groups, sizes, heard, waits, which_ref, scale_ref, up_ref, *refs):
    lines, outs = refs[:heard], refs[heard + waits :]
    total = lines[0][...]
    for line in lines[1:]:
        total = total + line[...]
    twice, begin = [], 0
    for count in groups:
        lines = total[begin : begin + count, :]
        for side in (lines[:, :ADAPTER_RANK], lines[:, ADAPTER_RANK:]):
            twice.append(jnp.concatenate([side, side], axis=1))
        begin += count
    twice = jnp.concatenate(twice, axis=0)
    which = which_ref[...]
    parity = jnp.where(lax.broadcasted_iota(I32, (1, 2 * ADAPTER_RANK), 1) >= ADAPTER_RANK, 1, 0)
    pairs = up_ref.shape[0] // (2 * ADAPTER_RANK)
    wanted = [which == 2 * p + parity for p in range(pairs)]
    delta = None
    for term in split(twice, 3):
        spread = jnp.concatenate([jnp.where(w, term, 0.0).astype(BF16) for w in wanted], axis=1)
        product = jnp.dot(spread, up_ref[...], preferred_element_type=F32)
        delta = product if delta is None else delta + product
    adapters = lax.broadcasted_iota(I32, scale_ref.shape, 1)
    gain = jnp.sum(jnp.where(which == adapters, scale_ref[...], 0.0), axis=1, keepdims=True)
    delta = delta * gain
    begin = 0
    for size, out in zip(sizes, outs):
        piece = delta[begin : begin + size, :]
        if out.dtype == F32:
            out[...] = piece
        else:
            code_rows(piece, out)
        begin += size


def code_rows(x, out_ref):
    rows, columns = x.shape
    largest = jnp.maximum(jnp.max(jnp.abs(x), axis=1, keepdims=True), 2.0**-105)
    power = jnp.floor(jnp.log2(largest)) - 14.0
    power = power + jnp.where(largest * power_of_two(-power) > 32767.0, 1.0, 0.0)
    coded = jnp.round(x * power_of_two(-power))
    coded = jnp.minimum(jnp.maximum(coded, -32767.0), 32767.0)
    out_ref[:rows, :] = coded.astype(I32).astype(jnp.int16)
    down = lax.broadcasted_iota(I32, (rows, columns), 0)
    across = lax.broadcasted_iota(I32, (rows, columns), 1)
    line = jnp.sum(jnp.where(down == across, power, 0.0), axis=0, keepdims=True)
    line = jnp.broadcast_to(line, (16, columns)).astype(I32)
    out_ref[rows:, :] = line.astype(jnp.int16)


def power_of_two(power):
    return jnp.exp2(power).astype(BF16).astype(F32)


def expand(lines, groups, names, scale, up, sizes, kept=0, later_than=()):
    columns = up.shape[1]
    shapes = [
        jax.ShapeDtypeStruct((s, columns), F32)
        if i < kept
        else jax.ShapeDtypeStruct((s + 16, columns), jnp.int16)
        for i, s in enumerate(sizes)
    ]
    return pl.pallas_call(
        functools.partial(expand_kernel, groups, sizes, len(lines), len(later_than)),
        in_specs=[pl.BlockSpec(memory_space=pltpu.VMEM)] * (3 + len(lines))
        + [ANYWHERE] * len(later_than),
        out_shape=shapes,
        compiler_params=PARAMS,
        cost_estimate=COST,
        name="expand",
    )(names, scale, up, *lines, *later_than)


def place_kernel(begin, target_ref, rows_ref, out_ref):
    at = begin + lax.broadcasted_iota(I32, (1, rows_ref.shape[0]), 1)
    place = jnp.where(target_ref[...] == at, 1.0, 0.0).astype(BF16)
    total = None
    for term in split(rows_ref[...], 3):
        moved = jnp.dot(place, term.astype(BF16), preferred_element_type=F32)
        total = moved if total is None else total + moved
    out_ref[...] = total


def place_rows(target, begin, rows):
    return pl.pallas_call(
        functools.partial(place_kernel, begin),
        out_shape=jax.ShapeDtypeStruct((target.shape[0], rows.shape[1]), F32),
        compiler_params=PARAMS,
        cost_estimate=COST,
        name="place",
    )(target, rows)


def merge_kernel(begins, parts, target_ref, *refs):
    blocks, out_ref = refs[parts:-1], refs[-1]
    spots, powers, highs, lows = [], [], [], []
    for begin, block in zip(begins, blocks):
        count = block.shape[0] - 16
        spots.append(begin + lax.broadcasted_iota(I32, (1, count), 1))
        powers.append(block[count:, :].astype(I32)[:1, :count])
        coded = block[:count, :].astype(I32)
        high = (coded + 128) >> 8
        highs.append(high.astype(F32).astype(BF16))
        lows.append((coded - high * 256).astype(F32).astype(BF16))
    spot, power = jnp.concatenate(spots, axis=1), jnp.concatenate(powers, axis=1)
    place = jnp.where(target_ref[...] == spot, jnp.exp2(power.astype(F32)), 0.0).astype(BF16)
    total = jnp.dot(place, jnp.concatenate(highs, axis=0), preferred_element_type=F32) * 256.0
    total = total + jnp.dot(place, jnp.concatenate(lows, axis=0), preferred_element_type=F32)
    for part in refs[:parts]:
        total = total + part[...]
    out_ref[...] = total.astype(out_ref.dtype)


def merge(parts, target, begins, blocks, kind):
    return pl.pallas_call(
        functools.partial(merge_kernel, tuple(begins), len(parts)),
        out_shape=jax.ShapeDtypeStruct(parts[0].shape, kind),
        compiler_params=PARAMS,
        cost_estimate=COST,
        name="merge",
    )(target, *parts, *blocks)


def swap(x, axes, size, distance):
    return lax.ppermute(x, axes, [(i, i ^ distance) for i in range(size)])


def local(
    tokens,
    key_value_weight,
    adapter_down_weight,
    adapter_up_weight,
    adapter_scale,
    token_adapter_index,
):
    feature_axes = ("tensor", "sub")
    rows = tokens.shape[0]
    owned = adapter_down_weight.shape[0]
    owners = lax.axis_size("dp")
    sharers = lax.axis_size(feature_axes)
    me = lax.axis_index("dp")
    half = (lax.axis_index(feature_axes) >= sharers // 2).astype(I32)
    cap = up_to_16(owned * TOKEN_LIMIT)

    own, near = (0, 0, cap), (1, 0, cap)
    if owners == 4:
        usual = up_to_16(cap * 5 // 6)
        near = (1, 0, usual)
        first = up_to_16(usual * 3 // 5)
        far, last = [(3, 0, usual)], [[(2, 0, first)], [(2, first, usual - first)]]
        extra = [(j, usual, cap - usual) for j in (3, 2, 1)]
    else:
        usual, far, last, extra = cap, [], [[(j, 0, cap) for j in range(2, owners)]], []

    ids_row = token_adapter_index.reshape(1, rows)
    ids_heard = [ids_row] + [swap(ids_row, "dp", owners, j) for j in range(1, owners)]
    slot, target = route(ids_row, me.reshape(1), owners, owned, cap)
    sent = far + [near]
    packed = dict(zip(sent, sort_rows(tokens, slot, cap, sent, tuple(ids_heard[1:]))))
    received = {p: swap(packed[p], "dp", owners, p[0]) for p in sent}
    base_part = base_product(tokens, key_value_weight, packed[near])
    base = lax.psum_scatter(base_part, feature_axes, scatter_dimension=1, tiled=True)
    packed |= zip([own] + extra, sort_rows(tokens, slot, cap, [own] + extra, (base_part,)))
    gated = [p for pieces in last for p in pieces]
    packed |= zip(gated, sort_rows(tokens, slot, cap, gated, (received[near],)))
    received |= {p: swap(packed[p], "dp", owners, p[0]) for p in gated}

    early = [own, near] + far
    sets = [[p] for p in early] + [early] + last + ([extra] if extra else [])
    here = jnp.stack([me.astype(I32), half])
    names, ends, plans, largest = name_rows(ids_heard, here, owned, sets)

    if owned % 2:
        adapter_up_weight = jnp.pad(adapter_up_weight, ((0, 1), (0, 0), (0, 0)))
    up = adapter_up_weight.reshape(-1, adapter_up_weight.shape[2])
    scale = adapter_scale.reshape(1, owned)

    def exchange(mine, other, steps=2):
        if sharers == 4 and steps == 2:
            mine = mine + swap(other, "tensor", 2, 1)
            return [mine, swap(mine, "sub", 2, 1)]
        return [mine] + [
            swap(mine if d < sharers // 2 else other, feature_axes, sharers, d)
            for d in range(1, sharers)
        ]

    def deltas_of(pieces, blocks, names, ends, plan, down, up, scale, later_than):
        mine, other = shrink(pieces, blocks, names, ends, plan, down, later_than)
        sizes = tuple(b.shape[0] for b in blocks)
        lines = exchange(mine, other)
        return expand(lines, (mine.shape[0],), names, scale, up, sizes)

    def send_back(pieces, deltas):
        return [swap(d, "dp", owners, p[0]) for p, d in zip(pieces, deltas)]

    def begins(pieces):
        return [b * cap + f for b, f, _ in pieces]

    weights = (adapter_down_weight, up, scale)
    packed |= zip([own] + extra, sort_rows(tokens, slot, cap, [own] + extra, (base_part,)))
    for d in range(1, lax.axis_size("parts")):
        largest = jnp.maximum(largest, swap(largest, "parts", lax.axis_size("parts"), d))
    shares, waits = [], ()
    for k, p in enumerate(early):
        rows_here = received.get(p, packed[p])
        shares.append(
            shrink([p], [rows_here], names[k], ends, plans[k], adapter_down_weight, waits)
        )
        waits = (shares[-1][0], packed[gated[0]])
    lines = exchange(*(jnp.concatenate(pair, axis=0) for pair in zip(*shares)), steps=1)
    sizes = tuple(p[2] for p in early)
    here = len(early)
    deltas = expand(lines, tuple(c // 2 for c in sizes), names[here], scale, up, sizes, kept=1)
    parts = [base, place_rows(target, own[0] * cap, deltas[0])]
    returned = send_back(early[1:], deltas[1:])
    done = early[1:]
    for k, pieces in enumerate(last):
        blocks = [received[p] for p in pieces]
        waits = (deltas[0], parts[1], largest)
        deltas = deltas_of(
            pieces, blocks, names[here + 1 + k], ends, plans[here + 1 + k], *weights, waits
        )
        returned += send_back(pieces, deltas)
        done += pieces

    def finish(parts, target, returned, *_):
        return merge(parts, target, begins(done), returned, BF16)

    if not extra:
        return finish(parts, target, returned)

    def finish_with_extra(parts, target, returned, blocks, names, ends, plan, weights):
        blocks = send_back(extra, blocks)
        deltas = deltas_of(extra, blocks, names, ends, plan, *weights, ())
        deltas = send_back(extra, deltas)
        return merge(parts, target, begins(done + extra), returned + deltas, BF16)

    return lax.cond(
        largest[0, 0] > usual,
        finish_with_extra,
        finish,
        parts,
        target,
        returned,
        [packed[p] for p in extra],
        names[-1],
        ends,
        plans[-1],
        weights,
    )


def solution(mesh):
    return jax.shard_map(
        local,
        mesh=mesh,
        in_specs=(
            P(("parts", "dp"), ("tensor", "sub")),
            P(("tensor", "sub"), None),
            P("dp", None, ("tensor", "sub")),
            P("dp", None, ("tensor", "sub")),
            P("dp"),
            P(("parts", "dp"), None),
        ),
        out_specs=P(("parts", "dp"), ("tensor", "sub")),
        check_vma=False,
    )
```

```python
import functools

import jax
import jax.numpy as jnp
from jax import lax
from jax.experimental import pallas as pl
from jax.experimental.pallas import tpu as pltpu
from jax.sharding import PartitionSpec as P

ADAPTER_RANK = 64
TOKEN_LIMIT = 12
VMEM_LIMIT = 28 * 1024 * 1024
F32 = jnp.float32
BF16 = jnp.bfloat16
I32 = jnp.int32
ANYWHERE = pl.BlockSpec(memory_space=pl.ANY)
COST = pl.CostEstimate(flops=1, transcendentals=0, bytes_accessed=1)
HEAD = pl.CostEstimate(flops=10**9, transcendentals=0, bytes_accessed=1)
PARAMS = pltpu.CompilerParams(vmem_limit_bytes=VMEM_LIMIT)


def up_to_16(count):
    return -(-count // 16) * 16


def owner_of(ids, owners, owned):
    total = jnp.zeros_like(ids)
    for o in range(1, owners):
        total = total + jnp.where(ids >= o * owned, 1, 0)
    return total


def as_column(line):
    size = line.shape[1]
    here = lax.broadcasted_iota(I32, (size, size), 0) == lax.broadcasted_iota(I32, (size, size), 1)
    return jnp.sum(jnp.where(here, line, 0), axis=1, keepdims=True)


def route_kernel(owners, owned, cap, me_ref, row_ref, slot_ref, target_ref):
    rows = row_ref.shape[1]
    id_row = row_ref[...]
    key_row = id_row * rows + lax.broadcasted_iota(I32, (1, rows), 1)
    key_col = as_column(key_row)
    own_row = owner_of(id_row, owners, owned)
    before = (key_col < key_row) & (key_col >= own_row * (owned * rows))
    rank = jnp.sum(jnp.where(before, 1, 0), axis=0, keepdims=True)
    found = (own_row ^ me_ref[0]) * cap + rank
    slot_ref[...] = found
    target_ref[...] = as_column(found)


def route(ids_row, me, owners, owned, cap):
    rows = ids_row.shape[1]
    return pl.pallas_call(
        functools.partial(route_kernel, owners, owned, cap),
        in_specs=[
            pl.BlockSpec(memory_space=pltpu.SMEM),
            pl.BlockSpec(memory_space=pltpu.VMEM),
        ],
        out_shape=[jax.ShapeDtypeStruct((1, rows), I32), jax.ShapeDtypeStruct((rows, 1), I32)],
        compiler_params=PARAMS,
        cost_estimate=HEAD,
        name="route",
    )(me, ids_row)


def sort_kernel(cap, pieces, waits, slot_ref, tok_ref, *refs):
    outs, place = refs[waits:-1], refs[-1]

    @pl.when(pl.program_id(0) == 0)
    def _():
        begin = 0
        for block, first, count in pieces:
            at = block * cap + first + lax.broadcasted_iota(I32, (count, slot_ref.shape[1]), 0)
            found = jnp.where(at == slot_ref[...], 1.0, 0.0).astype(BF16)
            place[begin : begin + count, :] = found
            begin += count

    moved = jnp.dot(place[...], tok_ref[...], preferred_element_type=F32).astype(BF16)
    begin = 0
    for (_, _, count), out in zip(pieces, outs):
        out[...] = moved[begin : begin + count, :]
        begin += count


def sort_rows(tokens, slot, cap, pieces, later_than=()):
    rows, width = tokens.shape
    step = min(512, width)
    return pl.pallas_call(
        functools.partial(sort_kernel, cap, pieces, len(later_than)),
        grid=(width // step,),
        in_specs=[
            pl.BlockSpec((1, rows), lambda i: (0, 0)),
            pl.BlockSpec((rows, step), lambda i: (0, i)),
        ]
        + [ANYWHERE] * len(later_than),
        out_specs=[pl.BlockSpec((count, step), lambda i: (0, i)) for _, _, count in pieces],
        out_shape=[jax.ShapeDtypeStruct((count, width), BF16) for _, _, count in pieces],
        scratch_shapes=[pltpu.VMEM((sum(c for _, _, c in pieces), rows), BF16)],
        compiler_params=PARAMS,
        cost_estimate=HEAD,
        name="sort",
    )(slot, tokens, *later_than)


def name_kernel(owners, owned, sets, here_ref, *refs):
    lines, outs, (ends_ref, plan_ref, most_ref) = refs[:owners], refs[owners:-3], refs[-3:]
    me, half = here_ref[0], here_ref[1]
    held = -(-owned // 8) * 8
    owner = lax.broadcasted_iota(I32, (-(-owners // 8) * 8, 1), 0)
    adapter = lax.broadcasted_iota(I32, (held, 1), 0)
    diagonal = adapter == lax.broadcasted_iota(I32, (held, 128), 1)
    used = lax.broadcasted_iota(I32, (1, 128), 1) < owned
    most = jnp.zeros(owner.shape, I32)
    ends = []
    for j, line in enumerate(lines):
        ids = line[...]
        chosen = jnp.where(owner_of(ids, owners, owned) == owner, 1, 0)
        count = jnp.sum(chosen, axis=1, keepdims=True)
        far = (me ^ j ^ owner >= 1) & (owner < owners)
        most = jnp.maximum(most, jnp.where(far, count, 0))
        mine = ids - me * owned
        upto = jnp.sum(jnp.where((mine >= 0) & (mine <= adapter), 1, 0), axis=1, keepdims=True)
        across = jnp.sum(jnp.where(diagonal, upto, 0), axis=0, keepdims=True)
        ends.append(jnp.where(used, across, 1 << 20))
        ends_ref[j : j + 1, :] = ends[j]
    most_ref[...] = jnp.broadcast_to(jnp.max(most, axis=0, keepdims=True), most_ref.shape)
    for k, (pieces, out) in enumerate(zip(sets, outs)):
        begin, low, high = 0, owned - 1, 0
        for block, first, count in pieces:
            at = first + lax.broadcasted_iota(I32, (count, 1), 0)
            names = jnp.sum(jnp.where(ends[block] <= at, 1, 0), axis=1, keepdims=True)
            out[begin : begin + count, :] = names
            low = jnp.minimum(low, jnp.min(names))
            high = jnp.maximum(high, jnp.max(jnp.where(names < owned, names, 0)))
            begin += count
        plan_ref[3 * k] = low
        plan_ref[3 * k + 1] = jnp.maximum(low, high)
        plan_ref[3 * k + 2] = half


def name_rows(lines, here, owned, sets):
    totals = [sum(c for _, _, c in pieces) for pieces in sets]
    on_chip, scalars = (pl.BlockSpec(memory_space=m) for m in (pltpu.VMEM, pltpu.SMEM))
    *names, ends, plan, most = pl.pallas_call(
        functools.partial(name_kernel, len(lines), owned, sets),
        in_specs=[scalars] + [on_chip] * len(lines),
        out_specs=[on_chip] * len(sets) + [on_chip, scalars, on_chip],
        out_shape=[jax.ShapeDtypeStruct((t, 1), I32) for t in totals]
        + [
            jax.ShapeDtypeStruct((len(lines), 128), I32),
            jax.ShapeDtypeStruct((3 * len(sets),), I32),
            jax.ShapeDtypeStruct((1, 128), I32),
        ],
        compiler_params=PARAMS,
        cost_estimate=COST,
        name="name_rows",
    )(here, *lines)
    plans = [plan[3 * k : 3 * k + 3] for k in range(len(sets))]
    return names, ends, plans, most


def base_kernel(tok_ref, weight_ref, _, out_ref):
    out_ref[...] = jnp.dot(tok_ref[...], weight_ref[...], preferred_element_type=F32)


def base_product(tokens, weight, later_than):
    (rows, width), columns = tokens.shape, weight.shape[1]
    step = min(256, columns)
    return pl.pallas_call(
        base_kernel,
        grid=(columns // step,),
        in_specs=[
            pl.BlockSpec((rows, width), lambda i: (0, 0)),
            pl.BlockSpec((width, step), lambda i: (0, i)),
            ANYWHERE,
        ],
        out_specs=pl.BlockSpec((rows, step), lambda i: (0, i)),
        out_shape=jax.ShapeDtypeStruct((rows, columns), F32),
        compiler_params=PARAMS,
        cost_estimate=HEAD,
        name="base",
    )(tokens, weight, later_than)


def shrink_kernel(pieces, group, fine, plan_ref, ends_ref, which_ref, down_ref, *refs):
    blocks, (mine_ref, other_ref, acc) = refs[: len(pieces)], refs[-3:]
    step, rank2 = pl.program_id(0), 2 * ADAPTER_RANK
    low, high, second = plan_ref[0], plan_ref[1], plan_ref[2] == 1
    begin = (low // group + step) * group

    @pl.when(step == 0)
    def _():
        acc[...] = jnp.zeros_like(acc)

    for f in range(0, group, fine):

        @pl.when((begin + f <= high) & (begin + f + fine > low))
        def _(f=f):
            adapter = begin + f
            windows, spans, at = [], [], 0
            for (block, first, size), rows in zip(pieces, blocks):
                span = min(up_to_16(fine * TOKEN_LIMIT + 15), size)
                ahead = ends_ref[block, jnp.maximum(adapter - 1, 0)]
                start = jnp.where(adapter > 0, ahead, 0) - first
                start = jnp.minimum(jnp.maximum(start, 0), size - span) // 16 * 16
                windows.append(rows[pl.ds(pl.multiple_of(start, 16), span), :])
                spans.append((pl.ds(pl.multiple_of(at + start, 16), span), span))
                at += size
            factors = down_ref[f : f + fine].reshape(fine * rank2, down_ref.shape[2])
            product = lax.dot_general(
                jnp.concatenate(windows, axis=0),
                factors,
                (((1,), (1,)), ((), ())),
                preferred_element_type=F32,
            )
            at = 0
            for here, span in spans:
                which = which_ref[here, :] - adapter
                found = acc[here, :]
                for q in range(fine):
                    part = product[at : at + span, q * rank2 : (q + 1) * rank2]
                    found = found + jnp.where(which == q, part, 0.0)
                acc[here, :] = found
                at += span

    @pl.when(step == pl.num_programs(0) - 1)
    def _():
        total = acc.shape[0]
        upper, lower = acc[: total // 2, :], acc[total // 2 :, :]
        keys = jnp.concatenate([upper[:, :ADAPTER_RANK], lower[:, :ADAPTER_RANK]], axis=1)
        values = jnp.concatenate([upper[:, ADAPTER_RANK:], lower[:, ADAPTER_RANK:]], axis=1)
        mine_ref[...] = jnp.where(second, values, keys)
        other_ref[...] = jnp.where(second, keys, values)


def shrink(pieces, blocks, names, ends, plan, down, later_than=()):
    total = sum(b.shape[0] for b in blocks)
    owned, rank2, width = down.shape
    group = next(g for g in (4, 3, 2, 1) if owned % g == 0)
    fine = next(g for g in (2, 3, 1) if group % g == 0)
    line = jax.ShapeDtypeStruct((total // 2, 2 * ADAPTER_RANK), F32)
    return pl.pallas_call(
        functools.partial(shrink_kernel, pieces, group, fine),
        grid_spec=pltpu.PrefetchScalarGridSpec(
            num_scalar_prefetch=1,
            grid=(owned // group,),
            in_specs=[
                pl.BlockSpec(memory_space=pltpu.SMEM),
                pl.BlockSpec((total, 1), lambda i, p: (0, 0)),
                pl.BlockSpec(
                    (group, rank2, width),
                    lambda i, p: (jnp.minimum(p[0] // group + i, p[1] // group), 0, 0),
                ),
            ]
            + [pl.BlockSpec(b.shape, lambda i, p: (0, 0)) for b in blocks]
            + [ANYWHERE] * len(later_than),
            out_specs=[pl.BlockSpec((total // 2, rank2), lambda i, p: (0, 0))] * 2,
            scratch_shapes=[pltpu.VMEM((total, rank2), F32)],
        ),
        out_shape=[line, line],
        compiler_params=PARAMS,
        cost_estimate=COST,
        name="shrink",
    )(plan, ends, names, down, *blocks, *later_than)


def split(x, terms):
    parts = []
    for _ in range(terms - 1):
        parts.append(x.astype(BF16).astype(F32))
        x = x - parts[-1]
    return parts + [x]


def expand_kernel(groups, sizes, heard, waits, which_ref, scale_ref, up_ref, *refs):
    lines, outs = refs[:heard], refs[heard + waits :]
    total = lines[0][...]
    for line in lines[1:]:
        total = total + line[...]
    twice, begin = [], 0
    for count in groups:
        lines = total[begin : begin + count, :]
        for side in (lines[:, :ADAPTER_RANK], lines[:, ADAPTER_RANK:]):
            twice.append(jnp.concatenate([side, side], axis=1))
        begin += count
    twice = jnp.concatenate(twice, axis=0)
    which = which_ref[...]
    parity = jnp.where(lax.broadcasted_iota(I32, (1, 2 * ADAPTER_RANK), 1) >= ADAPTER_RANK, 1, 0)
    pairs = up_ref.shape[0] // (2 * ADAPTER_RANK)
    wanted = [which == 2 * p + parity for p in range(pairs)]
    delta = None
    for term in split(twice, 3):
        spread = jnp.concatenate([jnp.where(w, term, 0.0).astype(BF16) for w in wanted], axis=1)
        product = jnp.dot(spread, up_ref[...], preferred_element_type=F32)
        delta = product if delta is None else delta + product
    adapters = lax.broadcasted_iota(I32, scale_ref.shape, 1)
    gain = jnp.sum(jnp.where(which == adapters, scale_ref[...], 0.0), axis=1, keepdims=True)
    delta = delta * gain
    begin = 0
    for size, out in zip(sizes, outs):
        piece = delta[begin : begin + size, :]
        if out.dtype == F32:
            out[...] = piece
        else:
            code_rows(piece, out)
        begin += size


def code_rows(x, out_ref):
    rows, columns = x.shape
    largest = jnp.maximum(jnp.max(jnp.abs(x), axis=1, keepdims=True), 2.0**-105)
    power = jnp.floor(jnp.log2(largest)) - 14.0
    power = power + jnp.where(largest * power_of_two(-power) > 32767.0, 1.0, 0.0)
    coded = jnp.round(x * power_of_two(-power))
    coded = jnp.minimum(jnp.maximum(coded, -32767.0), 32767.0)
    out_ref[:rows, :] = coded.astype(I32).astype(jnp.int16)
    down = lax.broadcasted_iota(I32, (rows, columns), 0)
    across = lax.broadcasted_iota(I32, (rows, columns), 1)
    line = jnp.sum(jnp.where(down == across, power, 0.0), axis=0, keepdims=True)
    line = jnp.broadcast_to(line, (16, columns)).astype(I32)
    out_ref[rows:, :] = line.astype(jnp.int16)


def power_of_two(power):
    return jnp.exp2(power).astype(BF16).astype(F32)


def expand(lines, groups, names, scale, up, sizes, kept=0, later_than=()):
    columns = up.shape[1]
    shapes = [
        jax.ShapeDtypeStruct((s, columns), F32)
        if i < kept
        else jax.ShapeDtypeStruct((s + 16, columns), jnp.int16)
        for i, s in enumerate(sizes)
    ]
    return pl.pallas_call(
        functools.partial(expand_kernel, groups, sizes, len(lines), len(later_than)),
        in_specs=[pl.BlockSpec(memory_space=pltpu.VMEM)] * (3 + len(lines))
        + [ANYWHERE] * len(later_than),
        out_shape=shapes,
        compiler_params=PARAMS,
        cost_estimate=COST,
        name="expand",
    )(names, scale, up, *lines, *later_than)


def place_kernel(begin, target_ref, rows_ref, out_ref):
    at = begin + lax.broadcasted_iota(I32, (1, rows_ref.shape[0]), 1)
    place = jnp.where(target_ref[...] == at, 1.0, 0.0).astype(BF16)
    total = None
    for term in split(rows_ref[...], 3):
        moved = jnp.dot(place, term.astype(BF16), preferred_element_type=F32)
        total = moved if total is None else total + moved
    out_ref[...] = total


def place_rows(target, begin, rows):
    return pl.pallas_call(
        functools.partial(place_kernel, begin),
        out_shape=jax.ShapeDtypeStruct((target.shape[0], rows.shape[1]), F32),
        compiler_params=PARAMS,
        cost_estimate=COST,
        name="place",
    )(target, rows)


def merge_kernel(begins, parts, target_ref, *refs):
    blocks, out_ref = refs[parts:-1], refs[-1]
    spots, powers, highs, lows = [], [], [], []
    for begin, block in zip(begins, blocks):
        count = block.shape[0] - 16
        spots.append(begin + lax.broadcasted_iota(I32, (1, count), 1))
        powers.append(block[count:, :].astype(I32)[:1, :count])
        coded = block[:count, :].astype(I32)
        high = (coded + 128) >> 8
        highs.append(high.astype(F32).astype(BF16))
        lows.append((coded - high * 256).astype(F32).astype(BF16))
    spot, power = jnp.concatenate(spots, axis=1), jnp.concatenate(powers, axis=1)
    place = jnp.where(target_ref[...] == spot, jnp.exp2(power.astype(F32)), 0.0).astype(BF16)
    total = jnp.dot(place, jnp.concatenate(highs, axis=0), preferred_element_type=F32) * 256.0
    total = total + jnp.dot(place, jnp.concatenate(lows, axis=0), preferred_element_type=F32)
    for part in refs[:parts]:
        total = total + part[...]
    out_ref[...] = total.astype(out_ref.dtype)


def merge(parts, target, begins, blocks, kind):
    return pl.pallas_call(
        functools.partial(merge_kernel, tuple(begins), len(parts)),
        out_shape=jax.ShapeDtypeStruct(parts[0].shape, kind),
        compiler_params=PARAMS,
        cost_estimate=COST,
        name="merge",
    )(target, *parts, *blocks)


def swap(x, axes, size, distance):
    return lax.ppermute(x, axes, [(i, i ^ distance) for i in range(size)])


def local(
    tokens,
    key_value_weight,
    adapter_down_weight,
    adapter_up_weight,
    adapter_scale,
    token_adapter_index,
):
    feature_axes = ("tensor", "sub")
    rows = tokens.shape[0]
    owned = adapter_down_weight.shape[0]
    owners = lax.axis_size("dp")
    sharers = lax.axis_size(feature_axes)
    me = lax.axis_index("dp")
    half = (lax.axis_index(feature_axes) >= sharers // 2).astype(I32)
    cap = up_to_16(owned * TOKEN_LIMIT)

    own, near = (0, 0, cap), (1, 0, cap)
    if owners == 4:
        usual = up_to_16(cap * 5 // 6)
        near = (1, 0, usual)
        first = up_to_16(usual * 3 // 5)
        far, last = [(3, 0, usual)], [[(2, 0, first)], [(2, first, usual - first)]]
        extra = [(j, usual, cap - usual) for j in (3, 2, 1)]
    else:
        usual, far, last, extra = cap, [], [[(j, 0, cap) for j in range(2, owners)]], []

    ids_row = token_adapter_index.reshape(1, rows)
    ids_heard = [ids_row] + [swap(ids_row, "dp", owners, j) for j in range(1, owners)]
    slot, target = route(ids_row, me.reshape(1), owners, owned, cap)
    sent = far + [near]
    packed = dict(zip(sent, sort_rows(tokens, slot, cap, sent, tuple(ids_heard[1:]))))
    received = {p: swap(packed[p], "dp", owners, p[0]) for p in sent}
    base_part = base_product(tokens, key_value_weight, packed[near])
    base = lax.psum_scatter(base_part, feature_axes, scatter_dimension=1, tiled=True)
    packed |= zip([own] + extra, sort_rows(tokens, slot, cap, [own] + extra, (base_part,)))
    gated = [p for pieces in last for p in pieces]
    packed |= zip(gated, sort_rows(tokens, slot, cap, gated, (received[near],)))
    received |= {p: swap(packed[p], "dp", owners, p[0]) for p in gated}

    early = [own, near] + far
    sets = [[p] for p in early] + [early] + last + ([extra] if extra else [])
    here = jnp.stack([me.astype(I32), half])
    names, ends, plans, largest = name_rows(ids_heard, here, owned, sets)

    if owned % 2:
        adapter_up_weight = jnp.pad(adapter_up_weight, ((0, 1), (0, 0), (0, 0)))
    up = adapter_up_weight.reshape(-1, adapter_up_weight.shape[2])
    scale = adapter_scale.reshape(1, owned)

    def exchange(mine, other, steps=2):
        if sharers == 4 and steps == 2:
            mine = mine + swap(other, "tensor", 2, 1)
            return [mine, swap(mine, "sub", 2, 1)]
        return [mine] + [
            swap(mine if d < sharers // 2 else other, feature_axes, sharers, d)
            for d in range(1, sharers)
        ]

    def deltas_of(pieces, blocks, names, ends, plan, down, up, scale, later_than, sooner=()):
        mine, other = shrink(pieces, blocks, names, ends, plan, down, later_than)
        sizes = tuple(b.shape[0] for b in blocks)
        lines = exchange(mine, other)
        groups = (mine.shape[0],)
        return expand(lines, groups, names, scale, up, sizes, later_than=sooner)

    def send_back(pieces, deltas):
        return [swap(d, "dp", owners, p[0]) for p, d in zip(pieces, deltas)]

    def begins(pieces):
        return [b * cap + f for b, f, _ in pieces]

    weights = (adapter_down_weight, up, scale)
    packed |= zip([own] + extra, sort_rows(tokens, slot, cap, [own] + extra, (base_part,)))
    for d in range(1, lax.axis_size("parts")):
        largest = jnp.maximum(largest, swap(largest, "parts", lax.axis_size("parts"), d))
    shares, waits = [], ()
    for k, p in enumerate(early):
        rows_here = received.get(p, packed[p])
        shares.append(
            shrink([p], [rows_here], names[k], ends, plans[k], adapter_down_weight, waits)
        )
        waits = (shares[-1][0], packed[gated[0]])
    lines = exchange(*(jnp.concatenate(pair, axis=0) for pair in zip(*shares)), steps=1)
    sizes = tuple(p[2] for p in early)
    here = len(early)
    deltas = expand(lines, tuple(c // 2 for c in sizes), names[here], scale, up, sizes, kept=1)
    parts = [base, place_rows(target, own[0] * cap, deltas[0])]
    returned = send_back(early[1:], deltas[1:])
    done = early[1:]
    for k, pieces in enumerate(last):
        blocks = [received[p] for p in pieces]
        waits = (deltas[0], parts[1], largest)
        deltas = deltas_of(
            pieces, blocks, names[here + 1 + k], ends, plans[here + 1 + k], *weights, waits, returned[-1:] if k else ()
        )
        returned += send_back(pieces, deltas)
        done += pieces

    def finish(parts, target, returned, *_):
        return merge(parts, target, begins(done), returned, BF16)

    if not extra:
        return finish(parts, target, returned)

    def finish_with_extra(parts, target, returned, blocks, names, ends, plan, weights):
        blocks = send_back(extra, blocks)
        deltas = deltas_of(extra, blocks, names, ends, plan, *weights, ())
        deltas = send_back(extra, deltas)
        return merge(parts, target, begins(done + extra), returned + deltas, BF16)

    return lax.cond(
        largest[0, 0] > usual,
        finish_with_extra,
        finish,
        parts,
        target,
        returned,
        [packed[p] for p in extra],
        names[-1],
        ends,
        plans[-1],
        weights,
    )


def solution(mesh):
    return jax.shard_map(
        local,
        mesh=mesh,
        in_specs=(
            P(("parts", "dp"), ("tensor", "sub")),
            P(("tensor", "sub"), None),
            P("dp", None, ("tensor", "sub")),
            P("dp", None, ("tensor", "sub")),
            P("dp"),
            P(("parts", "dp"), None),
        ),
        out_specs=P(("parts", "dp"), ("tensor", "sub")),
        check_vma=False,
    )
```

```python
import functools

import jax
import jax.numpy as jnp
from jax import lax
from jax.experimental import pallas as pl
from jax.experimental.pallas import tpu as pltpu
from jax.sharding import PartitionSpec as P

ADAPTER_RANK = 64
TOKEN_LIMIT = 12
VMEM_LIMIT = 28 * 1024 * 1024
F32 = jnp.float32
BF16 = jnp.bfloat16
I32 = jnp.int32
ANYWHERE = pl.BlockSpec(memory_space=pl.ANY)
COST = pl.CostEstimate(flops=1, transcendentals=0, bytes_accessed=1)
HEAD = pl.CostEstimate(flops=10**9, transcendentals=0, bytes_accessed=1)
PARAMS = pltpu.CompilerParams(vmem_limit_bytes=VMEM_LIMIT)


def up_to_16(count):
    return -(-count // 16) * 16


def owner_of(ids, owners, owned):
    total = jnp.zeros_like(ids)
    for o in range(1, owners):
        total = total + jnp.where(ids >= o * owned, 1, 0)
    return total


def as_column(line):
    size = line.shape[1]
    here = lax.broadcasted_iota(I32, (size, size), 0) == lax.broadcasted_iota(I32, (size, size), 1)
    return jnp.sum(jnp.where(here, line, 0), axis=1, keepdims=True)


def route_kernel(owners, owned, cap, me_ref, row_ref, slot_ref, target_ref):
    rows = row_ref.shape[1]
    id_row = row_ref[...]
    key_row = id_row * rows + lax.broadcasted_iota(I32, (1, rows), 1)
    key_col = as_column(key_row)
    own_row = owner_of(id_row, owners, owned)
    before = (key_col < key_row) & (key_col >= own_row * (owned * rows))
    rank = jnp.sum(jnp.where(before, 1, 0), axis=0, keepdims=True)
    found = (own_row ^ me_ref[0]) * cap + rank
    slot_ref[...] = found
    target_ref[...] = as_column(found)


def route(ids_row, me, owners, owned, cap):
    rows = ids_row.shape[1]
    return pl.pallas_call(
        functools.partial(route_kernel, owners, owned, cap),
        in_specs=[
            pl.BlockSpec(memory_space=pltpu.SMEM),
            pl.BlockSpec(memory_space=pltpu.VMEM),
        ],
        out_shape=[jax.ShapeDtypeStruct((1, rows), I32), jax.ShapeDtypeStruct((rows, 1), I32)],
        compiler_params=PARAMS,
        cost_estimate=HEAD,
        name="route",
    )(me, ids_row)


def sort_kernel(cap, pieces, waits, slot_ref, tok_ref, *refs):
    outs, place = refs[waits:-1], refs[-1]

    @pl.when(pl.program_id(0) == 0)
    def _():
        begin = 0
        for block, first, count in pieces:
            at = block * cap + first + lax.broadcasted_iota(I32, (count, slot_ref.shape[1]), 0)
            found = jnp.where(at == slot_ref[...], 1.0, 0.0).astype(BF16)
            place[begin : begin + count, :] = found
            begin += count

    moved = jnp.dot(place[...], tok_ref[...], preferred_element_type=F32).astype(BF16)
    begin = 0
    for (_, _, count), out in zip(pieces, outs):
        out[...] = moved[begin : begin + count, :]
        begin += count


def sort_rows(tokens, slot, cap, pieces, later_than=(), kind=jax.ShapeDtypeStruct):
    rows, width = tokens.shape
    step = min(512, width)
    return pl.pallas_call(
        functools.partial(sort_kernel, cap, pieces, len(later_than)),
        grid=(width // step,),
        in_specs=[
            pl.BlockSpec((1, rows), lambda i: (0, 0)),
            pl.BlockSpec((rows, step), lambda i: (0, i)),
        ]
        + [ANYWHERE] * len(later_than),
        out_specs=[pl.BlockSpec((count, step), lambda i: (0, i)) for _, _, count in pieces],
        out_shape=[kind((count, width), BF16) for _, _, count in pieces],
        scratch_shapes=[pltpu.VMEM((sum(c for _, _, c in pieces), rows), BF16)],
        compiler_params=PARAMS,
        cost_estimate=HEAD,
        name="sort",
    )(slot, tokens, *later_than)


def name_kernel(owners, owned, sets, here_ref, *refs):
    lines, outs, (ends_ref, plan_ref, most_ref) = refs[:owners], refs[owners:-3], refs[-3:]
    me, half = here_ref[0], here_ref[1]
    held = -(-owned // 8) * 8
    owner = lax.broadcasted_iota(I32, (-(-owners // 8) * 8, 1), 0)
    adapter = lax.broadcasted_iota(I32, (held, 1), 0)
    diagonal = adapter == lax.broadcasted_iota(I32, (held, 128), 1)
    used = lax.broadcasted_iota(I32, (1, 128), 1) < owned
    most = jnp.zeros(owner.shape, I32)
    ends = []
    for j, line in enumerate(lines):
        ids = line[...]
        chosen = jnp.where(owner_of(ids, owners, owned) == owner, 1, 0)
        count = jnp.sum(chosen, axis=1, keepdims=True)
        far = (me ^ j ^ owner >= 1) & (owner < owners)
        most = jnp.maximum(most, jnp.where(far, count, 0))
        mine = ids - me * owned
        upto = jnp.sum(jnp.where((mine >= 0) & (mine <= adapter), 1, 0), axis=1, keepdims=True)
        across = jnp.sum(jnp.where(diagonal, upto, 0), axis=0, keepdims=True)
        ends.append(jnp.where(used, across, 1 << 20))
        ends_ref[j : j + 1, :] = ends[j]
    most_ref[...] = jnp.broadcast_to(jnp.max(most, axis=0, keepdims=True), most_ref.shape)
    for k, (pieces, out) in enumerate(zip(sets, outs)):
        begin, low, high = 0, owned - 1, 0
        for block, first, count in pieces:
            at = first + lax.broadcasted_iota(I32, (count, 1), 0)
            names = jnp.sum(jnp.where(ends[block] <= at, 1, 0), axis=1, keepdims=True)
            out[begin : begin + count, :] = names
            low = jnp.minimum(low, jnp.min(names))
            high = jnp.maximum(high, jnp.max(jnp.where(names < owned, names, 0)))
            begin += count
        plan_ref[3 * k] = low
        plan_ref[3 * k + 1] = jnp.maximum(low, high)
        plan_ref[3 * k + 2] = half


def name_rows(lines, here, owned, sets):
    totals = [sum(c for _, _, c in pieces) for pieces in sets]
    on_chip, scalars = (pl.BlockSpec(memory_space=m) for m in (pltpu.VMEM, pltpu.SMEM))
    *names, ends, plan, most = pl.pallas_call(
        functools.partial(name_kernel, len(lines), owned, sets),
        in_specs=[scalars] + [on_chip] * len(lines),
        out_specs=[on_chip] * len(sets) + [on_chip, scalars, on_chip],
        out_shape=[jax.ShapeDtypeStruct((t, 1), I32) for t in totals]
        + [
            jax.ShapeDtypeStruct((len(lines), 128), I32),
            jax.ShapeDtypeStruct((3 * len(sets),), I32),
            jax.ShapeDtypeStruct((1, 128), I32),
        ],
        compiler_params=PARAMS,
        cost_estimate=COST,
        name="name_rows",
    )(here, *lines)
    plans = [plan[3 * k : 3 * k + 3] for k in range(len(sets))]
    return names, ends, plans, most


def base_kernel(tok_ref, weight_ref, _, out_ref):
    out_ref[...] = jnp.dot(tok_ref[...], weight_ref[...], preferred_element_type=F32)


def base_product(tokens, weight, later_than):
    (rows, width), columns = tokens.shape, weight.shape[1]
    step = min(256, columns)
    return pl.pallas_call(
        base_kernel,
        grid=(columns // step,),
        in_specs=[
            pl.BlockSpec((rows, width), lambda i: (0, 0)),
            pl.BlockSpec((width, step), lambda i: (0, i)),
            ANYWHERE,
        ],
        out_specs=pl.BlockSpec((rows, step), lambda i: (0, i)),
        out_shape=jax.ShapeDtypeStruct((rows, columns), F32),
        compiler_params=PARAMS,
        cost_estimate=HEAD,
        name="base",
    )(tokens, weight, later_than)


def shrink_kernel(pieces, group, fine, plan_ref, ends_ref, which_ref, down_ref, *refs):
    blocks, (mine_ref, other_ref, acc) = refs[: len(pieces)], refs[-3:]
    step, rank2 = pl.program_id(0), 2 * ADAPTER_RANK
    low, high, second = plan_ref[0], plan_ref[1], plan_ref[2] == 1
    begin = (low // group + step) * group

    @pl.when(step == 0)
    def _():
        acc[...] = jnp.zeros_like(acc)

    for f in range(0, group, fine):

        @pl.when((begin + f <= high) & (begin + f + fine > low))
        def _(f=f):
            adapter = begin + f
            windows, spans, at = [], [], 0
            for (block, first, size), rows in zip(pieces, blocks):
                span = min(up_to_16(fine * TOKEN_LIMIT + 15), size)
                ahead = ends_ref[block, jnp.maximum(adapter - 1, 0)]
                start = jnp.where(adapter > 0, ahead, 0) - first
                start = jnp.minimum(jnp.maximum(start, 0), size - span) // 16 * 16
                windows.append(rows[pl.ds(pl.multiple_of(start, 16), span), :])
                spans.append((pl.ds(pl.multiple_of(at + start, 16), span), span))
                at += size
            factors = down_ref[f : f + fine].reshape(fine * rank2, down_ref.shape[2])
            product = lax.dot_general(
                jnp.concatenate(windows, axis=0),
                factors,
                (((1,), (1,)), ((), ())),
                preferred_element_type=F32,
            )
            at = 0
            for here, span in spans:
                which = which_ref[here, :] - adapter
                found = acc[here, :]
                for q in range(fine):
                    part = product[at : at + span, q * rank2 : (q + 1) * rank2]
                    found = found + jnp.where(which == q, part, 0.0)
                acc[here, :] = found
                at += span

    @pl.when(step == pl.num_programs(0) - 1)
    def _():
        total = acc.shape[0]
        upper, lower = acc[: total // 2, :], acc[total // 2 :, :]
        keys = jnp.concatenate([upper[:, :ADAPTER_RANK], lower[:, :ADAPTER_RANK]], axis=1)
        values = jnp.concatenate([upper[:, ADAPTER_RANK:], lower[:, ADAPTER_RANK:]], axis=1)
        mine_ref[...] = jnp.where(second, values, keys)
        other_ref[...] = jnp.where(second, keys, values)


def shrink(pieces, blocks, names, ends, plan, down, later_than=()):
    total = sum(b.shape[0] for b in blocks)
    owned, rank2, width = down.shape
    group = next(g for g in (4, 3, 2, 1) if owned % g == 0)
    fine = next(g for g in (2, 3, 1) if group % g == 0)
    line = jax.ShapeDtypeStruct((total // 2, 2 * ADAPTER_RANK), F32)
    return pl.pallas_call(
        functools.partial(shrink_kernel, pieces, group, fine),
        grid_spec=pltpu.PrefetchScalarGridSpec(
            num_scalar_prefetch=1,
            grid=(owned // group,),
            in_specs=[
                pl.BlockSpec(memory_space=pltpu.SMEM),
                pl.BlockSpec((total, 1), lambda i, p: (0, 0)),
                pl.BlockSpec(
                    (group, rank2, width),
                    lambda i, p: (jnp.minimum(p[0] // group + i, p[1] // group), 0, 0),
                ),
            ]
            + [pl.BlockSpec(b.shape, lambda i, p: (0, 0)) for b in blocks]
            + [ANYWHERE] * len(later_than),
            out_specs=[pl.BlockSpec((total // 2, rank2), lambda i, p: (0, 0))] * 2,
            scratch_shapes=[pltpu.VMEM((total, rank2), F32)],
        ),
        out_shape=[line, line],
        compiler_params=PARAMS,
        cost_estimate=COST,
        name="shrink",
    )(plan, ends, names, down, *blocks, *later_than)


def split(x, terms):
    parts = []
    for _ in range(terms - 1):
        parts.append(x.astype(BF16).astype(F32))
        x = x - parts[-1]
    return parts + [x]


def expand_kernel(groups, sizes, heard, waits, which_ref, scale_ref, up_ref, *refs):
    lines, outs = refs[:heard], refs[heard + waits :]
    total = lines[0][...]
    for line in lines[1:]:
        total = total + line[...]
    twice, begin = [], 0
    for count in groups:
        lines = total[begin : begin + count, :]
        for side in (lines[:, :ADAPTER_RANK], lines[:, ADAPTER_RANK:]):
            twice.append(jnp.concatenate([side, side], axis=1))
        begin += count
    twice = jnp.concatenate(twice, axis=0)
    which = which_ref[...]
    parity = jnp.where(lax.broadcasted_iota(I32, (1, 2 * ADAPTER_RANK), 1) >= ADAPTER_RANK, 1, 0)
    pairs = up_ref.shape[0] // (2 * ADAPTER_RANK)
    wanted = [which == 2 * p + parity for p in range(pairs)]
    delta = None
    for term in split(twice, 3):
        spread = jnp.concatenate([jnp.where(w, term, 0.0).astype(BF16) for w in wanted], axis=1)
        product = jnp.dot(spread, up_ref[...], preferred_element_type=F32)
        delta = product if delta is None else delta + product
    adapters = lax.broadcasted_iota(I32, scale_ref.shape, 1)
    gain = jnp.sum(jnp.where(which == adapters, scale_ref[...], 0.0), axis=1, keepdims=True)
    delta = delta * gain
    begin = 0
    for size, out in zip(sizes, outs):
        piece = delta[begin : begin + size, :]
        if out.dtype == F32:
            out[...] = piece
        else:
            code_rows(piece, out)
        begin += size


def code_rows(x, out_ref):
    rows, columns = x.shape
    largest = jnp.maximum(jnp.max(jnp.abs(x), axis=1, keepdims=True), 2.0**-105)
    power = jnp.floor(jnp.log2(largest)) - 14.0
    power = power + jnp.where(largest * power_of_two(-power) > 32767.0, 1.0, 0.0)
    coded = jnp.round(x * power_of_two(-power))
    coded = jnp.minimum(jnp.maximum(coded, -32767.0), 32767.0)
    out_ref[:rows, :] = coded.astype(I32).astype(jnp.int16)
    down = lax.broadcasted_iota(I32, (rows, columns), 0)
    across = lax.broadcasted_iota(I32, (rows, columns), 1)
    line = jnp.sum(jnp.where(down == across, power, 0.0), axis=0, keepdims=True)
    line = jnp.broadcast_to(line, (16, columns)).astype(I32)
    out_ref[rows:, :] = line.astype(jnp.int16)


def power_of_two(power):
    return jnp.exp2(power).astype(BF16).astype(F32)


def expand(lines, groups, names, scale, up, sizes, kept=0, later_than=()):
    columns = up.shape[1]
    shapes = [
        jax.ShapeDtypeStruct((s, columns), F32)
        if i < kept
        else jax.ShapeDtypeStruct((s + 16, columns), jnp.int16)
        for i, s in enumerate(sizes)
    ]
    return pl.pallas_call(
        functools.partial(expand_kernel, groups, sizes, len(lines), len(later_than)),
        in_specs=[pl.BlockSpec(memory_space=pltpu.VMEM)] * (3 + len(lines))
        + [ANYWHERE] * len(later_than),
        out_shape=shapes,
        compiler_params=PARAMS,
        cost_estimate=COST,
        name="expand",
    )(names, scale, up, *lines, *later_than)


def place_kernel(begin, target_ref, rows_ref, out_ref):
    at = begin + lax.broadcasted_iota(I32, (1, rows_ref.shape[0]), 1)
    place = jnp.where(target_ref[...] == at, 1.0, 0.0).astype(BF16)
    total = None
    for term in split(rows_ref[...], 3):
        moved = jnp.dot(place, term.astype(BF16), preferred_element_type=F32)
        total = moved if total is None else total + moved
    out_ref[...] = total


def place_rows(target, begin, rows):
    return pl.pallas_call(
        functools.partial(place_kernel, begin),
        out_shape=jax.ShapeDtypeStruct((target.shape[0], rows.shape[1]), F32),
        compiler_params=PARAMS,
        cost_estimate=COST,
        name="place",
    )(target, rows)


def merge_kernel(begins, parts, target_ref, *refs):
    blocks, out_ref = refs[parts:-1], refs[-1]
    spots, powers, highs, lows = [], [], [], []
    for begin, block in zip(begins, blocks):
        count = block.shape[0] - 16
        spots.append(begin + lax.broadcasted_iota(I32, (1, count), 1))
        powers.append(block[count:, :].astype(I32)[:1, :count])
        coded = block[:count, :].astype(I32)
        high = (coded + 128) >> 8
        highs.append(high.astype(F32).astype(BF16))
        lows.append((coded - high * 256).astype(F32).astype(BF16))
    spot, power = jnp.concatenate(spots, axis=1), jnp.concatenate(powers, axis=1)
    place = jnp.where(target_ref[...] == spot, jnp.exp2(power.astype(F32)), 0.0).astype(BF16)
    total = jnp.dot(place, jnp.concatenate(highs, axis=0), preferred_element_type=F32) * 256.0
    total = total + jnp.dot(place, jnp.concatenate(lows, axis=0), preferred_element_type=F32)
    for part in refs[:parts]:
        total = total + part[...]
    out_ref[...] = total.astype(out_ref.dtype)


def merge(parts, target, begins, blocks, kind):
    return pl.pallas_call(
        functools.partial(merge_kernel, tuple(begins), len(parts)),
        out_shape=jax.ShapeDtypeStruct(parts[0].shape, kind),
        compiler_params=PARAMS,
        cost_estimate=COST,
        name="merge",
    )(target, *parts, *blocks)


def swap(x, axes, size, distance):
    return lax.ppermute(x, axes, [(i, i ^ distance) for i in range(size)])


def local(
    tokens,
    key_value_weight,
    adapter_down_weight,
    adapter_up_weight,
    adapter_scale,
    token_adapter_index,
):
    feature_axes = ("tensor", "sub")
    rows = tokens.shape[0]
    owned = adapter_down_weight.shape[0]
    owners = lax.axis_size("dp")
    sharers = lax.axis_size(feature_axes)
    me = lax.axis_index("dp")
    half = (lax.axis_index(feature_axes) >= sharers // 2).astype(I32)
    cap = up_to_16(owned * TOKEN_LIMIT)

    own, near = (0, 0, cap), (1, 0, cap)
    if owners == 4:
        usual = up_to_16(cap * 5 // 6)
        near = (1, 0, usual)
        first = up_to_16(usual * 3 // 5)
        far, last = [(3, 0, usual)], [[(2, 0, first)], [(2, first, usual - first)]]
        extra = [(j, usual, cap - usual) for j in (3, 2, 1)]
    else:
        usual, far, last, extra = cap, [], [[(j, 0, cap) for j in range(2, owners)]], []

    ids_row = token_adapter_index.reshape(1, rows)
    ids_heard = [ids_row] + [swap(ids_row, "dp", owners, j) for j in range(1, owners)]
    slot, target = route(ids_row, me.reshape(1), owners, owned, cap)
    sent = far + [near]
    packed = dict(zip(sent, sort_rows(tokens, slot, cap, sent, tuple(ids_heard[1:]), pltpu.HBM)))
    received = {p: swap(packed[p], "dp", owners, p[0]) for p in sent}
    base_part = base_product(tokens, key_value_weight, packed[near])
    base = lax.psum_scatter(base_part, feature_axes, scatter_dimension=1, tiled=True)
    packed |= zip([own] + extra, sort_rows(tokens, slot, cap, [own] + extra, (base_part,)))
    gated = [p for pieces in last for p in pieces]
    packed |= zip(gated, sort_rows(tokens, slot, cap, gated, (received[near],)))
    received |= {p: swap(packed[p], "dp", owners, p[0]) for p in gated}

    early = [own, near] + far
    sets = [[p] for p in early] + [early] + last + ([extra] if extra else [])
    here = jnp.stack([me.astype(I32), half])
    names, ends, plans, largest = name_rows(ids_heard, here, owned, sets)

    if owned % 2:
        adapter_up_weight = jnp.pad(adapter_up_weight, ((0, 1), (0, 0), (0, 0)))
    up = adapter_up_weight.reshape(-1, adapter_up_weight.shape[2])
    scale = adapter_scale.reshape(1, owned)

    def exchange(mine, other, steps=2):
        if sharers == 4 and steps == 2:
            mine = mine + swap(other, "tensor", 2, 1)
            return [mine, swap(mine, "sub", 2, 1)]
        return [mine] + [
            swap(mine if d < sharers // 2 else other, feature_axes, sharers, d)
            for d in range(1, sharers)
        ]

    def deltas_of(pieces, blocks, names, ends, plan, down, up, scale, later_than, sooner=()):
        mine, other = shrink(pieces, blocks, names, ends, plan, down, later_than)
        sizes = tuple(b.shape[0] for b in blocks)
        lines = exchange(mine, other)
        groups = (mine.shape[0],)
        return expand(lines, groups, names, scale, up, sizes, later_than=sooner)

    def send_back(pieces, deltas):
        return [swap(d, "dp", owners, p[0]) for p, d in zip(pieces, deltas)]

    def begins(pieces):
        return [b * cap + f for b, f, _ in pieces]

    weights = (adapter_down_weight, up, scale)
    packed |= zip([own] + extra, sort_rows(tokens, slot, cap, [own] + extra, (base_part,)))
    for d in range(1, lax.axis_size("parts")):
        largest = jnp.maximum(largest, swap(largest, "parts", lax.axis_size("parts"), d))
    shares, waits = [], ()
    for k, p in enumerate(early):
        rows_here = received.get(p, packed[p])
        shares.append(
            shrink([p], [rows_here], names[k], ends, plans[k], adapter_down_weight, waits)
        )
        waits = (shares[-1][0], packed[gated[0]])
    lines = exchange(*(jnp.concatenate(pair, axis=0) for pair in zip(*shares)), steps=1)
    sizes = tuple(p[2] for p in early)
    here = len(early)
    deltas = expand(lines, tuple(c // 2 for c in sizes), names[here], scale, up, sizes, kept=1)
    parts = [base, place_rows(target, own[0] * cap, deltas[0])]
    returned = send_back(early[1:], deltas[1:])
    done = early[1:]
    for k, pieces in enumerate(last):
        blocks = [received[p] for p in pieces]
        waits = (deltas[0], parts[1], largest)
        deltas = deltas_of(
            pieces, blocks, names[here + 1 + k], ends, plans[here + 1 + k], *weights, waits, returned[-1:] if k else ()
        )
        returned += send_back(pieces, deltas)
        done += pieces

    def finish(parts, target, returned, *_):
        return merge(parts, target, begins(done), returned, BF16)

    if not extra:
        return finish(parts, target, returned)

    def finish_with_extra(parts, target, returned, blocks, names, ends, plan, weights):
        blocks = send_back(extra, blocks)
        deltas = deltas_of(extra, blocks, names, ends, plan, *weights, ())
        deltas = send_back(extra, deltas)
        return merge(parts, target, begins(done + extra), returned + deltas, BF16)

    return lax.cond(
        largest[0, 0] > usual,
        finish_with_extra,
        finish,
        parts,
        target,
        returned,
        [packed[p] for p in extra],
        names[-1],
        ends,
        plans[-1],
        weights,
    )


def solution(mesh):
    return jax.shard_map(
        local,
        mesh=mesh,
        in_specs=(
            P(("parts", "dp"), ("tensor", "sub")),
            P(("tensor", "sub"), None),
            P("dp", None, ("tensor", "sub")),
            P("dp", None, ("tensor", "sub")),
            P("dp"),
            P(("parts", "dp"), None),
        ),
        out_specs=P(("parts", "dp"), ("tensor", "sub")),
        check_vma=False,
    )
```
